32 devices in a mesh: groups: 2 (over y), et: 4 (over z), ep: 4 (over x, core).
Axes of the slice: x: 2, y: 2, z: 4, core: 2. Of those that a mesh axis runs over, the one named last changes fastest.
Arguments:
- tokens: bfloat16 [768, 3072], P(('groups', 'et', 'ep')), parts along dimension 0, may hold values from -6 to 6
- expert_ids: int32 [768, 2], P(('groups', 'et', 'ep')), parts along dimension 0, may hold values from 0 to 3, all different within a row; in each aligned block of 24 rows (0 to 23, 24 to 47, ...) at most 12 rows name the same one
- gate_weights: float32 [768, 2], P(('groups', 'et', 'ep')), parts along dimension 0, may hold values from 0.2 to 1
- w_gate: bfloat16 [4, 3072, 8192], P('ep', None, 'et'), may hold values from -0.109375 to 0.109375
- w_up: bfloat16 [4, 3072, 8192], P('ep', None, 'et'), may hold values from -0.109375 to 0.109375
Outputs:
- routed_hidden: bfloat16 [768, 2, 8192], P(('groups', 'et', 'ep')), parts along dimension 0
The draws below stay inside these ranges and needn't reach their ends.
There are 2 independent parts, one for each index of `groups`. The reference program is written for one: setup_inputs(seed, part) draws one part's arguments, and reference() takes and returns one part's arrays. A program takes and returns all parts, laid end to end along the dimension named above; an argument that names none is the same for every part. Nothing has to cross between parts.
Inputs may be any that keep to these rules, and one draw needn't show every extreme that they name: `expert_ids`: A token's 2 experts differ. Among the 24 tokens of one device no expert is named more than 12 times, and in every draw some device names some expert exactly 12 times.
All inputs are finite; a program needn't handle non-finite values.
Results may differ from the reference program's by a relative error of at most 0.005.
Values may be sent and summed in bfloat16 or wider, within the bound.
No kernel may reach another device: no remote copies, remote signals or barrier semaphores. Data moves between devices by JAX's collectives and lax.ppermute only.
A program may use at most 128 MiB of HBM per device.

```python
import math
import jax
import jax.numpy as jnp
import numpy as np
from jax import lax

D = 3072
FF = 8192
TOP = 2
TOK_DEV = 24
CAP = 12
EXPERTS = 4
TOKENS = 384


def block_levels(own_key, extent, shards, least, top_value):
    loudness = 1.0
    for dim, blocks in shards:
        heights = jax.random.uniform(jax.random.fold_in(jax.random.fold_in(own_key, 6), dim), (blocks,), jnp.float32, least / len(shards), top_value / len(shards))
        loudness = loudness * jnp.repeat(jnp.exp(heights), extent[dim] // blocks).reshape((-1,) + (1,) * (len(extent) - 1 - dim))
    return loudness


def shared_out(rng, own, number, rows, count, top, limit, lean):
    order = jax.random.permutation(rng, count)
    packed, usual = portions_of(count, rows * top, limit, lean, True), portions_of(count, rows * top, limit, lean, False)
    places = jnp.arange(count)

    def named(tallies, turn):
        used = int((tallies > 0).sum())
        fixed = max(1, used // 4)
        passed = fixed + (places - fixed + turn * (used - fixed)) % max(1, count - fixed)
        return jnp.zeros((count,), jnp.int32).at[order[jnp.where(places < fixed, places, passed)]].set(jnp.asarray(tallies, jnp.int32))

    tallies = jnp.where(number % 4 == 0, named(packed, number // 4), named(usual, number - number // 4 - 1))
    mixed = jax.random.permutation(jax.random.fold_in(own, 3), count)
    donor, sink = mixed[0:count // 2 * 2:2], mixed[1:count // 2 * 2:2]
    slack = jnp.minimum(tallies[donor] - 1, limit - tallies[sink]) // 2
    slack = jnp.where((donor == order[0]) | (sink == order[0]) | (tallies[sink] == 0), 0, jnp.maximum(slack, 0))
    passed = jax.random.randint(jax.random.fold_in(own, 4), (count // 2,), 0, 1 << 20) % (slack + 1)
    tallies = tallies.at[donor].add(-passed).at[sink].add(passed)
    items = jnp.searchsorted(jnp.cumsum(tallies), jnp.arange(rows * top), side="right").astype(jnp.int32)
    table = items.reshape(top, rows).T
    table = table[jax.random.permutation(jax.random.fold_in(own, 1), rows)]
    turn = jax.random.randint(jax.random.fold_in(own, 2), (rows, 1), 0, top)
    return jnp.take_along_axis(table, (jnp.arange(top)[None, :] + turn) % top, axis=1)


def portions_of(count, total, reach, lean, full):
    weights = [(1 << 20) // math.isqrt(grade ** lean) + 1 for grade in range(1, count + 1)]
    largest = reach if full else min(reach, max(-(-total // count), total * weights[0] // sum(weights)))
    least = 1 if total - largest >= count - 1 else 0
    counts, spare = [largest] + [least] * (count - 1), total - largest - least * (count - 1)
    while spare > 0:
        free = [i for i in range(1, count) if counts[i] < largest] or [i for i in range(1, count) if counts[i] < reach]
        pool, budget = sum([weights[i] for i in free]), spare
        for i in free:
            addition = min(reach - counts[i], max(1, budget * weights[i] // pool), spare)
            counts[i] = counts[i] + addition
            spare = spare - addition
    return np.array(counts)


def bell_draw(rng, shape, spread, bound, split=(), kind=jnp.bfloat16):
    array = spread * jax.random.normal(rng, shape, jnp.float32)
    if split:
        array = array * block_levels(rng, shape, split, -0.22, 0.18)
    return jnp.clip(array, -bound, bound).astype(kind)


def setup_inputs(seed: int = 0, part: int = 0) -> dict:
    keys = jax.random.split(jax.random.key(seed), 6)
    part_splits = jax.random.split(jax.random.fold_in(keys[5], part), 6)
    tokens = bell_draw(part_splits[0], (TOKENS, D), 1.0, 6.0, ((0, 16),))
    expert_ids_keys = jax.random.split(jax.random.fold_in(part_splits[1], 1), TOKENS // TOK_DEV)
    expert_ids_turns = jax.random.permutation(jax.random.fold_in(part_splits[1], 3), TOKENS // TOK_DEV)
    expert_ids = jax.vmap(lambda own, number: shared_out(jax.random.fold_in(part_splits[1], 2), own, number, TOK_DEV, EXPERTS, TOP, CAP, 2))(expert_ids_keys, expert_ids_turns).reshape((TOKENS, TOP))
    gate_weights = jnp.clip(0.2 + 0.8 * jax.random.uniform(part_splits[2], (TOKENS, TOP), jnp.float32) ** block_levels(part_splits[2], (TOKENS, TOP), ((0, 16),), -0.2, 0.2), 0.2, 1.0)
    w_gate = bell_draw(keys[3], (EXPERTS, D, FF), D ** -0.5, 0.109375, ((0, 4), (2, 4)))
    w_up = bell_draw(keys[4], (EXPERTS, D, FF), D ** -0.5, 0.109375, ((0, 4), (2, 4)))
    return dict(tokens=tokens, expert_ids=expert_ids, gate_weights=gate_weights, w_gate=w_gate, w_up=w_up)


def reference(tokens, expert_ids, gate_weights, w_gate, w_up):
    def one_expert(carry, expert_index):
        gate_val = jnp.dot(tokens, w_gate[expert_index], preferred_element_type=jnp.float32)
        up_val = jnp.dot(tokens, w_up[expert_index], preferred_element_type=jnp.float32)
        hidden = (jax.nn.silu(gate_val) * up_val).astype(jnp.bfloat16)
        hidden = lax.optimization_barrier(hidden).astype(jnp.float32)
        chosen = (expert_ids == expert_index)[:, :, None]
        carry = jnp.where(chosen, gate_weights[:, :, None] * hidden[:, None, :], carry)
        return carry, None

    start_total = jnp.zeros((TOKENS, TOP, FF), jnp.float32)
    result, _ = lax.scan(one_expert, start_total, jnp.arange(EXPERTS, dtype=jnp.int32))
    return result.astype(jnp.bfloat16)
```

```python
import jax
import jax.numpy as jnp
from jax import lax
from jax.sharding import PartitionSpec as P


def place_slots(id_block, experts, capacity):
    flat_ids = id_block.reshape(-1)
    onehot = (flat_ids[:, None] == jnp.arange(experts, dtype=jnp.int32)[None, :]).astype(jnp.int32)
    before = jnp.cumsum(onehot, axis=0) - onehot
    position = jnp.sum(before * onehot, axis=1)
    return (flat_ids * capacity + position).reshape(id_block.shape)


def build_select(slot_pairs, total):
    targets = jnp.arange(total, dtype=jnp.int32).reshape(-1, 1, 1)
    return jnp.sum(slot_pairs[..., None, :, :] == targets, axis=-1).astype(jnp.bfloat16)


def swiglu_rows(rows, gate_local, up_local):
    gate_val = jnp.dot(rows, gate_local, preferred_element_type=jnp.float32)
    up_val = jnp.dot(rows, up_local, preferred_element_type=jnp.float32)
    return (jax.nn.silu(gate_val) * up_val).astype(jnp.bfloat16)


def exchange(blocks):
    return lax.all_to_all(blocks, ("et", "ep"), split_axis=0, concat_axis=0, tiled=True)


def body(tokens, expert_ids, gate_weights, w_gate, w_up):
    tok_rows, width = tokens.shape
    experts = lax.axis_size("ep")
    tensor_size = lax.axis_size("et")
    peers = experts * tensor_size
    capacity = tok_rows // 2
    gate_local = w_gate[0]
    up_local = w_up[0]
    slot_pairs = place_slots(expert_ids, experts, capacity)
    selector = build_select(slot_pairs, experts * capacity)
    buffer = jnp.dot(selector, tokens, preferred_element_type=jnp.float32).astype(jnp.bfloat16)
    buffer = buffer.reshape(1, experts, capacity * width // 128, 128)
    buffer = jnp.broadcast_to(buffer, (tensor_size,) + buffer.shape[1:])
    arrived = exchange(buffer.reshape(peers, capacity * width // 128, 128))
    hidden = swiglu_rows(arrived.reshape(peers * capacity, width), gate_local, up_local)
    units = hidden.shape[1]
    returned = exchange(hidden.reshape(peers, capacity * units // 128, 128))
    returned = returned.reshape(tensor_size, experts * capacity, units)
    targets = jnp.arange(experts * capacity, dtype=jnp.int32)
    picker = (slot_pairs[:, :, None] == targets[None, None, :]).astype(jnp.bfloat16)
    gathered = jnp.einsum("tsj,ejf->tsef", picker, returned, preferred_element_type=jnp.float32)
    gathered = gathered.reshape(tok_rows, 2, tensor_size * units)
    return (gate_weights[:, :, None] * gathered).astype(jnp.bfloat16)


def solution(mesh):
    in_specs = (
        P(("groups", "et", "ep"), None),
        P(("groups", "et", "ep"), None),
        P(("groups", "et", "ep"), None),
        P("ep", None, "et"),
        P("ep", None, "et"),
    )
    out_specs = P(("groups", "et", "ep"), None, None)
    return jax.shard_map(body, mesh=mesh, in_specs=in_specs, out_specs=out_specs, check_vma=False)
```

```python
import functools

import jax
import jax.numpy as jnp
from jax import lax
from jax.experimental import pallas as pl
from jax.experimental.pallas import tpu as pltpu
from jax.sharding import PartitionSpec as P


def place_slots(id_block, experts, capacity):
    flat_ids = id_block.reshape(-1)
    onehot = (flat_ids[:, None] == jnp.arange(experts, dtype=jnp.int32)[None, :]).astype(jnp.int32)
    before = jnp.cumsum(onehot, axis=0) - onehot
    position = jnp.sum(before * onehot, axis=1)
    return (flat_ids * capacity + position).reshape(id_block.shape)


def build_select(slot_pairs, total):
    targets = jnp.arange(total, dtype=jnp.int32).reshape(-1, 1, 1)
    return jnp.sum(slot_pairs[..., None, :, :] == targets, axis=-1).astype(jnp.bfloat16)


def swiglu_rows(rows, gate_local, up_local):
    gate_val = jnp.dot(rows, gate_local, preferred_element_type=jnp.float32)
    up_val = jnp.dot(rows, up_local, preferred_element_type=jnp.float32)
    return (jax.nn.silu(gate_val) * up_val).astype(jnp.bfloat16)


def exchange(blocks):
    return lax.all_to_all(blocks, ("et", "ep"), split_axis=0, concat_axis=0, tiled=True)


def exact_dot(a, b):
    return jnp.dot(a, b, preferred_element_type=jnp.float32)


def hidden_kernel(folds, x_ref, gate_ref, up_ref, out_ref, hidden_ref):
    peers = out_ref.shape[0]
    capacity = hidden_ref.shape[0] // peers
    span = hidden_ref.shape[1] // folds
    gate_val = exact_dot(x_ref[...], gate_ref[...])
    up_val = exact_dot(x_ref[...], up_ref[...])
    hidden_ref[...] = gate_val / (1.0 + jnp.exp(-gate_val)) * up_val
    for peer in range(peers):
        rows = hidden_ref[peer * capacity : (peer + 1) * capacity, :]
        pieces = [rows[:, fold * span : (fold + 1) * span] for fold in range(folds)]
        out_ref[peer] = jnp.concatenate(pieces, axis=0).astype(out_ref.dtype)


def hidden_blocks(x, gate_local, up_local, peers, folds):
    rows, width = x.shape
    units = gate_local.shape[1]
    whole = pl.BlockSpec(memory_space=pltpu.VMEM)
    return pl.pallas_call(
        functools.partial(hidden_kernel, folds),
        out_shape=jax.ShapeDtypeStruct((peers, rows // peers * folds, units // folds), x.dtype),
        in_specs=[whole] * 3,
        out_specs=whole,
        scratch_shapes=[pltpu.VMEM((rows, units), jnp.float32)],
        compiler_params=pltpu.CompilerParams(vmem_limit_bytes=16 << 20),
        cost_estimate=pl.CostEstimate(
            flops=4 * rows * width * units,
            bytes_accessed=4 * width * units,
            transcendentals=rows * units,
        ),
    )(x, gate_local, up_local)


def picks_of(ids, experts, capacity, folds):
    tok_rows = ids.shape[0]
    lower = (
        lax.broadcasted_iota(jnp.int32, (tok_rows, tok_rows), 0)
        > lax.broadcasted_iota(jnp.int32, (tok_rows, tok_rows), 1)
    ).astype(jnp.bfloat16)
    expert = lax.broadcasted_iota(jnp.int32, (tok_rows, 128), 1)
    first, second = ids[:, 0:1], ids[:, 1:2]
    named = ((expert == first) | (expert == second)).astype(jnp.bfloat16)
    before = exact_dot(lower, named).astype(jnp.int32)
    wide = experts * folds * capacity
    lane = lax.broadcasted_iota(jnp.int32, (tok_rows, wide), 1)
    spread = lax.broadcasted_iota(jnp.int32, (2 * tok_rows, tok_rows), 0)
    token = lax.broadcasted_iota(jnp.int32, (2 * tok_rows, tok_rows), 1)
    targets, doubles = [], []
    for slot, chosen in enumerate((first, second)):
        position = jnp.sum(jnp.where(expert == chosen, before, 0), axis=1, keepdims=True)
        targets.append(chosen * (folds * capacity) + position)
        doubles.append((spread == 2 * token + slot).astype(jnp.bfloat16))
    picks = []
    for fold in range(folds):
        rows = sum(
            exact_dot(double, (lane == target + fold * capacity).astype(jnp.bfloat16))
            for double, target in zip(doubles, targets)
        )
        picks.append(rows.astype(jnp.bfloat16))
    return jnp.concatenate(picks, axis=0)


def slot_weights(weights):
    tok_rows = weights.shape[0]
    row = lax.broadcasted_iota(jnp.int32, (2 * tok_rows, tok_rows), 0)
    token = lax.broadcasted_iota(jnp.int32, (2 * tok_rows, tok_rows), 1)
    column = jnp.zeros((2 * tok_rows, 1), jnp.float32)
    for slot in range(2):
        double = (row == 2 * token + slot).astype(jnp.bfloat16)
        rest = weights[:, slot : slot + 1]
        for _ in range(3):
            part = rest.astype(jnp.bfloat16)
            spread = exact_dot(double, jnp.broadcast_to(part, (tok_rows, 128)))
            column = column + spread[:, 0:1]
            rest = rest - part.astype(jnp.float32)
    return column


def final_kernel(experts, folds, ids_ref, weights_ref, recv_ref, out_ref):
    tok_rows = ids_ref.shape[0]
    peers, tall, span = recv_ref.shape
    picks = picks_of(ids_ref[...], experts, tall // folds, folds)
    column = slot_weights(weights_ref[...])
    for part in range(peers // experts):
        block = recv_ref[part * experts : (part + 1) * experts].reshape(experts * tall, span)
        rows = exact_dot(picks, block)
        for fold in range(folds):
            scaled = rows[fold * 2 * tok_rows : (fold + 1) * 2 * tok_rows] * column
            start = (part * folds + fold) * span
            out_ref[:, :, start : start + span] = scaled.astype(out_ref.dtype).reshape(tok_rows, 2, span)


def finish(expert_ids, gate_weights, received, experts, folds):
    tok_rows = expert_ids.shape[0]
    peers, tall, span = received.shape
    whole = pl.BlockSpec(memory_space=pltpu.VMEM)
    units = peers // experts * folds * span
    return pl.pallas_call(
        functools.partial(final_kernel, experts, folds),
        out_shape=jax.ShapeDtypeStruct((tok_rows, 2, units), received.dtype),
        in_specs=[whole] * 3,
        out_specs=whole,
        compiler_params=pltpu.CompilerParams(vmem_limit_bytes=16 << 20),
    )(expert_ids, gate_weights, received)


def body(tokens, expert_ids, gate_weights, w_gate, w_up):
    tok_rows, width = tokens.shape
    experts = lax.axis_size("ep")
    tensor_size = lax.axis_size("et")
    peers = experts * tensor_size
    capacity = tok_rows // 2
    gate_local = w_gate[0]
    up_local = w_up[0]
    slot_pairs = place_slots(expert_ids, experts, capacity)
    selector = build_select(slot_pairs, experts * capacity)
    buffer = jnp.dot(selector, tokens, preferred_element_type=jnp.float32).astype(jnp.bfloat16)
    buffer = buffer.reshape(1, experts, capacity * width // 128, 128)
    buffer = jnp.broadcast_to(buffer, (tensor_size,) + buffer.shape[1:])
    arrived = exchange(buffer.reshape(peers, capacity * width // 128, 128))
    units = gate_local.shape[1]
    if peers <= 16:
        folds = 4
        blocks = hidden_blocks(arrived.reshape(peers * capacity, width), gate_local, up_local, peers, folds)
        return finish(expert_ids, gate_weights, exchange(blocks), experts, folds)
    hidden = swiglu_rows(arrived.reshape(peers * capacity, width), gate_local, up_local)
    returned = exchange(hidden.reshape(peers, capacity * units // 128, 128))
    returned = returned.reshape(tensor_size, experts * capacity, units)
    targets = jnp.arange(experts * capacity, dtype=jnp.int32)
    picker = (slot_pairs[:, :, None] == targets[None, None, :]).astype(jnp.bfloat16)
    gathered = jnp.einsum("tsj,ejf->tsef", picker, returned, preferred_element_type=jnp.float32)
    gathered = gathered.reshape(tok_rows, 2, tensor_size * units)
    return (gate_weights[:, :, None] * gathered).astype(jnp.bfloat16)


def solution(mesh):
    in_specs = (
        P(("groups", "et", "ep"), None),
        P(("groups", "et", "ep"), None),
        P(("groups", "et", "ep"), None),
        P("ep", None, "et"),
        P("ep", None, "et"),
    )
    out_specs = P(("groups", "et", "ep"), None, None)
    return jax.shard_map(body, mesh=mesh, in_specs=in_specs, out_specs=out_specs, check_vma=False)
```

```python
import functools

import jax
import jax.numpy as jnp
from jax import lax
from jax.experimental import pallas as pl
from jax.experimental.pallas import tpu as pltpu
from jax.sharding import PartitionSpec as P


def place_slots(id_block, experts, capacity):
    flat_ids = id_block.reshape(-1)
    onehot = (flat_ids[:, None] == jnp.arange(experts, dtype=jnp.int32)[None, :]).astype(jnp.int32)
    before = jnp.cumsum(onehot, axis=0) - onehot
    position = jnp.sum(before * onehot, axis=1)
    return (flat_ids * capacity + position).reshape(id_block.shape)


def build_select(slot_pairs, total):
    targets = jnp.arange(total, dtype=jnp.int32).reshape(-1, 1, 1)
    return jnp.sum(slot_pairs[..., None, :, :] == targets, axis=-1).astype(jnp.bfloat16)


def swiglu_rows(rows, gate_local, up_local):
    gate_val = jnp.dot(rows, gate_local, preferred_element_type=jnp.float32)
    up_val = jnp.dot(rows, up_local, preferred_element_type=jnp.float32)
    return (jax.nn.silu(gate_val) * up_val).astype(jnp.bfloat16)


def exchange(blocks):
    return lax.all_to_all(blocks, ("et", "ep"), split_axis=0, concat_axis=0, tiled=True)


def exact_dot(a, b):
    return jnp.dot(a, b, preferred_element_type=jnp.float32)


def store_blocks(folds, hidden_ref, out_ref):
    peers = out_ref.shape[0]
    capacity = hidden_ref.shape[0] // peers
    span = hidden_ref.shape[1] // folds
    for peer in range(peers):
        rows = hidden_ref[peer * capacity : (peer + 1) * capacity, :]
        pieces = [rows[:, fold * span : (fold + 1) * span] for fold in range(folds)]
        out_ref[peer] = jnp.concatenate(pieces, axis=0).astype(out_ref.dtype)


def rows_of(ids_block, source, mine, experts, rows, tok_rows, capacity):
    tall = ids_block.shape[0]
    names = ids_block.astype(jnp.float32)
    expert = mine.astype(jnp.float32)
    named = (names[:, 0:1] == expert) | (names[:, 1:2] == expert)
    later = lax.broadcasted_iota(jnp.int32, (tall, tall), 0)
    earlier = lax.broadcasted_iota(jnp.int32, (tall, tall), 1)
    lower = ((later > earlier) & (later // tok_rows == earlier // tok_rows)).astype(jnp.bfloat16)
    flags = jnp.broadcast_to(named.astype(jnp.float32), (tall, 128)).astype(jnp.bfloat16)
    before = exact_dot(lower, flags)[:, 0:1].astype(jnp.int32)
    layer = lax.broadcasted_iota(jnp.int32, (tall, 1), 0) // tok_rows
    target = jnp.where(named, (layer * experts + source) * capacity + before, -1)
    return (lax.broadcasted_iota(jnp.int32, (tall, rows), 1) == target).astype(jnp.bfloat16)


def transposed_dot(a, b):
    return lax.dot_general(a, b, (((0,), (0,)), ((), ())), preferred_element_type=jnp.float32)


def weight_copies(weights, held, sems, start, step):
    return [
        [
            pltpu.make_async_copy(
                ref.at[pl.ds(start + part * step, step), :],
                into.at[pl.ds(part * step, step), :],
                sems.at[which, part],
            )
            for which, (ref, into) in enumerate(zip(weights, held))
        ]
        for part in range(held[0].shape[0] // step)
    ]


def first_kernel(step, tok_rows, capacity, experts, *refs):
    blocks, (gate_hbm, up_hbm, gate_ref, up_ref, sel_ref, x_ref, gate_held, up_held, sems) = refs[:experts], refs[experts:]
    copies = weight_copies((gate_hbm, up_hbm), (gate_held, up_held), sems, 0, step)
    for pair in copies:
        for copy in pair:
            copy.start()
    mine = lax.axis_index("ep")
    rows = gate_ref.shape[0]
    chosen = 0.0
    for number, block in enumerate(blocks):
        tall = block.shape[0]
        sel = rows_of(block[:, :128], mine ^ number, mine, experts, rows, tok_rows, capacity)
        sel_ref[number] = sel
        chosen = chosen + transposed_dot(sel, block[:, 128:])
    x_ref[...] = chosen.astype(x_ref.dtype)
    for part, pair in enumerate(copies):
        span = pl.ds(part * step, step)
        for copy, held, ref in zip(pair, (gate_held, up_held), (gate_ref, up_ref)):
            copy.wait()
            product = exact_dot(x_ref[:, span], held[span, :])
            ref[...] = product if part == 0 else ref[...] + product


def second_kernel(step, start, folds, *refs):
    experts = len(refs) - 11
    blocks = refs[:experts]
    sel_ref, gate_in, up_in, gate_hbm, up_hbm, out_ref, x_ref, gate_held, up_held, hidden_ref, sems = refs[experts:]
    copies = weight_copies((gate_hbm, up_hbm), (gate_held, up_held), sems, start, step)
    for pair in copies:
        for copy in pair:
            copy.start()
    x_ref[...] = sum(transposed_dot(sel_ref[number], block[...]) for number, block in enumerate(blocks)).astype(x_ref.dtype)
    sums = [gate_in[...], up_in[...]]
    for part, pair in enumerate(copies):
        span = pl.ds(part * step, step)
        for which, (copy, held) in enumerate(zip(pair, (gate_held, up_held))):
            copy.wait()
            sums[which] = sums[which] + exact_dot(x_ref[:, span], held[span, :])
    gate_val, up_val = sums
    hidden_ref[...] = gate_val / (1.0 + jnp.exp(-gate_val)) * up_val
    store_blocks(folds, hidden_ref, out_ref)


def split_hidden(first_blocks, finish_blocks, gate_local, up_local, peers, capacity, tok_rows, folds):
    width, units = gate_local.shape
    experts = len(first_blocks)
    rows = peers * capacity
    tall = first_blocks[0].shape[0]
    cut = first_blocks[0].shape[1] - 128
    step = 256
    whole = pl.BlockSpec(memory_space=pltpu.VMEM)
    outside = pl.BlockSpec(memory_space=pltpu.HBM)
    params = pltpu.CompilerParams(vmem_limit_bytes=26 << 20)
    kind = gate_local.dtype

    def scratch(depth):
        return [pltpu.VMEM((rows, depth), kind), pltpu.VMEM((depth, units), kind), pltpu.VMEM((depth, units), kind)]

    def cost(depth, activations):
        return pl.CostEstimate(flops=4 * rows * depth * units, bytes_accessed=4 * depth * units, transcendentals=activations)

    gate_sum, up_sum, sel = pl.pallas_call(
        functools.partial(first_kernel, step, tok_rows, capacity, experts),
        out_shape=[jax.ShapeDtypeStruct((rows, units), jnp.float32)] * 2 + [jax.ShapeDtypeStruct((experts, tall, rows), kind)],
        in_specs=[whole] * experts + [outside] * 2,
        out_specs=[whole] * 3,
        scratch_shapes=scratch(cut) + [pltpu.SemaphoreType.DMA((2, cut // step))],
        compiler_params=params,
        cost_estimate=cost(cut, 0),
    )(*first_blocks, gate_local, up_local)
    rest = width - cut
    second_blocks, sel = finish_blocks(sel)
    return pl.pallas_call(
        functools.partial(second_kernel, step, cut, folds),
        out_shape=jax.ShapeDtypeStruct((peers, capacity * folds, units // folds), kind),
        in_specs=[whole] * (experts + 3) + [outside] * 2,
        out_specs=whole,
        scratch_shapes=scratch(rest) + [pltpu.VMEM((rows, units), jnp.float32), pltpu.SemaphoreType.DMA((2, rest // step))],
        compiler_params=params,
        cost_estimate=cost(rest, rows * units),
    )(*second_blocks, sel, gate_sum, up_sum, gate_local, up_local)


def routed_by_columns(tokens, expert_ids, gate_local, up_local, peers, capacity, folds):
    tok_rows, width = tokens.shape
    cut = width // 2
    ids = jnp.pad(expert_ids.astype(tokens.dtype), ((0, 0), (0, 126)))
    packed = jnp.concatenate([ids, tokens], axis=1)
    own = lax.all_gather(packed, "et", axis=0, tiled=True)

    def swap(block, bit):
        return lax.ppermute(block, "ep", [(i, i ^ bit) for i in range(4)])

    part, later = own[:, : 128 + cut], own[:, 128 + cut :]
    far, later_far = swap(part, 2), swap(later, 2)
    later_near = swap(later, 1)

    def finish_blocks(sel):
        held, sel = lax.optimization_barrier((later_far, sel))
        return [later, later_near, held, swap(held, 1)], sel

    first_blocks = [part, swap(part, 1), far, swap(far, 1)]
    return split_hidden(first_blocks, finish_blocks, gate_local, up_local, peers, capacity, tok_rows, folds)


def picks_of(ids, experts, capacity, folds):
    tok_rows = ids.shape[0]
    lower = (
        lax.broadcasted_iota(jnp.int32, (tok_rows, tok_rows), 0)
        > lax.broadcasted_iota(jnp.int32, (tok_rows, tok_rows), 1)
    ).astype(jnp.bfloat16)
    expert = lax.broadcasted_iota(jnp.int32, (tok_rows, 128), 1)
    first, second = ids[:, 0:1], ids[:, 1:2]
    named = ((expert == first) | (expert == second)).astype(jnp.bfloat16)
    before = exact_dot(lower, named).astype(jnp.int32)
    wide = experts * folds * capacity
    lane = lax.broadcasted_iota(jnp.int32, (tok_rows, wide), 1)
    spread = lax.broadcasted_iota(jnp.int32, (2 * tok_rows, tok_rows), 0)
    token = lax.broadcasted_iota(jnp.int32, (2 * tok_rows, tok_rows), 1)
    targets, doubles = [], []
    for slot, chosen in enumerate((first, second)):
        position = jnp.sum(jnp.where(expert == chosen, before, 0), axis=1, keepdims=True)
        targets.append(chosen * (folds * capacity) + position)
        doubles.append((spread == 2 * token + slot).astype(jnp.bfloat16))
    picks = []
    for fold in range(folds):
        rows = sum(
            exact_dot(double, (lane == target + fold * capacity).astype(jnp.bfloat16))
            for double, target in zip(doubles, targets)
        )
        picks.append(rows.astype(jnp.bfloat16))
    return jnp.concatenate(picks, axis=0)


def slot_weights(weights):
    tok_rows = weights.shape[0]
    row = lax.broadcasted_iota(jnp.int32, (2 * tok_rows, tok_rows), 0)
    token = lax.broadcasted_iota(jnp.int32, (2 * tok_rows, tok_rows), 1)
    column = jnp.zeros((2 * tok_rows, 1), jnp.float32)
    for slot in range(2):
        double = (row == 2 * token + slot).astype(jnp.bfloat16)
        rest = weights[:, slot : slot + 1]
        for _ in range(3):
            part = rest.astype(jnp.bfloat16)
            spread = exact_dot(double, jnp.broadcast_to(part, (tok_rows, 128)))
            column = column + spread[:, 0:1]
            rest = rest - part.astype(jnp.float32)
    return column


def final_kernel(experts, folds, ids_ref, weights_ref, recv_ref, out_ref):
    tok_rows = ids_ref.shape[0]
    peers, tall, span = recv_ref.shape
    picks = picks_of(ids_ref[...], experts, tall // folds, folds)
    column = slot_weights(weights_ref[...])
    for part in range(peers // experts):
        block = recv_ref[part * experts : (part + 1) * experts].reshape(experts * tall, span)
        rows = exact_dot(picks, block)
        for fold in range(folds):
            scaled = rows[fold * 2 * tok_rows : (fold + 1) * 2 * tok_rows] * column
            start = (part * folds + fold) * span
            out_ref[:, :, start : start + span] = scaled.astype(out_ref.dtype).reshape(tok_rows, 2, span)


def finish(expert_ids, gate_weights, received, experts, folds):
    tok_rows = expert_ids.shape[0]
    peers, tall, span = received.shape
    whole = pl.BlockSpec(memory_space=pltpu.VMEM)
    units = peers // experts * folds * span
    return pl.pallas_call(
        functools.partial(final_kernel, experts, folds),
        out_shape=jax.ShapeDtypeStruct((tok_rows, 2, units), received.dtype),
        in_specs=[whole] * 3,
        out_specs=whole,
        compiler_params=pltpu.CompilerParams(vmem_limit_bytes=16 << 20),
    )(expert_ids, gate_weights, received)


def body(tokens, expert_ids, gate_weights, w_gate, w_up):
    tok_rows, width = tokens.shape
    experts = lax.axis_size("ep")
    tensor_size = lax.axis_size("et")
    peers = experts * tensor_size
    capacity = tok_rows // 2
    gate_local = w_gate[0]
    up_local = w_up[0]
    if experts == 4 and tensor_size == 4:
        folds = 4
        blocks = routed_by_columns(tokens, expert_ids, gate_local, up_local, peers, capacity, folds)
        return finish(expert_ids, gate_weights, exchange(blocks), experts, folds)
    slot_pairs = place_slots(expert_ids, experts, capacity)
    selector = build_select(slot_pairs, experts * capacity)
    buffer = jnp.dot(selector, tokens, preferred_element_type=jnp.float32).astype(jnp.bfloat16)
    buffer = buffer.reshape(1, experts, capacity * width // 128, 128)
    buffer = jnp.broadcast_to(buffer, (tensor_size,) + buffer.shape[1:])
    arrived = exchange(buffer.reshape(peers, capacity * width // 128, 128))
    units = gate_local.shape[1]
    hidden = swiglu_rows(arrived.reshape(peers * capacity, width), gate_local, up_local)
    returned = exchange(hidden.reshape(peers, capacity * units // 128, 128))
    returned = returned.reshape(tensor_size, experts * capacity, units)
    targets = jnp.arange(experts * capacity, dtype=jnp.int32)
    picker = (slot_pairs[:, :, None] == targets[None, None, :]).astype(jnp.bfloat16)
    gathered = jnp.einsum("tsj,ejf->tsef", picker, returned, preferred_element_type=jnp.float32)
    gathered = gathered.reshape(tok_rows, 2, tensor_size * units)
    return (gate_weights[:, :, None] * gathered).astype(jnp.bfloat16)


def solution(mesh):
    in_specs = (
        P(("groups", "et", "ep"), None),
        P(("groups", "et", "ep"), None),
        P(("groups", "et", "ep"), None),
        P("ep", None, "et"),
        P("ep", None, "et"),
    )
    out_specs = P(("groups", "et", "ep"), None, None)
    return jax.shard_map(body, mesh=mesh, in_specs=in_specs, out_specs=out_specs, check_vma=False)
```

```python
import functools

import jax
import jax.numpy as jnp
from jax import lax
from jax.experimental import pallas as pl
from jax.experimental.pallas import tpu as pltpu
from jax.sharding import PartitionSpec as P


def place_slots(id_block, experts, capacity):
    flat_ids = id_block.reshape(-1)
    onehot = (flat_ids[:, None] == jnp.arange(experts, dtype=jnp.int32)[None, :]).astype(jnp.int32)
    before = jnp.cumsum(onehot, axis=0) - onehot
    position = jnp.sum(before * onehot, axis=1)
    return (flat_ids * capacity + position).reshape(id_block.shape)


def build_select(slot_pairs, total):
    targets = jnp.arange(total, dtype=jnp.int32).reshape(-1, 1, 1)
    return jnp.sum(slot_pairs[..., None, :, :] == targets, axis=-1).astype(jnp.bfloat16)


def swiglu_rows(rows, gate_local, up_local):
    gate_val = jnp.dot(rows, gate_local, preferred_element_type=jnp.float32)
    up_val = jnp.dot(rows, up_local, preferred_element_type=jnp.float32)
    return (jax.nn.silu(gate_val) * up_val).astype(jnp.bfloat16)


def exchange(blocks):
    return lax.all_to_all(blocks, ("et", "ep"), split_axis=0, concat_axis=0, tiled=True)


def exact_dot(a, b):
    return jnp.dot(a, b, preferred_element_type=jnp.float32)


def store_blocks(folds, hidden_ref, out_ref):
    peers = out_ref.shape[0]
    capacity = hidden_ref.shape[0] // peers
    span = hidden_ref.shape[1] // folds
    for peer in range(peers):
        rows = hidden_ref[peer * capacity : (peer + 1) * capacity, :]
        pieces = [rows[:, fold * span : (fold + 1) * span] for fold in range(folds)]
        out_ref[peer] = jnp.concatenate(pieces, axis=0).astype(out_ref.dtype)


def rows_of(ids_block, source, mine, experts, rows, tok_rows, capacity):
    tall = ids_block.shape[0]
    names = ids_block.astype(jnp.float32)
    expert = mine.astype(jnp.float32)
    named = (names[:, 0:1] == expert) | (names[:, 1:2] == expert)
    later = lax.broadcasted_iota(jnp.int32, (tall, tall), 0)
    earlier = lax.broadcasted_iota(jnp.int32, (tall, tall), 1)
    lower = ((later > earlier) & (later // tok_rows == earlier // tok_rows)).astype(jnp.bfloat16)
    flags = jnp.broadcast_to(named.astype(jnp.float32), (tall, 128)).astype(jnp.bfloat16)
    before = exact_dot(lower, flags)[:, 0:1].astype(jnp.int32)
    layer = lax.broadcasted_iota(jnp.int32, (tall, 1), 0) // tok_rows
    target = jnp.where(named, (layer * experts + source) * capacity + before, -1)
    return (lax.broadcasted_iota(jnp.int32, (tall, rows), 1) == target).astype(jnp.bfloat16)


def transposed_dot(a, b):
    return lax.dot_general(a, b, (((0,), (0,)), ((), ())), preferred_element_type=jnp.float32)


def weight_copies(weights, held, sems, start, step):
    return [
        [
            pltpu.make_async_copy(
                ref.at[pl.ds(start + part * step, step), :],
                into.at[pl.ds(part * step, step), :],
                sems.at[which, part],
            )
            for which, (ref, into) in enumerate(zip(weights, held))
        ]
        for part in range(held[0].shape[0] // step)
    ]


def first_kernel(step, tok_rows, capacity, experts, *refs):
    blocks, (gate_hbm, up_hbm, gate_ref, up_ref, sel_ref, x_ref, gate_held, up_held, sems) = refs[:experts], refs[experts:]
    copies = weight_copies((gate_hbm, up_hbm), (gate_held, up_held), sems, 0, step)
    for pair in copies:
        for copy in pair:
            copy.start()
    mine = lax.axis_index("ep")
    rows = gate_ref.shape[0]
    chosen = 0.0
    for number, block in enumerate(blocks):
        tall = block.shape[0]
        sel = rows_of(block[:, :128], mine ^ number, mine, experts, rows, tok_rows, capacity)
        sel_ref[number] = sel
        chosen = chosen + transposed_dot(sel, block[:, 128:])
    x_ref[...] = chosen.astype(x_ref.dtype)
    for part, pair in enumerate(copies):
        span = pl.ds(part * step, step)
        for copy, held, ref in zip(pair, (gate_held, up_held), (gate_ref, up_ref)):
            copy.wait()
            product = exact_dot(x_ref[:, span], held[span, :])
            ref[...] = product if part == 0 else ref[...] + product


def second_kernel(step, start, folds, *refs):
    experts = len(refs) - 11
    blocks = refs[:experts]
    sel_ref, gate_in, up_in, gate_hbm, up_hbm, out_ref, x_ref, gate_held, up_held, hidden_ref, sems = refs[experts:]
    copies = weight_copies((gate_hbm, up_hbm), (gate_held, up_held), sems, start, step)
    for pair in copies:
        for copy in pair:
            copy.start()
    x_ref[...] = sum(transposed_dot(sel_ref[number], block[...]) for number, block in enumerate(blocks)).astype(x_ref.dtype)
    sums = [gate_in[...], up_in[...]]
    for part, pair in enumerate(copies):
        span = pl.ds(part * step, step)
        for which, (copy, held) in enumerate(zip(pair, (gate_held, up_held))):
            copy.wait()
            sums[which] = sums[which] + exact_dot(x_ref[:, span], held[span, :])
    gate_val, up_val = sums
    hidden_ref[...] = gate_val / (1.0 + jnp.exp(-gate_val)) * up_val
    store_blocks(folds, hidden_ref, out_ref)


def split_hidden(first_blocks, finish_blocks, gate_local, up_local, peers, capacity, tok_rows, folds):
    width, units = gate_local.shape
    experts = len(first_blocks)
    rows = peers * capacity
    tall = first_blocks[0].shape[0]
    cut = first_blocks[0].shape[1] - 128
    step = 256
    whole = pl.BlockSpec(memory_space=pltpu.VMEM)
    outside = pl.BlockSpec(memory_space=pltpu.HBM)
    params = pltpu.CompilerParams(vmem_limit_bytes=48 << 20)
    kind = gate_local.dtype

    def scratch(depth):
        return [pltpu.VMEM((rows, depth), kind), pltpu.VMEM((depth, units), kind), pltpu.VMEM((depth, units), kind)]

    def cost(depth, activations):
        return pl.CostEstimate(flops=4 * rows * depth * units, bytes_accessed=4 * depth * units, transcendentals=activations)

    gate_sum, up_sum, sel = pl.pallas_call(
        functools.partial(first_kernel, step, tok_rows, capacity, experts),
        out_shape=[jax.ShapeDtypeStruct((rows, units), jnp.float32)] * 2 + [jax.ShapeDtypeStruct((experts, tall, rows), kind)],
        in_specs=[whole] * experts + [outside] * 2,
        out_specs=[whole] * 3,
        scratch_shapes=scratch(cut) + [pltpu.SemaphoreType.DMA((2, cut // step))],
        compiler_params=params,
        cost_estimate=cost(cut, 0),
    )(*first_blocks, gate_local, up_local)
    rest = width - cut
    second_blocks, sel = finish_blocks(sel)
    return pl.pallas_call(
        functools.partial(second_kernel, step, cut, folds),
        out_shape=jax.ShapeDtypeStruct((peers, capacity * folds, units // folds), kind),
        in_specs=[whole] * (experts + 3) + [outside] * 2,
        out_specs=whole,
        scratch_shapes=scratch(rest) + [pltpu.VMEM((rows, units), jnp.float32), pltpu.SemaphoreType.DMA((2, rest // step))],
        compiler_params=params,
        cost_estimate=cost(rest, rows * units),
    )(*second_blocks, sel, gate_sum, up_sum, gate_local, up_local)


def routed_by_columns(tokens, expert_ids, gate_local, up_local, peers, capacity, folds):
    tok_rows, width = tokens.shape
    cut = width // 2
    ids = jnp.pad(expert_ids.astype(tokens.dtype), ((0, 0), (0, 126)))
    packed = jnp.concatenate([ids, tokens], axis=1)
    own = lax.all_gather(packed, "et", axis=0, tiled=True)

    def swap(block, bit):
        return lax.ppermute(block, "ep", [(i, i ^ bit) for i in range(4)])

    part, later = own[:, : 128 + cut], own[:, 128 + cut :]
    far, later_far = swap(part, 2), swap(later, 2)
    later_near = swap(later, 1)

    def finish_blocks(sel):
        held, sel = lax.optimization_barrier((later_far, sel))
        return [later, later_near, held, swap(held, 1)], sel

    first_blocks = [part, swap(part, 1), far, swap(far, 1)]
    return split_hidden(first_blocks, finish_blocks, gate_local, up_local, peers, capacity, tok_rows, folds)


def picks_of(ids, experts, capacity, folds):
    tok_rows = ids.shape[0]
    lower = (
        lax.broadcasted_iota(jnp.int32, (tok_rows, tok_rows), 0)
        > lax.broadcasted_iota(jnp.int32, (tok_rows, tok_rows), 1)
    ).astype(jnp.bfloat16)
    expert = lax.broadcasted_iota(jnp.int32, (tok_rows, 128), 1)
    first, second = ids[:, 0:1], ids[:, 1:2]
    named = ((expert == first) | (expert == second)).astype(jnp.bfloat16)
    before = exact_dot(lower, named).astype(jnp.int32)
    wide = experts * folds * capacity
    lane = lax.broadcasted_iota(jnp.int32, (tok_rows, wide), 1)
    spread = lax.broadcasted_iota(jnp.int32, (2 * tok_rows, tok_rows), 0)
    token = lax.broadcasted_iota(jnp.int32, (2 * tok_rows, tok_rows), 1)
    targets, doubles = [], []
    for slot, chosen in enumerate((first, second)):
        position = jnp.sum(jnp.where(expert == chosen, before, 0), axis=1, keepdims=True)
        targets.append(chosen * (folds * capacity) + position)
        doubles.append((spread == 2 * token + slot).astype(jnp.bfloat16))
    picks = []
    for fold in range(folds):
        rows = sum(
            exact_dot(double, (lane == target + fold * capacity).astype(jnp.bfloat16))
            for double, target in zip(doubles, targets)
        )
        picks.append(rows.astype(jnp.bfloat16))
    return jnp.concatenate(picks, axis=0)


def slot_weights(weights):
    tok_rows = weights.shape[0]
    row = lax.broadcasted_iota(jnp.int32, (2 * tok_rows, tok_rows), 0)
    token = lax.broadcasted_iota(jnp.int32, (2 * tok_rows, tok_rows), 1)
    column = jnp.zeros((2 * tok_rows, 1), jnp.float32)
    for slot in range(2):
        double = (row == 2 * token + slot).astype(jnp.bfloat16)
        rest = weights[:, slot : slot + 1]
        for _ in range(3):
            part = rest.astype(jnp.bfloat16)
            spread = exact_dot(double, jnp.broadcast_to(part, (tok_rows, 128)))
            column = column + spread[:, 0:1]
            rest = rest - part.astype(jnp.float32)
    return column


def final_kernel(experts, folds, ids_ref, weights_ref, recv_ref, out_ref):
    tok_rows = ids_ref.shape[0]
    peers, tall, span = recv_ref.shape
    picks = picks_of(ids_ref[...], experts, tall // folds, folds)
    column = slot_weights(weights_ref[...])
    for part in range(peers // experts):
        block = recv_ref[part * experts : (part + 1) * experts].reshape(experts * tall, span)
        rows = exact_dot(picks, block)
        for fold in range(folds):
            scaled = rows[fold * 2 * tok_rows : (fold + 1) * 2 * tok_rows] * column
            start = (part * folds + fold) * span
            out_ref[:, :, start : start + span] = scaled.astype(out_ref.dtype).reshape(tok_rows, 2, span)


def finish(expert_ids, gate_weights, received, experts, folds):
    tok_rows = expert_ids.shape[0]
    peers, tall, span = received.shape
    whole = pl.BlockSpec(memory_space=pltpu.VMEM)
    units = peers // experts * folds * span
    return pl.pallas_call(
        functools.partial(final_kernel, experts, folds),
        out_shape=jax.ShapeDtypeStruct((tok_rows, 2, units), received.dtype),
        in_specs=[whole] * 3,
        out_specs=whole,
        compiler_params=pltpu.CompilerParams(vmem_limit_bytes=16 << 20),
    )(expert_ids, gate_weights, received)


def body(tokens, expert_ids, gate_weights, w_gate, w_up):
    tok_rows, width = tokens.shape
    experts = lax.axis_size("ep")
    tensor_size = lax.axis_size("et")
    peers = experts * tensor_size
    capacity = tok_rows // 2
    gate_local = w_gate[0]
    up_local = w_up[0]
    if experts == 4 and tensor_size == 4:
        folds = 4
        blocks = routed_by_columns(tokens, expert_ids, gate_local, up_local, peers, capacity, folds)
        return finish(expert_ids, gate_weights, exchange(blocks), experts, folds)
    slot_pairs = place_slots(expert_ids, experts, capacity)
    selector = build_select(slot_pairs, experts * capacity)
    buffer = jnp.dot(selector, tokens, preferred_element_type=jnp.float32).astype(jnp.bfloat16)
    buffer = buffer.reshape(1, experts, capacity * width // 128, 128)
    buffer = jnp.broadcast_to(buffer, (tensor_size,) + buffer.shape[1:])
    arrived = exchange(buffer.reshape(peers, capacity * width // 128, 128))
    units = gate_local.shape[1]
    hidden = swiglu_rows(arrived.reshape(peers * capacity, width), gate_local, up_local)
    returned = exchange(hidden.reshape(peers, capacity * units // 128, 128))
    returned = returned.reshape(tensor_size, experts * capacity, units)
    targets = jnp.arange(experts * capacity, dtype=jnp.int32)
    picker = (slot_pairs[:, :, None] == targets[None, None, :]).astype(jnp.bfloat16)
    gathered = jnp.einsum("tsj,ejf->tsef", picker, returned, preferred_element_type=jnp.float32)
    gathered = gathered.reshape(tok_rows, 2, tensor_size * units)
    return (gate_weights[:, :, None] * gathered).astype(jnp.bfloat16)


def solution(mesh):
    in_specs = (
        P(("groups", "et", "ep"), None),
        P(("groups", "et", "ep"), None),
        P(("groups", "et", "ep"), None),
        P("ep", None, "et"),
        P("ep", None, "et"),
    )
    out_specs = P(("groups", "et", "ep"), None, None)
    return jax.shard_map(body, mesh=mesh, in_specs=in_specs, out_specs=out_specs, check_vma=False)
```

```python
import functools

import jax
import jax.numpy as jnp
from jax import lax
from jax.experimental import pallas as pl
from jax.experimental.pallas import tpu as pltpu
from jax.sharding import PartitionSpec as P


def place_slots(id_block, experts, capacity):
    flat_ids = id_block.reshape(-1)
    onehot = (flat_ids[:, None] == jnp.arange(experts, dtype=jnp.int32)[None, :]).astype(jnp.int32)
    before = jnp.cumsum(onehot, axis=0) - onehot
    position = jnp.sum(before * onehot, axis=1)
    return (flat_ids * capacity + position).reshape(id_block.shape)


def build_select(slot_pairs, total):
    targets = jnp.arange(total, dtype=jnp.int32).reshape(-1, 1, 1)
    return jnp.sum(slot_pairs[..., None, :, :] == targets, axis=-1).astype(jnp.bfloat16)


def swiglu_rows(rows, gate_local, up_local):
    gate_val = jnp.dot(rows, gate_local, preferred_element_type=jnp.float32)
    up_val = jnp.dot(rows, up_local, preferred_element_type=jnp.float32)
    return (jax.nn.silu(gate_val) * up_val).astype(jnp.bfloat16)


def exchange(blocks):
    return lax.all_to_all(blocks, ("et", "ep"), split_axis=0, concat_axis=0, tiled=True)


def exact_dot(a, b):
    return jnp.dot(a, b, preferred_element_type=jnp.float32)


def store_blocks(folds, hidden_ref, out_ref):
    peers = out_ref.shape[0]
    capacity = hidden_ref.shape[0] // peers
    span = hidden_ref.shape[1] // folds
    for peer in range(peers):
        rows = hidden_ref[peer * capacity : (peer + 1) * capacity, :]
        pieces = [rows[:, fold * span : (fold + 1) * span] for fold in range(folds)]
        out_ref[peer] = jnp.concatenate(pieces, axis=0).astype(out_ref.dtype)


def rows_of(ids_block, source, mine, experts, rows, tok_rows, capacity):
    tall = ids_block.shape[0]
    names = ids_block.astype(jnp.float32)
    expert = mine.astype(jnp.float32)
    named = (names[:, 0:1] == expert) | (names[:, 1:2] == expert)
    later = lax.broadcasted_iota(jnp.int32, (tall, tall), 0)
    earlier = lax.broadcasted_iota(jnp.int32, (tall, tall), 1)
    lower = ((later > earlier) & (later // tok_rows == earlier // tok_rows)).astype(jnp.bfloat16)
    flags = jnp.broadcast_to(named.astype(jnp.float32), (tall, 128)).astype(jnp.bfloat16)
    before = exact_dot(lower, flags)[:, 0:1].astype(jnp.int32)
    layer = lax.broadcasted_iota(jnp.int32, (tall, 1), 0) // tok_rows
    target = jnp.where(named, (layer * experts + source) * capacity + before, -1)
    return (lax.broadcasted_iota(jnp.int32, (tall, rows), 1) == target).astype(jnp.bfloat16)


def transposed_dot(a, b):
    return lax.dot_general(a, b, (((0,), (0,)), ((), ())), preferred_element_type=jnp.float32)


def weight_copies(weights, held, sems, start, step):
    return [
        pltpu.make_async_copy(
            ref.at[pl.ds(start + part * step, step), :], into.at[pl.ds(part * step, step), :], sems.at[which, part]
        )
        for part in range(held[0].shape[0] // step)
        for which, (ref, into) in enumerate(zip(weights, held))
    ]


def select_kernel(step, tok_rows, capacity, experts, *refs):
    first, second, gate_hbm, up_hbm, sel_ref, chosen_ref, gate_held, up_held, sems = refs
    copies = weight_copies((gate_hbm, up_hbm), (gate_held, up_held), sems, 0, step)
    for copy in copies:
        copy.start()
    mine = lax.axis_index("ep")
    rows = sel_ref.shape[2]
    chosen = 0.0
    for number, block in enumerate((first, second)):
        sel = rows_of(block[:, :128], mine ^ number, mine, experts, rows, tok_rows, capacity)
        sel_ref[number] = sel
        chosen = chosen + transposed_dot(sel, block[:, 128:])
    chosen_ref[...] = chosen.astype(chosen_ref.dtype)
    for copy in copies:
        copy.wait()


def first_kernel(step, tok_rows, capacity, experts, *refs):
    third, fourth, near_ref, gate_held, up_held, gate_hbm, up_hbm = refs[:7]
    gate_ref, up_ref, sel_ref, gate_rest, up_rest, sems = refs[7:]
    copies = weight_copies((gate_hbm, up_hbm), (gate_rest, up_rest), sems, gate_held.shape[0], step)
    for copy in copies:
        copy.start()
    mine = lax.axis_index("ep")
    rows = gate_ref.shape[0]
    chosen = near_ref[...].astype(jnp.float32)
    for number, block in enumerate((third, fourth)):
        sel = rows_of(block[:, :128], mine ^ (2 + number), mine, experts, rows, tok_rows, capacity)
        sel_ref[number] = sel
        chosen = chosen + transposed_dot(sel, block[:, 128:])
    x = chosen.astype(gate_held.dtype)
    gate_ref[...] = exact_dot(x, gate_held[: x.shape[1], :])
    up_ref[...] = exact_dot(x, up_held[: x.shape[1], :])
    for copy in copies:
        copy.wait()


def second_kernel(start, folds, *refs):
    blocks = refs[:4]
    near_sel, far_sel, gate_in, up_in, gate_held, up_held, gate_rest, up_rest, out_ref, hidden_ref = refs[4:]
    sels = [ref[number] for ref in (near_sel, far_sel) for number in range(2)]
    x = sum(transposed_dot(sel, block[...]) for sel, block in zip(sels, blocks)).astype(out_ref.dtype)
    middle = gate_held.shape[0] - start
    sums = []
    for held, rest, total in ((gate_held, gate_rest, gate_in), (up_held, up_rest, up_in)):
        total = total[...] + exact_dot(x[:, middle:], rest[...])
        if middle:
            total = total + exact_dot(x[:, :middle], held[start:, :])
        sums.append(total)
    gate_val, up_val = sums
    hidden_ref[...] = gate_val / (1.0 + jnp.exp(-gate_val)) * up_val
    store_blocks(folds, hidden_ref, out_ref)


WHOLE = pl.BlockSpec(memory_space=pltpu.VMEM)
OUTSIDE = pl.BlockSpec(memory_space=pltpu.HBM)


def local_kernel(kernel, out_shape, args, weights=(), flops=0, moved=0, scratch=(), limit=12):
    return pl.pallas_call(
        kernel,
        out_shape=out_shape,
        in_specs=[WHOLE] * len(args) + [OUTSIDE] * len(weights),
        out_specs=jax.tree.map(lambda _: WHOLE, out_shape),
        scratch_shapes=scratch,
        compiler_params=pltpu.CompilerParams(vmem_limit_bytes=limit << 20),
        cost_estimate=pl.CostEstimate(flops=flops, bytes_accessed=moved, transcendentals=0),
    )(*args, *(pltpu.with_memory_space_constraint(w, pltpu.HBM) for w in weights))


def pack_kernel(ids_ref, tokens_ref, out_ref):
    names = ids_ref[...].astype(jnp.float32)
    lane = lax.broadcasted_iota(jnp.int32, (names.shape[0], 128), 1)
    out_ref[:, :128] = jnp.where(lane == 0, names[:, 0:1], names[:, 1:2]).astype(out_ref.dtype)
    out_ref[:, 128:] = tokens_ref[...]


def cut_kernel(in_ref, first_ref, second_ref):
    cut = first_ref.shape[1]
    first_ref[...] = in_ref[:, :cut]
    second_ref[...] = in_ref[:, cut:]


def routed_by_columns(tokens, expert_ids, gate_local, up_local, peers, capacity, folds):
    tok_rows, width = tokens.shape
    units = gate_local.shape[1]
    experts = 4
    rows = peers * capacity
    cut = width // 2
    kind = tokens.dtype

    def swap(block, bit):
        return lax.ppermute(block, "ep", [(i, i ^ bit) for i in range(experts)])

    def product_flops(depth):
        return 4 * rows * depth * units

    packed = local_kernel(
        pack_kernel, jax.ShapeDtypeStruct((tok_rows, 128 + width), kind), (expert_ids, tokens), moved=4 * tokens.size
    )
    own = lax.all_gather(packed, "et", axis=0, tiled=True)
    tall = own.shape[0]
    shapes = [jax.ShapeDtypeStruct((tall, 128 + cut), kind), jax.ShapeDtypeStruct((tall, width - cut), kind)]
    part, later = local_kernel(cut_kernel, shapes, (own,), moved=4 * own.size)
    far, later_far = swap(part, 2), swap(later, 2)
    near, later_near = swap(part, 1), swap(later, 1)
    sel_shape = jax.ShapeDtypeStruct((2, tall, rows), kind)
    held = 2 * width // 3
    step = 256
    near_sel, near_rows, gate_held, up_held = local_kernel(
        functools.partial(select_kernel, step, tok_rows, capacity, experts),
        [sel_shape, jax.ShapeDtypeStruct((rows, cut), kind)] + [pltpu.VMEM((held, units), kind)] * 2,
        (part, near),
        (gate_local, up_local),
        flops=4 * tall * rows * cut,
        moved=4 * held * units,
        scratch=[pltpu.SemaphoreType.DMA((2, held // step))],
    )
    far, near_rows = lax.optimization_barrier((far, near_rows))
    rest = width - held
    gate_sum, up_sum, far_sel, gate_rest, up_rest = local_kernel(
        functools.partial(first_kernel, step, tok_rows, capacity, experts),
        [jax.ShapeDtypeStruct((rows, units), jnp.float32)] * 2
        + [sel_shape]
        + [pltpu.VMEM((rest, units), kind)] * 2,
        (far, swap(far, 1), near_rows, gate_held, up_held),
        (gate_local, up_local),
        flops=product_flops(cut),
        moved=4 * rest * units,
        scratch=[pltpu.SemaphoreType.DMA((2, rest // step))],
    )
    later_far, far_sel = lax.optimization_barrier((later_far, far_sel))
    return local_kernel(
        functools.partial(second_kernel, cut, folds),
        jax.ShapeDtypeStruct((peers, capacity * folds, units // folds), kind),
        (later, later_near, later_far, swap(later_far, 1), near_sel, far_sel)
        + (gate_sum, up_sum, gate_held, up_held, gate_rest, up_rest),
        flops=product_flops(width - cut),
        scratch=[pltpu.VMEM((rows, units), jnp.float32)],
    )


def picks_of(ids, experts, capacity, folds):
    tok_rows = ids.shape[0]
    lower = (
        lax.broadcasted_iota(jnp.int32, (tok_rows, tok_rows), 0)
        > lax.broadcasted_iota(jnp.int32, (tok_rows, tok_rows), 1)
    ).astype(jnp.bfloat16)
    expert = lax.broadcasted_iota(jnp.int32, (tok_rows, 128), 1)
    first, second = ids[:, 0:1], ids[:, 1:2]
    named = ((expert == first) | (expert == second)).astype(jnp.bfloat16)
    before = exact_dot(lower, named).astype(jnp.int32)
    wide = experts * folds * capacity
    lane = lax.broadcasted_iota(jnp.int32, (tok_rows, wide), 1)
    spread = lax.broadcasted_iota(jnp.int32, (2 * tok_rows, tok_rows), 0)
    token = lax.broadcasted_iota(jnp.int32, (2 * tok_rows, tok_rows), 1)
    targets, doubles = [], []
    for slot, chosen in enumerate((first, second)):
        position = jnp.sum(jnp.where(expert == chosen, before, 0), axis=1, keepdims=True)
        targets.append(chosen * (folds * capacity) + position)
        doubles.append((spread == 2 * token + slot).astype(jnp.bfloat16))
    picks = []
    for fold in range(folds):
        rows = sum(
            exact_dot(double, (lane == target + fold * capacity).astype(jnp.bfloat16))
            for double, target in zip(doubles, targets)
        )
        picks.append(rows.astype(jnp.bfloat16))
    return jnp.concatenate(picks, axis=0)


def slot_weights(weights):
    tok_rows = weights.shape[0]
    row = lax.broadcasted_iota(jnp.int32, (2 * tok_rows, tok_rows), 0)
    token = lax.broadcasted_iota(jnp.int32, (2 * tok_rows, tok_rows), 1)
    column = jnp.zeros((2 * tok_rows, 1), jnp.float32)
    for slot in range(2):
        double = (row == 2 * token + slot).astype(jnp.bfloat16)
        rest = weights[:, slot : slot + 1]
        for _ in range(3):
            part = rest.astype(jnp.bfloat16)
            spread = exact_dot(double, jnp.broadcast_to(part, (tok_rows, 128)))
            column = column + spread[:, 0:1]
            rest = rest - part.astype(jnp.float32)
    return column


def final_kernel(experts, folds, ids_ref, weights_ref, recv_ref, out_ref):
    tok_rows = ids_ref.shape[0]
    peers, tall, span = recv_ref.shape
    picks = picks_of(ids_ref[...], experts, tall // folds, folds)
    column = slot_weights(weights_ref[...])
    for part in range(peers // experts):
        block = recv_ref[part * experts : (part + 1) * experts].reshape(experts * tall, span)
        rows = exact_dot(picks, block)
        for fold in range(folds):
            scaled = rows[fold * 2 * tok_rows : (fold + 1) * 2 * tok_rows] * column
            start = (part * folds + fold) * span
            out_ref[:, :, start : start + span] = scaled.astype(out_ref.dtype).reshape(tok_rows, 2, span)


def finish(expert_ids, gate_weights, received, experts, folds):
    tok_rows = expert_ids.shape[0]
    peers, tall, span = received.shape
    whole = pl.BlockSpec(memory_space=pltpu.VMEM)
    units = peers // experts * folds * span
    return pl.pallas_call(
        functools.partial(final_kernel, experts, folds),
        out_shape=jax.ShapeDtypeStruct((tok_rows, 2, units), received.dtype),
        in_specs=[whole] * 3,
        out_specs=whole,
        compiler_params=pltpu.CompilerParams(vmem_limit_bytes=16 << 20),
    )(expert_ids, gate_weights, received)


def body(tokens, expert_ids, gate_weights, w_gate, w_up):
    tok_rows, width = tokens.shape
    experts = lax.axis_size("ep")
    tensor_size = lax.axis_size("et")
    peers = experts * tensor_size
    capacity = tok_rows // 2
    gate_local = w_gate[0]
    up_local = w_up[0]
    if experts == 4 and tensor_size == 4:
        folds = 4
        blocks = routed_by_columns(tokens, expert_ids, gate_local, up_local, peers, capacity, folds)
        return finish(expert_ids, gate_weights, exchange(blocks), experts, folds)
    slot_pairs = place_slots(expert_ids, experts, capacity)
    selector = build_select(slot_pairs, experts * capacity)
    buffer = jnp.dot(selector, tokens, preferred_element_type=jnp.float32).astype(jnp.bfloat16)
    buffer = buffer.reshape(1, experts, capacity * width // 128, 128)
    buffer = jnp.broadcast_to(buffer, (tensor_size,) + buffer.shape[1:])
    arrived = exchange(buffer.reshape(peers, capacity * width // 128, 128))
    units = gate_local.shape[1]
    hidden = swiglu_rows(arrived.reshape(peers * capacity, width), gate_local, up_local)
    returned = exchange(hidden.reshape(peers, capacity * units // 128, 128))
    returned = returned.reshape(tensor_size, experts * capacity, units)
    targets = jnp.arange(experts * capacity, dtype=jnp.int32)
    picker = (slot_pairs[:, :, None] == targets[None, None, :]).astype(jnp.bfloat16)
    gathered = jnp.einsum("tsj,ejf->tsef", picker, returned, preferred_element_type=jnp.float32)
    gathered = gathered.reshape(tok_rows, 2, tensor_size * units)
    return (gate_weights[:, :, None] * gathered).astype(jnp.bfloat16)


def solution(mesh):
    in_specs = (
        P(("groups", "et", "ep"), None),
        P(("groups", "et", "ep"), None),
        P(("groups", "et", "ep"), None),
        P("ep", None, "et"),
        P("ep", None, "et"),
    )
    out_specs = P(("groups", "et", "ep"), None, None)
    return jax.shard_map(body, mesh=mesh, in_specs=in_specs, out_specs=out_specs, check_vma=False)
```

```python
import functools

import jax
import jax.numpy as jnp
from jax import lax
from jax.experimental import pallas as pl
from jax.experimental.pallas import tpu as pltpu
from jax.sharding import PartitionSpec as P

WHOLE = pl.BlockSpec(memory_space=pltpu.VMEM)
OUTSIDE = pl.BlockSpec(memory_space=pltpu.HBM)


def place_slots(id_block, experts, capacity):
    flat_ids = id_block.reshape(-1)
    onehot = (flat_ids[:, None] == jnp.arange(experts, dtype=jnp.int32)[None, :]).astype(jnp.int32)
    before = jnp.cumsum(onehot, axis=0) - onehot
    position = jnp.sum(before * onehot, axis=1)
    return (flat_ids * capacity + position).reshape(id_block.shape)


def build_select(slot_pairs, total):
    targets = jnp.arange(total, dtype=jnp.int32).reshape(-1, 1, 1)
    return jnp.sum(slot_pairs[..., None, :, :] == targets, axis=-1).astype(jnp.bfloat16)


def swiglu_rows(rows, gate_local, up_local):
    gate_val = jnp.dot(rows, gate_local, preferred_element_type=jnp.float32)
    up_val = jnp.dot(rows, up_local, preferred_element_type=jnp.float32)
    return (jax.nn.silu(gate_val) * up_val).astype(jnp.bfloat16)


def exchange(blocks):
    return lax.all_to_all(blocks, ("et", "ep"), split_axis=0, concat_axis=0, tiled=True)


def local_kernel(kernel, out_shape, args, outside=(), flops=0, moved=0, scratch=(), limit=12):
    return pl.pallas_call(
        kernel,
        out_shape=out_shape,
        in_specs=[WHOLE] * len(args) + [OUTSIDE] * len(outside),
        out_specs=jax.tree.map(lambda _: WHOLE, out_shape),
        scratch_shapes=scratch,
        compiler_params=pltpu.CompilerParams(vmem_limit_bytes=limit << 20),
        cost_estimate=pl.CostEstimate(flops=flops, bytes_accessed=moved, transcendentals=0),
    )(*args, *(pltpu.with_memory_space_constraint(array, pltpu.HBM) for array in outside))


def exact_dot(a, b):
    return jnp.dot(a, b, preferred_element_type=jnp.float32)


def transposed_dot(a, b):
    return lax.dot_general(a, b, (((0,), (0,)), ((), ())), preferred_element_type=jnp.float32)


def iota(shape, dim):
    return lax.broadcasted_iota(jnp.int32, shape, dim)


def as_column(row):
    size = row.shape[1]
    eye = iota((size, size), 0) == iota((size, size), 1)
    return jnp.sum(jnp.where(eye, row, jnp.zeros_like(row)), axis=1, keepdims=True)


def as_row(column):
    size = column.shape[0]
    eye = iota((size, size), 0) == iota((size, size), 1)
    return jnp.sum(jnp.where(eye, column, jnp.zeros_like(column)), axis=0, keepdims=True)


def pack_kernel(ids_ref, tokens_hbm, out_ref, sem):
    copy = pltpu.make_async_copy(tokens_hbm, out_ref.at[:, 128:], sem)
    copy.start()
    names = ids_ref[...].astype(jnp.float32)
    lane = iota((out_ref.shape[0], 128), 1)
    out_ref[:, :128] = jnp.where(lane == 0, as_column(names[0:1]), as_column(names[1:2])).astype(out_ref.dtype)
    copy.wait()


def rows_of(ids_block, source, expert, rows, tok_rows, capacity):
    tall = ids_block.shape[0]
    names = ids_block.astype(jnp.float32)
    expert = expert.astype(jnp.float32)
    named = (names[:, 0:1] == expert) | (names[:, 1:2] == expert)
    later, earlier = iota((tall, tall), 0), iota((tall, tall), 1)
    lower = ((later > earlier) & (later // tok_rows == earlier // tok_rows)).astype(jnp.bfloat16)
    flags = jnp.broadcast_to(named.astype(jnp.float32), (tall, 128)).astype(jnp.bfloat16)
    before = exact_dot(lower, flags)[:, 0:1].astype(jnp.int32)
    layer = iota((tall, 1), 0) // tok_rows
    target = jnp.where(named, (layer * 2 + source) * capacity + before, -1)
    return (iota((tall, rows), 1) == target).astype(jnp.bfloat16)


def select_kernel(tok_rows, capacity, own_ref, near_ref, first_ref, second_ref, stay_ref):
    mine = lax.axis_index("ep")
    core = mine % 2
    rows = stay_ref.shape[0]
    blocks = ((own_ref, core), (near_ref, 1 - core))
    cut = first_ref.shape[1]

    def chosen(sels, start, stop):
        parts = [transposed_dot(sel, ref[:, 128 + start : 128 + stop]) for sel, (ref, _) in zip(sels, blocks)]
        return (parts[0] + parts[1]).astype(stay_ref.dtype)

    def columns_of(expert):
        return [rows_of(ref[:, :128], source, expert, rows, tok_rows, capacity) for ref, source in blocks]

    sels = columns_of(mine ^ 2)
    first_ref[...] = chosen(sels, 0, cut)
    second_ref[...] = chosen(sels, cut, stay_ref.shape[1])
    stay_ref[...] = chosen(columns_of(mine), 0, stay_ref.shape[1])


def weight_copies(weights, held, sems, start, step):
    return [
        pltpu.make_async_copy(
            ref.at[pl.ds(start + part * step, step), :], into.at[pl.ds(part * step, step), :], sems.at[which, part]
        )
        for part in range(held[0].shape[0] // step)
        for which, (ref, into) in enumerate(zip(weights, held))
    ]


def fetch_kernel(step, stay_ref, gate_hbm, up_hbm, gate_held, up_held, sems):
    copies = weight_copies((gate_hbm, up_hbm), (gate_held, up_held), sems, 0, step)
    for copy in copies:
        copy.start()
    for copy in copies:
        copy.wait()


def gather_rows(x_ref, stay, far):
    rows = stay.shape[0]
    chip = lax.axis_index("ep") // 2
    x_ref[pl.ds(pl.multiple_of(chip * rows, rows), rows), :] = stay
    x_ref[pl.ds(pl.multiple_of((1 - chip) * rows, rows), rows), :] = far


def first_kernel(step, far_ref, stay_ref, gate_held, up_held, gate_hbm, up_hbm, *refs):
    gate_ref, up_ref, gate_rest, up_rest, x_ref, sems = refs
    copies = weight_copies((gate_hbm, up_hbm), (gate_rest, up_rest), sems, gate_held.shape[0], step)
    for copy in copies:
        copy.start()
    cut = far_ref.shape[1]
    gather_rows(x_ref, stay_ref[:, :cut], far_ref[...])
    gate_ref[...] = exact_dot(x_ref[...], gate_held[:cut, :])
    up_ref[...] = exact_dot(x_ref[...], up_held[:cut, :])
    for copy in copies:
        copy.wait()


def second_kernel(folds, experts, far_ref, stay_ref, gate_in, up_in, *refs):
    gate_held, up_held, gate_rest, up_rest, out_ref, x_ref, hidden_ref = refs
    cut = stay_ref.shape[1] - far_ref.shape[1]
    gather_rows(x_ref, stay_ref[:, cut:], far_ref[...])
    middle = gate_held.shape[0] - cut
    sums = []
    for held, rest, total in ((gate_held, gate_rest, gate_in), (up_held, up_rest, up_in)):
        total = total[...] + exact_dot(x_ref[:, middle:], rest[...])
        if middle:
            total = total + exact_dot(x_ref[:, :middle], held[cut:, :])
        sums.append(total)
    gate_val, up_val = sums
    hidden_ref[...] = gate_val / (1.0 + jnp.exp(-gate_val)) * up_val
    store_blocks(folds, experts, hidden_ref, out_ref)


def store_blocks(folds, experts, hidden_ref, out_ref):
    peers = out_ref.shape[0]
    capacity = hidden_ref.shape[0] // peers
    span = hidden_ref.shape[1] // folds
    for peer in range(peers):
        layer, chip, core = peer // experts, peer % experts // 2, peer % 2
        start = (chip * (peers // 2) + layer * 2 + core) * capacity
        rows = hidden_ref[start : start + capacity, :]
        pieces = [rows[:, fold * span : (fold + 1) * span] for fold in range(folds)]
        out_ref[peer] = jnp.concatenate(pieces, axis=0).astype(out_ref.dtype)


def routed_by_columns(tokens, expert_ids, gate_local, up_local, peers, capacity, folds):
    tok_rows, width = tokens.shape
    units = gate_local.shape[1]
    experts = 4
    rows = peers * capacity
    half = rows // 2
    cut = width // 2
    held = 2 * width // 3
    rest = width - held
    step = 256
    kind = tokens.dtype

    def array(*shape):
        return jax.ShapeDtypeStruct(shape, kind)

    def swap(block, bit):
        return lax.ppermute(block, "ep", [(i, i ^ bit) for i in range(experts)])

    packed = local_kernel(
        pack_kernel, array(tok_rows, 128 + width), (expert_ids.T,), (tokens,), scratch=[pltpu.SemaphoreType.DMA]
    )
    own = lax.all_gather(packed, "et", axis=0, tiled=True)
    first, second, stay = local_kernel(
        functools.partial(select_kernel, tok_rows, capacity),
        [array(half, cut), array(half, width - cut), array(half, width)],
        (own, swap(own, 1)),
        flops=8 * own.shape[0] * half * width,
        moved=8 * own.size,
    )
    far, later = swap(first, 2), swap(second, 2)
    gate_held, up_held = local_kernel(
        functools.partial(fetch_kernel, step),
        [pltpu.VMEM((held, units), kind)] * 2,
        (stay,),
        (gate_local, up_local),
        moved=8 * held * units,
        scratch=[pltpu.SemaphoreType.DMA((2, held // step))],
    )
    far, gate_held, up_held = lax.optimization_barrier((far, gate_held, up_held))
    gate_sum, up_sum, gate_rest, up_rest = local_kernel(
        functools.partial(first_kernel, step),
        [jax.ShapeDtypeStruct((rows, units), jnp.float32)] * 2 + [pltpu.VMEM((rest, units), kind)] * 2,
        (far, stay, gate_held, up_held),
        (gate_local, up_local),
        flops=4 * rows * cut * units,
        moved=4 * rest * units,
        scratch=[pltpu.VMEM((rows, cut), kind), pltpu.SemaphoreType.DMA((2, rest // step))],
    )
    later, gate_rest, up_rest = lax.optimization_barrier((later, gate_rest, up_rest))
    return local_kernel(
        functools.partial(second_kernel, folds, experts),
        array(peers, capacity * folds, units // folds),
        (later, stay, gate_sum, up_sum, gate_held, up_held, gate_rest, up_rest),
        flops=4 * rows * (width - cut) * units,
        scratch=[pltpu.VMEM((rows, width - cut), kind), pltpu.VMEM((rows, units), jnp.float32)],
    )


def picks_kernel(experts, capacity, folds, ids_ref, weights_ref, picks_ref, column_ref):
    tok_rows = ids_ref.shape[1]
    both = 2 * tok_rows
    ids = [as_column(ids_ref[slot : slot + 1, :]) for slot in range(2)]
    expert = iota((tok_rows, 128), 1)
    named = ((expert == ids[0]) | (expert == ids[1])).astype(jnp.bfloat16)
    lower = (iota((tok_rows, tok_rows), 0) > iota((tok_rows, tok_rows), 1)).astype(jnp.bfloat16)
    before = exact_dot(lower, named).astype(jnp.int32)
    slot_row, token = iota((both, tok_rows), 0), iota((both, tok_rows), 1)
    target = jnp.zeros((both, 1), jnp.int32)
    column = jnp.zeros((both, 1), jnp.float32)
    for slot, chosen in enumerate(ids):
        position = jnp.sum(jnp.where(expert == chosen, before, 0), axis=1, keepdims=True)
        mask = slot_row == 2 * token + slot
        place = as_row(chosen * (folds * capacity) + position)
        target = target + jnp.sum(jnp.where(mask, place, 0), axis=1, keepdims=True)
        column = column + jnp.sum(jnp.where(mask, weights_ref[slot : slot + 1, :], 0.0), axis=1, keepdims=True)
    column_ref[...] = jnp.broadcast_to(column, column_ref.shape)
    lane = iota((both, experts * folds * capacity), 1)
    for fold in range(folds):
        picks_ref[fold * both : (fold + 1) * both, :] = (lane == target + fold * capacity).astype(picks_ref.dtype)


def final_kernel(experts, folds, picks_ref, column_ref, recv_ref, out_ref):
    tok_rows = out_ref.shape[0]
    both = 2 * tok_rows
    peers, tall, span = recv_ref.shape
    column = column_ref[:, 0:1]
    for part in range(peers // experts):
        block = recv_ref[part * experts : (part + 1) * experts].reshape(experts * tall, span)
        rows = exact_dot(picks_ref[...], block)
        for fold in range(folds):
            scaled = rows[fold * both : (fold + 1) * both] * column
            start = (part * folds + fold) * span
            out_ref[:, :, start : start + span] = scaled.astype(out_ref.dtype).reshape(tok_rows, 2, span)


def finish(expert_ids, gate_weights, received, experts, folds):
    tok_rows = expert_ids.shape[0]
    peers, tall, span = received.shape
    capacity = tall // folds
    kind = received.dtype
    picks, column = local_kernel(
        functools.partial(picks_kernel, experts, capacity, folds),
        [
            jax.ShapeDtypeStruct((2 * tok_rows * folds, experts * tall), kind),
            jax.ShapeDtypeStruct((2 * tok_rows, 128), jnp.float32),
        ],
        (expert_ids.T, gate_weights.T),
        moved=1 << 20,
    )
    units = peers // experts * folds * span
    return local_kernel(
        functools.partial(final_kernel, experts, folds),
        jax.ShapeDtypeStruct((tok_rows, 2, units), kind),
        (picks, column, received),
        moved=4 * received.size,
    )


def body(tokens, expert_ids, gate_weights, w_gate, w_up):
    tok_rows, width = tokens.shape
    experts = lax.axis_size("ep")
    tensor_size = lax.axis_size("et")
    peers = experts * tensor_size
    capacity = tok_rows // 2
    gate_local = w_gate[0]
    up_local = w_up[0]
    if experts == 4 and tensor_size == 4:
        folds = 4
        blocks = routed_by_columns(tokens, expert_ids, gate_local, up_local, peers, capacity, folds)
        return finish(expert_ids, gate_weights, exchange(blocks), experts, folds)
    slot_pairs = place_slots(expert_ids, experts, capacity)
    selector = build_select(slot_pairs, experts * capacity)
    buffer = jnp.dot(selector, tokens, preferred_element_type=jnp.float32).astype(jnp.bfloat16)
    buffer = buffer.reshape(1, experts, capacity * width // 128, 128)
    buffer = jnp.broadcast_to(buffer, (tensor_size,) + buffer.shape[1:])
    arrived = exchange(buffer.reshape(peers, capacity * width // 128, 128))
    hidden = swiglu_rows(arrived.reshape(peers * capacity, width), gate_local, up_local)
    units = hidden.shape[1]
    returned = exchange(hidden.reshape(peers, capacity * units // 128, 128))
    returned = returned.reshape(tensor_size, experts * capacity, units)
    targets = jnp.arange(experts * capacity, dtype=jnp.int32)
    picker = (slot_pairs[:, :, None] == targets[None, None, :]).astype(jnp.bfloat16)
    gathered = jnp.einsum("tsj,ejf->tsef", picker, returned, preferred_element_type=jnp.float32)
    gathered = gathered.reshape(tok_rows, 2, tensor_size * units)
    return (gate_weights[:, :, None] * gathered).astype(jnp.bfloat16)


def solution(mesh):
    in_specs = (
        P(("groups", "et", "ep"), None),
        P(("groups", "et", "ep"), None),
        P(("groups", "et", "ep"), None),
        P("ep", None, "et"),
        P("ep", None, "et"),
    )
    out_specs = P(("groups", "et", "ep"), None, None)
    return jax.shard_map(body, mesh=mesh, in_specs=in_specs, out_specs=out_specs, check_vma=False)
```

```python
import functools

import jax
import jax.numpy as jnp
from jax import lax
from jax.experimental import pallas as pl
from jax.experimental.pallas import tpu as pltpu
from jax.sharding import PartitionSpec as P

WHOLE = pl.BlockSpec(memory_space=pltpu.VMEM)
OUTSIDE = pl.BlockSpec(memory_space=pltpu.HBM)


def place_slots(id_block, experts, capacity):
    flat_ids = id_block.reshape(-1)
    onehot = (flat_ids[:, None] == jnp.arange(experts, dtype=jnp.int32)[None, :]).astype(jnp.int32)
    before = jnp.cumsum(onehot, axis=0) - onehot
    position = jnp.sum(before * onehot, axis=1)
    return (flat_ids * capacity + position).reshape(id_block.shape)


def build_select(slot_pairs, total):
    targets = jnp.arange(total, dtype=jnp.int32).reshape(-1, 1, 1)
    return jnp.sum(slot_pairs[..., None, :, :] == targets, axis=-1).astype(jnp.bfloat16)


def swiglu_rows(rows, gate_local, up_local):
    gate_val = jnp.dot(rows, gate_local, preferred_element_type=jnp.float32)
    up_val = jnp.dot(rows, up_local, preferred_element_type=jnp.float32)
    return (jax.nn.silu(gate_val) * up_val).astype(jnp.bfloat16)


def exchange(blocks):
    return lax.all_to_all(blocks, ("et", "ep"), split_axis=0, concat_axis=0, tiled=True)


def local_kernel(kernel, out_shape, args, outside=(), flops=0, moved=0, scratch=(), limit=12):
    return pl.pallas_call(
        kernel,
        out_shape=out_shape,
        in_specs=[WHOLE] * len(args) + [OUTSIDE] * len(outside),
        out_specs=jax.tree.map(lambda _: WHOLE, out_shape),
        scratch_shapes=scratch,
        compiler_params=pltpu.CompilerParams(vmem_limit_bytes=limit << 20),
        cost_estimate=pl.CostEstimate(flops=flops, bytes_accessed=moved, transcendentals=0),
    )(*args, *(pltpu.with_memory_space_constraint(array, pltpu.HBM) for array in outside))


def exact_dot(a, b):
    return jnp.dot(a, b, preferred_element_type=jnp.float32)


def transposed_dot(a, b):
    return lax.dot_general(a, b, (((0,), (0,)), ((), ())), preferred_element_type=jnp.float32)


def iota(shape, dim):
    return lax.broadcasted_iota(jnp.int32, shape, dim)


def as_column(row):
    size = row.shape[1]
    eye = iota((size, size), 0) == iota((size, size), 1)
    return jnp.sum(jnp.where(eye, row, jnp.zeros_like(row)), axis=1, keepdims=True)


def as_row(column):
    size = column.shape[0]
    eye = iota((size, size), 0) == iota((size, size), 1)
    return jnp.sum(jnp.where(eye, column, jnp.zeros_like(column)), axis=0, keepdims=True)


def pack_kernel(ids_hbm, tokens_hbm, out_ref, ids_ref, sems):
    named = pltpu.make_async_copy(ids_hbm, ids_ref, sems.at[0])
    named.start()
    copy = pltpu.make_async_copy(tokens_hbm, out_ref.at[:, 128:], sems.at[1])
    copy.start()
    named.wait()
    names = ids_ref[...].astype(jnp.float32)
    lane = iota((out_ref.shape[0], 128), 1)
    out_ref[:, :128] = jnp.where(lane == 0, as_column(names[0:1]), as_column(names[1:2])).astype(out_ref.dtype)
    copy.wait()


def rows_of(ids_block, source, expert, rows, tok_rows, capacity):
    tall = ids_block.shape[0]
    names = ids_block.astype(jnp.float32)
    expert = expert.astype(jnp.float32)
    named = (names[:, 0:1] == expert) | (names[:, 1:2] == expert)
    later, earlier = iota((tall, tall), 0), iota((tall, tall), 1)
    lower = ((later > earlier) & (later // tok_rows == earlier // tok_rows)).astype(jnp.bfloat16)
    flags = jnp.broadcast_to(named.astype(jnp.float32), (tall, 128)).astype(jnp.bfloat16)
    before = exact_dot(lower, flags)[:, 0:1].astype(jnp.int32)
    layer = iota((tall, 1), 0) // tok_rows
    target = jnp.where(named, (layer * 2 + source) * capacity + before, -1)
    return (iota((tall, rows), 1) == target).astype(jnp.bfloat16)


def chosen_rows(own_ref, near_ref, expert, rows, tok_rows, capacity, spans):
    core = lax.axis_index("ep") % 2
    blocks = ((own_ref, core), (near_ref, 1 - core))
    sels = [rows_of(ref[:, :128], source, expert, rows, tok_rows, capacity) for ref, source in blocks]
    for start, stop in spans:
        parts = [transposed_dot(sel, ref[:, 128 + start : 128 + stop]) for sel, (ref, _) in zip(sels, blocks)]
        yield (parts[0] + parts[1]).astype(own_ref.dtype)


def select_kernel(tok_rows, capacity, own_ref, near_ref, first_ref, second_ref):
    rows, cut = first_ref.shape
    expert = lax.axis_index("ep") ^ 2
    spans = ((0, cut), (cut, cut + second_ref.shape[1]))
    found = chosen_rows(own_ref, near_ref, expert, rows, tok_rows, capacity, spans)
    for ref, part in zip((first_ref, second_ref), found):
        ref[...] = part


def weight_copies(weights, held, sems, start, step):
    return [
        pltpu.make_async_copy(
            ref.at[pl.ds(start + part * step, step), :], into.at[pl.ds(part * step, step), :], sems.at[which, part]
        )
        for part in range(held[0].shape[0] // step)
        for which, (ref, into) in enumerate(zip(weights, held))
    ]


def fetch_kernel(step, tok_rows, capacity, own_ref, near_ref, *refs):
    gate_hbm, up_hbm, stay_ref, gate_held, up_held, sems = refs
    copies = weight_copies((gate_hbm, up_hbm), (gate_held, up_held), sems, 0, step)
    for copy in copies:
        copy.start()
    rows, width = stay_ref.shape
    expert = lax.axis_index("ep")
    (stay_ref[...],) = chosen_rows(own_ref, near_ref, expert, rows, tok_rows, capacity, ((0, width),))
    for copy in copies:
        copy.wait()


def gather_rows(x_ref, stay, far):
    rows = stay.shape[0]
    chip = lax.axis_index("ep") // 2
    x_ref[pl.ds(pl.multiple_of(chip * rows, rows), rows), :] = stay
    x_ref[pl.ds(pl.multiple_of((1 - chip) * rows, rows), rows), :] = far


def first_kernel(step, far_ref, stay_ref, gate_held, up_held, gate_hbm, up_hbm, *refs):
    gate_ref, up_ref, gate_rest, up_rest, x_ref, sems = refs
    copies = weight_copies((gate_hbm, up_hbm), (gate_rest, up_rest), sems, gate_held.shape[0], step)
    for copy in copies:
        copy.start()
    cut = far_ref.shape[1]
    gather_rows(x_ref, stay_ref[:, :cut], far_ref[...])
    gate_ref[...] = exact_dot(x_ref[...], gate_held[:cut, :])
    up_ref[...] = exact_dot(x_ref[...], up_held[:cut, :])
    for copy in copies:
        copy.wait()


def second_kernel(folds, experts, far_ref, stay_ref, gate_in, up_in, *refs):
    gate_held, up_held, gate_rest, up_rest, out_ref, x_ref, hidden_ref = refs
    cut = stay_ref.shape[1] - far_ref.shape[1]
    gather_rows(x_ref, stay_ref[:, cut:], far_ref[...])
    middle = gate_held.shape[0] - cut
    sums = []
    for held, rest, total in ((gate_held, gate_rest, gate_in), (up_held, up_rest, up_in)):
        total = total[...] + exact_dot(x_ref[:, middle:], rest[...])
        if middle:
            total = total + exact_dot(x_ref[:, :middle], held[cut:, :])
        sums.append(total)
    gate_val, up_val = sums
    hidden_ref[...] = gate_val / (1.0 + jnp.exp(-gate_val)) * up_val
    store_blocks(folds, experts, hidden_ref, out_ref)


def store_blocks(folds, experts, hidden_ref, out_ref):
    peers = out_ref.shape[0]
    capacity = hidden_ref.shape[0] // peers
    span = hidden_ref.shape[1] // folds
    for peer in range(peers):
        layer, chip, core = peer // experts, peer % experts // 2, peer % 2
        start = (chip * (peers // 2) + layer * 2 + core) * capacity
        rows = hidden_ref[start : start + capacity, :]
        pieces = [rows[:, fold * span : (fold + 1) * span] for fold in range(folds)]
        out_ref[peer] = jnp.concatenate(pieces, axis=0).astype(out_ref.dtype)


def routed_by_columns(tokens, expert_ids, gate_local, up_local, peers, capacity, folds):
    tok_rows, width = tokens.shape
    units = gate_local.shape[1]
    experts = 4
    rows = peers * capacity
    half = rows // 2
    cut = 7 * width // 12
    held = 2 * width // 3
    rest = width - held
    step = 256
    kind = tokens.dtype

    def array(*shape):
        return jax.ShapeDtypeStruct(shape, kind)

    def swap(block, bit):
        return lax.ppermute(block, "ep", [(i, i ^ bit) for i in range(experts)])

    packed = local_kernel(
        pack_kernel,
        array(tok_rows, 128 + width),
        (),
        (expert_ids.T, tokens),
        scratch=[pltpu.VMEM((2, tok_rows), jnp.int32), pltpu.SemaphoreType.DMA((2,))],
    )
    own = lax.all_gather(packed, "et", axis=0, tiled=True)
    near = swap(own, 1)
    first, second = local_kernel(
        functools.partial(select_kernel, tok_rows, capacity),
        [array(half, cut), array(half, width - cut)],
        (own, near),
        flops=4 * own.shape[0] * half * width,
        moved=4 * own.size,
    )
    far, later = swap(first, 2), swap(second, 2)
    stay, gate_held, up_held = local_kernel(
        functools.partial(fetch_kernel, step, tok_rows, capacity),
        [array(half, width)] + [pltpu.VMEM((held, units), kind)] * 2,
        (own, near),
        (gate_local, up_local),
        moved=8 * held * units,
        scratch=[pltpu.SemaphoreType.DMA((2, held // step))],
    )
    far, gate_held, up_held = lax.optimization_barrier((far, gate_held, up_held))
    gate_sum, up_sum, gate_rest, up_rest = local_kernel(
        functools.partial(first_kernel, step),
        [jax.ShapeDtypeStruct((rows, units), jnp.float32)] * 2 + [pltpu.VMEM((rest, units), kind)] * 2,
        (far, stay, gate_held, up_held),
        (gate_local, up_local),
        flops=4 * rows * cut * units,
        moved=4 * rest * units,
        scratch=[pltpu.VMEM((rows, cut), kind), pltpu.SemaphoreType.DMA((2, rest // step))],
    )
    later, gate_rest, up_rest = lax.optimization_barrier((later, gate_rest, up_rest))
    return local_kernel(
        functools.partial(second_kernel, folds, experts),
        array(peers, capacity * folds, units // folds),
        (later, stay, gate_sum, up_sum, gate_held, up_held, gate_rest, up_rest),
        flops=4 * rows * (width - cut) * units,
        scratch=[pltpu.VMEM((rows, width - cut), kind), pltpu.VMEM((rows, units), jnp.float32)],
    )


def picks_kernel(experts, capacity, folds, ids_ref, weights_ref, picks_ref, column_ref):
    tok_rows = ids_ref.shape[1]
    both = 2 * tok_rows
    ids = [as_column(ids_ref[slot : slot + 1, :]) for slot in range(2)]
    expert = iota((tok_rows, 128), 1)
    named = ((expert == ids[0]) | (expert == ids[1])).astype(jnp.bfloat16)
    lower = (iota((tok_rows, tok_rows), 0) > iota((tok_rows, tok_rows), 1)).astype(jnp.bfloat16)
    before = exact_dot(lower, named).astype(jnp.int32)
    slot_row, token = iota((both, tok_rows), 0), iota((both, tok_rows), 1)
    target = jnp.zeros((both, 1), jnp.int32)
    column = jnp.zeros((both, 1), jnp.float32)
    for slot, chosen in enumerate(ids):
        position = jnp.sum(jnp.where(expert == chosen, before, 0), axis=1, keepdims=True)
        mask = slot_row == 2 * token + slot
        place = as_row(chosen * (folds * capacity) + position)
        target = target + jnp.sum(jnp.where(mask, place, 0), axis=1, keepdims=True)
        column = column + jnp.sum(jnp.where(mask, weights_ref[slot : slot + 1, :], 0.0), axis=1, keepdims=True)
    column_ref[...] = jnp.broadcast_to(column, column_ref.shape)
    lane = iota((both, experts * folds * capacity), 1)
    for fold in range(folds):
        picks_ref[fold * both : (fold + 1) * both, :] = (lane == target + fold * capacity).astype(picks_ref.dtype)


def final_kernel(experts, folds, picks_ref, column_ref, recv_ref, out_ref):
    tok_rows = out_ref.shape[0]
    both = 2 * tok_rows
    peers, tall, span = recv_ref.shape
    column = column_ref[:, 0:1]
    for part in range(peers // experts):
        block = recv_ref[part * experts : (part + 1) * experts].reshape(experts * tall, span)
        rows = exact_dot(picks_ref[...], block)
        for fold in range(folds):
            scaled = rows[fold * both : (fold + 1) * both] * column
            start = (part * folds + fold) * span
            out_ref[:, :, start : start + span] = scaled.astype(out_ref.dtype).reshape(tok_rows, 2, span)


def finish(expert_ids, gate_weights, received, experts, folds):
    tok_rows = expert_ids.shape[0]
    peers, tall, span = received.shape
    capacity = tall // folds
    kind = received.dtype
    picks, column = local_kernel(
        functools.partial(picks_kernel, experts, capacity, folds),
        [
            jax.ShapeDtypeStruct((2 * tok_rows * folds, experts * tall), kind),
            jax.ShapeDtypeStruct((2 * tok_rows, 128), jnp.float32),
        ],
        (expert_ids.T, gate_weights.T),
        moved=1 << 20,
    )
    units = peers // experts * folds * span
    return local_kernel(
        functools.partial(final_kernel, experts, folds),
        jax.ShapeDtypeStruct((tok_rows, 2, units), kind),
        (picks, column, received),
        moved=4 * received.size,
    )


def body(tokens, expert_ids, gate_weights, w_gate, w_up):
    tok_rows, width = tokens.shape
    experts = lax.axis_size("ep")
    tensor_size = lax.axis_size("et")
    peers = experts * tensor_size
    capacity = tok_rows // 2
    gate_local = w_gate[0]
    up_local = w_up[0]
    if experts == 4 and tensor_size == 4:
        folds = 4
        blocks = routed_by_columns(tokens, expert_ids, gate_local, up_local, peers, capacity, folds)
        return finish(expert_ids, gate_weights, exchange(blocks), experts, folds)
    slot_pairs = place_slots(expert_ids, experts, capacity)
    selector = build_select(slot_pairs, experts * capacity)
    buffer = jnp.dot(selector, tokens, preferred_element_type=jnp.float32).astype(jnp.bfloat16)
    buffer = buffer.reshape(1, experts, capacity * width // 128, 128)
    buffer = jnp.broadcast_to(buffer, (tensor_size,) + buffer.shape[1:])
    arrived = exchange(buffer.reshape(peers, capacity * width // 128, 128))
    hidden = swiglu_rows(arrived.reshape(peers * capacity, width), gate_local, up_local)
    units = hidden.shape[1]
    returned = exchange(hidden.reshape(peers, capacity * units // 128, 128))
    returned = returned.reshape(tensor_size, experts * capacity, units)
    targets = jnp.arange(experts * capacity, dtype=jnp.int32)
    picker = (slot_pairs[:, :, None] == targets[None, None, :]).astype(jnp.bfloat16)
    gathered = jnp.einsum("tsj,ejf->tsef", picker, returned, preferred_element_type=jnp.float32)
    gathered = gathered.reshape(tok_rows, 2, tensor_size * units)
    return (gate_weights[:, :, None] * gathered).astype(jnp.bfloat16)


def solution(mesh):
    in_specs = (
        P(("groups", "et", "ep"), None),
        P(("groups", "et", "ep"), None),
        P(("groups", "et", "ep"), None),
        P("ep", None, "et"),
        P("ep", None, "et"),
    )
    out_specs = P(("groups", "et", "ep"), None, None)
    return jax.shard_map(body, mesh=mesh, in_specs=in_specs, out_specs=out_specs, check_vma=False)
```

```python
import functools

import jax
import jax.numpy as jnp
from jax import lax
from jax.experimental import pallas as pl
from jax.experimental.pallas import tpu as pltpu
from jax.sharding import PartitionSpec as P

WHOLE = pl.BlockSpec(memory_space=pltpu.VMEM)
OUTSIDE = pl.BlockSpec(memory_space=pltpu.HBM)


def place_slots(id_block, experts, capacity):
    flat_ids = id_block.reshape(-1)
    onehot = (flat_ids[:, None] == jnp.arange(experts, dtype=jnp.int32)[None, :]).astype(jnp.int32)
    before = jnp.cumsum(onehot, axis=0) - onehot
    position = jnp.sum(before * onehot, axis=1)
    return (flat_ids * capacity + position).reshape(id_block.shape)


def build_select(slot_pairs, total):
    targets = jnp.arange(total, dtype=jnp.int32).reshape(-1, 1, 1)
    return jnp.sum(slot_pairs[..., None, :, :] == targets, axis=-1).astype(jnp.bfloat16)


def swiglu_rows(rows, gate_local, up_local):
    gate_val = jnp.dot(rows, gate_local, preferred_element_type=jnp.float32)
    up_val = jnp.dot(rows, up_local, preferred_element_type=jnp.float32)
    return (jax.nn.silu(gate_val) * up_val).astype(jnp.bfloat16)


def exchange(blocks):
    return lax.all_to_all(blocks, ("et", "ep"), split_axis=0, concat_axis=0, tiled=True)


def local_kernel(kernel, out_shape, args, outside=(), flops=0, moved=0, scratch=(), limit=12):
    return pl.pallas_call(
        kernel,
        out_shape=out_shape,
        in_specs=[WHOLE] * len(args) + [OUTSIDE] * len(outside),
        out_specs=jax.tree.map(lambda _: WHOLE, out_shape),
        scratch_shapes=scratch,
        compiler_params=pltpu.CompilerParams(vmem_limit_bytes=limit << 20),
        cost_estimate=pl.CostEstimate(flops=flops, bytes_accessed=moved, transcendentals=0),
    )(*args, *(pltpu.with_memory_space_constraint(array, pltpu.HBM) for array in outside))


def exact_dot(a, b):
    return jnp.dot(a, b, preferred_element_type=jnp.float32)


def transposed_dot(a, b):
    return lax.dot_general(a, b, (((0,), (0,)), ((), ())), preferred_element_type=jnp.float32)


def iota(shape, dim):
    return lax.broadcasted_iota(jnp.int32, shape, dim)


def as_column(row):
    size = row.shape[1]
    eye = iota((size, size), 0) == iota((size, size), 1)
    return jnp.sum(jnp.where(eye, row, jnp.zeros_like(row)), axis=1, keepdims=True)


def as_row(column):
    size = column.shape[0]
    eye = iota((size, size), 0) == iota((size, size), 1)
    return jnp.sum(jnp.where(eye, column, jnp.zeros_like(column)), axis=0, keepdims=True)


def pack_kernel(ids_hbm, tokens_hbm, out_ref, ids_ref, sems):
    named = pltpu.make_async_copy(ids_hbm, ids_ref, sems.at[0])
    named.start()
    copy = pltpu.make_async_copy(tokens_hbm, out_ref.at[:, 128:], sems.at[1])
    copy.start()
    named.wait()
    names = ids_ref[...].astype(jnp.float32)
    lane = iota((out_ref.shape[0], 128), 1)
    out_ref[:, :128] = jnp.where(lane == 0, as_column(names[0:1]), as_column(names[1:2])).astype(out_ref.dtype)
    copy.wait()


def rows_of(ids_block, source, expert, rows, tok_rows, capacity):
    tall = ids_block.shape[0]
    names = ids_block.astype(jnp.float32)
    expert = expert.astype(jnp.float32)
    named = (names[:, 0:1] == expert) | (names[:, 1:2] == expert)
    later, earlier = iota((tall, tall), 0), iota((tall, tall), 1)
    lower = ((later > earlier) & (later // tok_rows == earlier // tok_rows)).astype(jnp.bfloat16)
    flags = jnp.broadcast_to(named.astype(jnp.float32), (tall, 128)).astype(jnp.bfloat16)
    before = exact_dot(lower, flags)[:, 0:1].astype(jnp.int32)
    layer = iota((tall, 1), 0) // tok_rows
    target = jnp.where(named, (layer * 2 + source) * capacity + before, -1)
    return (iota((tall, rows), 1) == target).astype(jnp.bfloat16)


def picked(ref, source, expert, rows, tok_rows, capacity, start, stop):
    sel = rows_of(ref[:, :128], source, expert, rows, tok_rows, capacity)
    return transposed_dot(sel, ref[:, 128 + start : 128 + stop])


def cut_kernel(in_ref, out_ref):
    out_ref[...] = in_ref[:, : out_ref.shape[1]]


def select_kernel(tok_rows, capacity, own_ref, near_ref, out_ref):
    expert, core = lax.axis_index("ep") ^ 2, lax.axis_index("ep") % 2
    rows, span = out_ref.shape
    stop = own_ref.shape[1] - 128
    parts = [
        picked(ref, source, expert, rows, tok_rows, capacity, stop - span, stop)
        for ref, source in ((own_ref, core), (near_ref, 1 - core))
    ]
    out_ref[...] = (parts[0] + parts[1]).astype(out_ref.dtype)


def weight_copies(weights, held, sems, start, step):
    return [
        pltpu.make_async_copy(
            ref.at[pl.ds(start + part * step, step), :], into.at[pl.ds(part * step, step), :], sems.at[which, part]
        )
        for part in range(held[0].shape[0] // step)
        for which, (ref, into) in enumerate(zip(weights, held))
    ]


def fetch_kernel(start, step, tok_rows, capacity, swapped, *refs):
    blocks = refs[: len(swapped)]
    gate_hbm, up_hbm, rows_ref, gate_held, up_held, sems = refs[len(swapped) :]
    copies = weight_copies((gate_hbm, up_hbm), (gate_held, up_held), sems, start, step)
    for copy in copies:
        copy.start()
    rows, width = rows_ref.shape
    expert, core = lax.axis_index("ep"), lax.axis_index("ep") % 2
    rows_ref[...] = sum(
        picked(ref, core ^ other, expert, rows, tok_rows, capacity, 0, width) for ref, other in zip(blocks, swapped)
    ).astype(rows_ref.dtype)
    for copy in copies:
        copy.wait()


def gather_rows(x_ref, stay, far):
    rows = stay.shape[0]
    chip = lax.axis_index("ep") // 2
    x_ref[pl.ds(pl.multiple_of(chip * rows, rows), rows), :] = stay
    x_ref[pl.ds(pl.multiple_of((1 - chip) * rows, rows), rows), :] = far


def partial_product(x_ref, pieces, start):
    total, base, stop = None, 0, start + x_ref.shape[1]
    for piece in pieces:
        low, high = max(base, start), min(base + piece.shape[0], stop)
        if low < high:
            product = exact_dot(x_ref[:, low - start : high - start], piece[low - base : high - base, :])
            total = product if total is None else total + product
        base = base + piece.shape[0]
    return total


def first_kernel(step, tok_rows, capacity, held, other_ref, part_ref, stay_ref, *refs):
    gates, ups = refs[: 2 * held : 2], refs[1 : 2 * held : 2]
    gate_hbm, up_hbm, gate_ref, up_ref, gate_rest, up_rest, x_ref, sems = refs[2 * held :]
    copies = weight_copies((gate_hbm, up_hbm), (gate_rest, up_rest), sems, sum(ref.shape[0] for ref in gates), step)
    for copy in copies:
        copy.start()
    rows, cut = part_ref.shape
    expert, core = lax.axis_index("ep"), lax.axis_index("ep") % 2
    far = picked(other_ref, 1 - core, expert, rows, tok_rows, capacity, 0, cut) + part_ref[...].astype(jnp.float32)
    gather_rows(x_ref, stay_ref[:, :cut], far.astype(x_ref.dtype))
    gate_ref[...] = partial_product(x_ref, gates, 0)
    up_ref[...] = partial_product(x_ref, ups, 0)
    for copy in copies:
        copy.wait()


def second_kernel(folds, experts, far_ref, stay_ref, gate_in, up_in, *refs):
    gates, ups, (out_ref, x_ref, hidden_ref) = refs[:-3:2], refs[1:-3:2], refs[-3:]
    cut = stay_ref.shape[1] - far_ref.shape[1]
    gather_rows(x_ref, stay_ref[:, cut:], far_ref[...])
    gate_val = gate_in[...] + partial_product(x_ref, gates, cut)
    up_val = up_in[...] + partial_product(x_ref, ups, cut)
    hidden_ref[...] = gate_val / (1.0 + jnp.exp(-gate_val)) * up_val
    store_blocks(folds, experts, hidden_ref, out_ref)


def store_blocks(folds, experts, hidden_ref, out_ref):
    peers = out_ref.shape[0]
    capacity = hidden_ref.shape[0] // peers
    span = hidden_ref.shape[1] // folds
    for peer in range(peers):
        layer, chip, core = peer // experts, peer % experts // 2, peer % 2
        start = (chip * (peers // 2) + layer * 2 + core) * capacity
        rows = hidden_ref[start : start + capacity, :]
        pieces = [rows[:, fold * span : (fold + 1) * span] for fold in range(folds)]
        out_ref[peer] = jnp.concatenate(pieces, axis=0).astype(out_ref.dtype)


def routed_by_columns(tokens, expert_ids, gate_local, up_local, peers, capacity, folds):
    tok_rows, width = tokens.shape
    units = gate_local.shape[1]
    experts = 4
    rows = peers * capacity
    half = rows // 2
    cut = 11 * width // 24
    helds = (7 * width // 12, width // 6)
    step = 256
    kind = tokens.dtype

    def array(*shape):
        return jax.ShapeDtypeStruct(shape, kind)

    def swap(block, bit):
        return lax.ppermute(block, "ep", [(i, i ^ bit) for i in range(experts)])

    packed = local_kernel(
        pack_kernel,
        array(tok_rows, 128 + width),
        (),
        (expert_ids.T, tokens),
        scratch=[pltpu.VMEM((2, tok_rows), jnp.int32), pltpu.SemaphoreType.DMA((2,))],
    )
    own = lax.all_gather(packed, "et", axis=0, tiled=True)
    part = local_kernel(cut_kernel, array(own.shape[0], 128 + cut), (own,))
    near, far = swap(own, 1), swap(part, 2)
    later = local_kernel(functools.partial(select_kernel, tok_rows, capacity), array(half, width - cut), (own, near))
    later_far = swap(later, 2)

    def fetch(start, held, blocks, swapped, span):
        return local_kernel(
            functools.partial(fetch_kernel, start, step, tok_rows, capacity, swapped),
            [array(half, span)] + [pltpu.VMEM((held, units), kind)] * 2,
            blocks,
            (gate_local, up_local),
            scratch=[pltpu.SemaphoreType.DMA((2, held // step))],
        )

    own, near, later = lax.optimization_barrier((own, near, later))
    stay, *pieces = fetch(0, helds[0], (own, near), (0, 1), width)
    far, *pieces = lax.optimization_barrier((far, *pieces))
    far_other = swap(far, 1)
    far_part, *more = fetch(helds[0], helds[1], (far,), (0,), cut)
    far_other, *more = lax.optimization_barrier((far_other, *more))
    pieces = (*pieces, *more)
    rest = width - sum(helds)
    gate_sum, up_sum, *last = local_kernel(
        functools.partial(first_kernel, step, tok_rows, capacity, len(helds)),
        [jax.ShapeDtypeStruct((rows, units), jnp.float32)] * 2 + [pltpu.VMEM((rest, units), kind)] * 2,
        (far_other, far_part, stay, *pieces),
        (gate_local, up_local),
        scratch=[pltpu.VMEM((rows, cut), kind), pltpu.SemaphoreType.DMA((2, rest // step))],
    )
    later_far, *last = lax.optimization_barrier((later_far, *last))
    return local_kernel(
        functools.partial(second_kernel, folds, experts),
        array(peers, capacity * folds, units // folds),
        (later_far, stay, gate_sum, up_sum, *pieces, *last),
        scratch=[pltpu.VMEM((rows, width - cut), kind), pltpu.VMEM((rows, units), jnp.float32)],
    )


def picks_kernel(experts, capacity, folds, ids_ref, weights_ref, picks_ref, column_ref):
    tok_rows = ids_ref.shape[1]
    both = 2 * tok_rows
    ids = [as_column(ids_ref[slot : slot + 1, :]) for slot in range(2)]
    expert = iota((tok_rows, 128), 1)
    named = ((expert == ids[0]) | (expert == ids[1])).astype(jnp.bfloat16)
    lower = (iota((tok_rows, tok_rows), 0) > iota((tok_rows, tok_rows), 1)).astype(jnp.bfloat16)
    before = exact_dot(lower, named).astype(jnp.int32)
    slot_row, token = iota((both, tok_rows), 0), iota((both, tok_rows), 1)
    target = jnp.zeros((both, 1), jnp.int32)
    column = jnp.zeros((both, 1), jnp.float32)
    for slot, chosen in enumerate(ids):
        position = jnp.sum(jnp.where(expert == chosen, before, 0), axis=1, keepdims=True)
        mask = slot_row == 2 * token + slot
        place = as_row(chosen * (folds * capacity) + position)
        target = target + jnp.sum(jnp.where(mask, place, 0), axis=1, keepdims=True)
        column = column + jnp.sum(jnp.where(mask, weights_ref[slot : slot + 1, :], 0.0), axis=1, keepdims=True)
    column_ref[...] = jnp.broadcast_to(column, column_ref.shape)
    lane = iota((both, experts * folds * capacity), 1)
    for fold in range(folds):
        picks_ref[fold * both : (fold + 1) * both, :] = (lane == target + fold * capacity).astype(picks_ref.dtype)


def final_kernel(experts, folds, picks_ref, column_ref, recv_ref, out_ref):
    tok_rows = out_ref.shape[0]
    both = 2 * tok_rows
    peers, tall, span = recv_ref.shape
    column = column_ref[:, 0:1]
    for part in range(peers // experts):
        block = recv_ref[part * experts : (part + 1) * experts].reshape(experts * tall, span)
        rows = exact_dot(picks_ref[...], block)
        for fold in range(folds):
            scaled = rows[fold * both : (fold + 1) * both] * column
            start = (part * folds + fold) * span
            out_ref[:, :, start : start + span] = scaled.astype(out_ref.dtype).reshape(tok_rows, 2, span)


def finish(expert_ids, gate_weights, received, experts, folds):
    tok_rows = expert_ids.shape[0]
    peers, tall, span = received.shape
    capacity = tall // folds
    kind = received.dtype
    picks, column = local_kernel(
        functools.partial(picks_kernel, experts, capacity, folds),
        [
            jax.ShapeDtypeStruct((2 * tok_rows * folds, experts * tall), kind),
            jax.ShapeDtypeStruct((2 * tok_rows, 128), jnp.float32),
        ],
        (expert_ids.T, gate_weights.T),
        moved=1 << 20,
    )
    units = peers // experts * folds * span
    return local_kernel(
        functools.partial(final_kernel, experts, folds),
        jax.ShapeDtypeStruct((tok_rows, 2, units), kind),
        (picks, column, received),
        moved=4 * received.size,
    )


def body(tokens, expert_ids, gate_weights, w_gate, w_up):
    tok_rows, width = tokens.shape
    experts = lax.axis_size("ep")
    tensor_size = lax.axis_size("et")
    peers = experts * tensor_size
    capacity = tok_rows // 2
    gate_local = w_gate[0]
    up_local = w_up[0]
    if experts == 4 and tensor_size == 4:
        folds = 4
        blocks = routed_by_columns(tokens, expert_ids, gate_local, up_local, peers, capacity, folds)
        return finish(expert_ids, gate_weights, exchange(blocks), experts, folds)
    slot_pairs = place_slots(expert_ids, experts, capacity)
    selector = build_select(slot_pairs, experts * capacity)
    buffer = jnp.dot(selector, tokens, preferred_element_type=jnp.float32).astype(jnp.bfloat16)
    buffer = buffer.reshape(1, experts, capacity * width // 128, 128)
    buffer = jnp.broadcast_to(buffer, (tensor_size,) + buffer.shape[1:])
    arrived = exchange(buffer.reshape(peers, capacity * width // 128, 128))
    hidden = swiglu_rows(arrived.reshape(peers * capacity, width), gate_local, up_local)
    units = hidden.shape[1]
    returned = exchange(hidden.reshape(peers, capacity * units // 128, 128))
    returned = returned.reshape(tensor_size, experts * capacity, units)
    targets = jnp.arange(experts * capacity, dtype=jnp.int32)
    picker = (slot_pairs[:, :, None] == targets[None, None, :]).astype(jnp.bfloat16)
    gathered = jnp.einsum("tsj,ejf->tsef", picker, returned, preferred_element_type=jnp.float32)
    gathered = gathered.reshape(tok_rows, 2, tensor_size * units)
    return (gate_weights[:, :, None] * gathered).astype(jnp.bfloat16)


def solution(mesh):
    in_specs = (
        P(("groups", "et", "ep"), None),
        P(("groups", "et", "ep"), None),
        P(("groups", "et", "ep"), None),
        P("ep", None, "et"),
        P("ep", None, "et"),
    )
    out_specs = P(("groups", "et", "ep"), None, None)
    return jax.shard_map(body, mesh=mesh, in_specs=in_specs, out_specs=out_specs, check_vma=False)
```

```python
import functools

import jax
import jax.numpy as jnp
from jax import lax
from jax.experimental import pallas as pl
from jax.experimental.pallas import tpu as pltpu
from jax.sharding import PartitionSpec as P

WHOLE = pl.BlockSpec(memory_space=pltpu.VMEM)
OUTSIDE = pl.BlockSpec(memory_space=pltpu.HBM)


def place_slots(id_block, experts, capacity):
    flat_ids = id_block.reshape(-1)
    onehot = (flat_ids[:, None] == jnp.arange(experts, dtype=jnp.int32)[None, :]).astype(jnp.int32)
    before = jnp.cumsum(onehot, axis=0) - onehot
    position = jnp.sum(before * onehot, axis=1)
    return (flat_ids * capacity + position).reshape(id_block.shape)


def build_select(slot_pairs, total):
    targets = jnp.arange(total, dtype=jnp.int32).reshape(-1, 1, 1)
    return jnp.sum(slot_pairs[..., None, :, :] == targets, axis=-1).astype(jnp.bfloat16)


def swiglu_rows(rows, gate_local, up_local):
    gate_val = jnp.dot(rows, gate_local, preferred_element_type=jnp.float32)
    up_val = jnp.dot(rows, up_local, preferred_element_type=jnp.float32)
    return (jax.nn.silu(gate_val) * up_val).astype(jnp.bfloat16)


def exchange(blocks):
    return lax.all_to_all(blocks, ("et", "ep"), split_axis=0, concat_axis=0, tiled=True)


def local_kernel(kernel, out_shape, args, outside=(), flops=0, moved=0, scratch=(), limit=12):
    return pl.pallas_call(
        kernel,
        out_shape=out_shape,
        in_specs=[WHOLE] * len(args) + [OUTSIDE] * len(outside),
        out_specs=jax.tree.map(lambda _: WHOLE, out_shape),
        scratch_shapes=scratch,
        compiler_params=pltpu.CompilerParams(vmem_limit_bytes=limit << 20),
        cost_estimate=pl.CostEstimate(flops=flops, bytes_accessed=moved, transcendentals=0),
    )(*args, *(pltpu.with_memory_space_constraint(array, pltpu.HBM) for array in outside))


def exact_dot(a, b):
    return jnp.dot(a, b, preferred_element_type=jnp.float32)


def transposed_dot(a, b):
    return lax.dot_general(a, b, (((0,), (0,)), ((), ())), preferred_element_type=jnp.float32)


def iota(shape, dim):
    return lax.broadcasted_iota(jnp.int32, shape, dim)


def as_column(row):
    size = row.shape[1]
    eye = iota((size, size), 0) == iota((size, size), 1)
    return jnp.sum(jnp.where(eye, row, jnp.zeros_like(row)), axis=1, keepdims=True)


def as_row(column):
    size = column.shape[0]
    eye = iota((size, size), 0) == iota((size, size), 1)
    return jnp.sum(jnp.where(eye, column, jnp.zeros_like(column)), axis=0, keepdims=True)


def pack_kernel(ids_hbm, tokens_hbm, out_ref, ids_ref, sems):
    named = pltpu.make_async_copy(ids_hbm, ids_ref, sems.at[0])
    named.start()
    copy = pltpu.make_async_copy(tokens_hbm, out_ref.at[:, 128:], sems.at[1])
    copy.start()
    named.wait()
    names = ids_ref[...].astype(jnp.float32)
    lane = iota((out_ref.shape[0], 128), 1)
    out_ref[:, :128] = jnp.where(lane == 0, as_column(names[0:1]), as_column(names[1:2])).astype(out_ref.dtype)
    copy.wait()


def rows_of(ids_block, source, expert, rows, tok_rows, capacity):
    tall = ids_block.shape[0]
    names = ids_block.astype(jnp.float32)
    expert = expert.astype(jnp.float32)
    named = (names[:, 0:1] == expert) | (names[:, 1:2] == expert)
    later, earlier = iota((tall, tall), 0), iota((tall, tall), 1)
    lower = ((later > earlier) & (later // tok_rows == earlier // tok_rows)).astype(jnp.bfloat16)
    flags = jnp.broadcast_to(named.astype(jnp.float32), (tall, 128)).astype(jnp.bfloat16)
    before = exact_dot(lower, flags)[:, 0:1].astype(jnp.int32)
    layer = iota((tall, 1), 0) // tok_rows
    target = jnp.where(named, (layer * 2 + source) * capacity + before, -1)
    return (iota((tall, rows), 1) == target).astype(jnp.bfloat16)


def picked(ref, source, expert, rows, tok_rows, capacity, start, stop):
    sel = rows_of(ref[:, :128], source, expert, rows, tok_rows, capacity)
    return transposed_dot(sel, ref[:, 128 + start : 128 + stop])


def cut_kernel(in_ref, out_ref):
    out_ref[...] = in_ref[:, : out_ref.shape[1]]


def select_kernel(tok_rows, capacity, own_ref, near_ref, out_ref):
    expert, core = lax.axis_index("ep") ^ 2, lax.axis_index("ep") % 2
    rows, span = out_ref.shape
    stop = own_ref.shape[1] - 128
    parts = [
        picked(ref, source, expert, rows, tok_rows, capacity, stop - span, stop)
        for ref, source in ((own_ref, core), (near_ref, 1 - core))
    ]
    out_ref[...] = (parts[0] + parts[1]).astype(out_ref.dtype)


def weight_copies(weights, held, sems, start, step):
    return [
        pltpu.make_async_copy(
            ref.at[pl.ds(start + part * step, step), :], into.at[pl.ds(part * step, step), :], sems.at[which, part]
        )
        for part in range(held[0].shape[0] // step)
        for which, (ref, into) in enumerate(zip(weights, held))
    ]


def fetch_kernel(start, step, tok_rows, capacity, swapped, *refs):
    blocks = refs[: len(swapped)]
    up_hbm, rows_ref, up_held, sems = refs[len(swapped) :]
    copies = weight_copies((up_hbm,), (up_held,), sems, start, step)
    for copy in copies:
        copy.start()
    rows, width = rows_ref.shape
    expert, core = lax.axis_index("ep"), lax.axis_index("ep") % 2
    rows_ref[...] = sum(
        picked(ref, core ^ other, expert, rows, tok_rows, capacity, 0, width) for ref, other in zip(blocks, swapped)
    ).astype(rows_ref.dtype)
    for copy in copies:
        copy.wait()


def gather_rows(x_ref, stay, far):
    rows = stay.shape[0]
    chip = lax.axis_index("ep") // 2
    x_ref[pl.ds(pl.multiple_of(chip * rows, rows), rows), :] = stay
    x_ref[pl.ds(pl.multiple_of((1 - chip) * rows, rows), rows), :] = far


def partial_product(x_ref, pieces, start):
    total, base, stop = None, 0, start + x_ref.shape[1]
    for piece in pieces:
        low, high = max(base, start), min(base + piece.shape[0], stop)
        if low < high:
            product = exact_dot(x_ref[:, low - start : high - start], piece[low - base : high - base, :])
            total = product if total is None else total + product
        base = base + piece.shape[0]
    return total


def first_kernel(step, tok_rows, capacity, held, other_ref, part_ref, stay_ref, *refs):
    gate_all, ups = refs[0], refs[1 : 1 + held]
    up_hbm, gate_ref, up_ref, up_rest, x_ref, sems = refs[1 + held :]
    copies = weight_copies((up_hbm,), (up_rest,), sems, sum(ref.shape[0] for ref in ups), step)
    for copy in copies:
        copy.start()
    rows, cut = part_ref.shape
    expert, core = lax.axis_index("ep"), lax.axis_index("ep") % 2
    far = picked(other_ref, 1 - core, expert, rows, tok_rows, capacity, 0, cut) + part_ref[...].astype(jnp.float32)
    gather_rows(x_ref, stay_ref[:, :cut], far.astype(x_ref.dtype))
    gate_ref[...] = partial_product(x_ref, (gate_all.at[0],), 0)
    up_ref[...] = partial_product(x_ref, ups, 0)
    for copy in copies:
        copy.wait()


def second_kernel(folds, experts, far_ref, stay_ref, gate_in, up_in, *refs):
    gate_all, ups, (out_ref, x_ref, hidden_ref) = refs[0], refs[1:-3], refs[-3:]
    cut = stay_ref.shape[1] - far_ref.shape[1]
    gather_rows(x_ref, stay_ref[:, cut:], far_ref[...])
    gate_val = gate_in[...] + partial_product(x_ref, (gate_all.at[0],), cut)
    up_val = up_in[...] + partial_product(x_ref, ups, cut)
    hidden_ref[...] = gate_val / (1.0 + jnp.exp(-gate_val)) * up_val
    store_blocks(folds, experts, hidden_ref, out_ref)


def store_blocks(folds, experts, hidden_ref, out_ref):
    peers = out_ref.shape[0]
    capacity = hidden_ref.shape[0] // peers
    span = hidden_ref.shape[1] // folds
    for peer in range(peers):
        layer, chip, core = peer // experts, peer % experts // 2, peer % 2
        start = (chip * (peers // 2) + layer * 2 + core) * capacity
        rows = hidden_ref[start : start + capacity, :]
        pieces = [rows[:, fold * span : (fold + 1) * span] for fold in range(folds)]
        out_ref[peer] = jnp.concatenate(pieces, axis=0).astype(out_ref.dtype)


def routed_by_columns(tokens, expert_ids, gate_whole, up_local, peers, capacity, folds):
    tok_rows, width = tokens.shape
    units = up_local.shape[1]
    experts = 4
    rows = peers * capacity
    half = rows // 2
    cut = 11 * width // 24
    helds = (2 * width // 3, width // 6)
    step = 256
    kind = tokens.dtype

    def array(*shape):
        return jax.ShapeDtypeStruct(shape, kind)

    def swap(block, bit):
        return lax.ppermute(block, "ep", [(i, i ^ bit) for i in range(experts)])

    packed = local_kernel(
        pack_kernel,
        array(tok_rows, 128 + width),
        (),
        (expert_ids.T, tokens),
        scratch=[pltpu.VMEM((2, tok_rows), jnp.int32), pltpu.SemaphoreType.DMA((2,))],
    )
    own = lax.all_gather(packed, "et", axis=0, tiled=True)
    part = local_kernel(cut_kernel, array(own.shape[0], 128 + cut), (own,))
    near, far = swap(own, 1), swap(part, 2)
    later = local_kernel(functools.partial(select_kernel, tok_rows, capacity), array(half, width - cut), (own, near))
    later_far = swap(later, 2)

    def fetch(start, held, blocks, swapped, span):
        return local_kernel(
            functools.partial(fetch_kernel, start, step, tok_rows, capacity, swapped),
            [array(half, span), pltpu.VMEM((held, units), kind)],
            blocks,
            (up_local,),
            scratch=[pltpu.SemaphoreType.DMA((1, held // step))],
        )

    own, near, later = lax.optimization_barrier((own, near, later))
    stay, *pieces = fetch(0, helds[0], (own, near), (0, 1), width)
    far, *pieces = lax.optimization_barrier((far, *pieces))
    far_other = swap(far, 1)
    far_part, *more = fetch(helds[0], helds[1], (far,), (0,), cut)
    far_other, *more = lax.optimization_barrier((far_other, *more))
    pieces = (*pieces, *more)
    rest = width - sum(helds)
    gate_sum, up_sum, *last = local_kernel(
        functools.partial(first_kernel, step, tok_rows, capacity, len(helds)),
        [jax.ShapeDtypeStruct((rows, units), jnp.float32)] * 2 + [pltpu.VMEM((rest, units), kind)],
        (far_other, far_part, stay, gate_whole, *pieces),
        (up_local,),
        scratch=[pltpu.VMEM((rows, cut), kind), pltpu.SemaphoreType.DMA((1, rest // step))],
    )
    later_far, *last = lax.optimization_barrier((later_far, *last))
    return local_kernel(
        functools.partial(second_kernel, folds, experts),
        array(peers, capacity * folds, units // folds),
        (later_far, stay, gate_sum, up_sum, gate_whole, *pieces, *last),
        scratch=[pltpu.VMEM((rows, width - cut), kind), pltpu.VMEM((rows, units), jnp.float32)],
    )


def picks_kernel(experts, capacity, folds, ids_ref, weights_ref, picks_ref, column_ref):
    tok_rows = ids_ref.shape[1]
    both = 2 * tok_rows
    ids = [as_column(ids_ref[slot : slot + 1, :]) for slot in range(2)]
    expert = iota((tok_rows, 128), 1)
    named = ((expert == ids[0]) | (expert == ids[1])).astype(jnp.bfloat16)
    lower = (iota((tok_rows, tok_rows), 0) > iota((tok_rows, tok_rows), 1)).astype(jnp.bfloat16)
    before = exact_dot(lower, named).astype(jnp.int32)
    slot_row, token = iota((both, tok_rows), 0), iota((both, tok_rows), 1)
    target = jnp.zeros((both, 1), jnp.int32)
    column = jnp.zeros((both, 1), jnp.float32)
    for slot, chosen in enumerate(ids):
        position = jnp.sum(jnp.where(expert == chosen, before, 0), axis=1, keepdims=True)
        mask = slot_row == 2 * token + slot
        place = as_row(chosen * (folds * capacity) + position)
        target = target + jnp.sum(jnp.where(mask, place, 0), axis=1, keepdims=True)
        column = column + jnp.sum(jnp.where(mask, weights_ref[slot : slot + 1, :], 0.0), axis=1, keepdims=True)
    column_ref[...] = jnp.broadcast_to(column, column_ref.shape)
    lane = iota((both, experts * folds * capacity), 1)
    for fold in range(folds):
        picks_ref[fold * both : (fold + 1) * both, :] = (lane == target + fold * capacity).astype(picks_ref.dtype)


def final_kernel(experts, folds, picks_ref, column_ref, recv_ref, out_ref):
    tok_rows = out_ref.shape[0]
    both = 2 * tok_rows
    peers, tall, span = recv_ref.shape
    column = column_ref[:, 0:1]
    for part in range(peers // experts):
        block = recv_ref[part * experts : (part + 1) * experts].reshape(experts * tall, span)
        rows = exact_dot(picks_ref[...], block)
        for fold in range(folds):
            scaled = rows[fold * both : (fold + 1) * both] * column
            start = (part * folds + fold) * span
            out_ref[:, :, start : start + span] = scaled.astype(out_ref.dtype).reshape(tok_rows, 2, span)


def finish(expert_ids, gate_weights, received, experts, folds):
    tok_rows = expert_ids.shape[0]
    peers, tall, span = received.shape
    capacity = tall // folds
    kind = received.dtype
    picks, column = local_kernel(
        functools.partial(picks_kernel, experts, capacity, folds),
        [
            jax.ShapeDtypeStruct((2 * tok_rows * folds, experts * tall), kind),
            jax.ShapeDtypeStruct((2 * tok_rows, 128), jnp.float32),
        ],
        (expert_ids.T, gate_weights.T),
        moved=1 << 20,
    )
    units = peers // experts * folds * span
    return local_kernel(
        functools.partial(final_kernel, experts, folds),
        jax.ShapeDtypeStruct((tok_rows, 2, units), kind),
        (picks, column, received),
        moved=4 * received.size,
    )


def body(tokens, expert_ids, gate_weights, w_gate, w_up):
    tok_rows, width = tokens.shape
    experts = lax.axis_size("ep")
    tensor_size = lax.axis_size("et")
    peers = experts * tensor_size
    capacity = tok_rows // 2
    gate_local = w_gate[0]
    up_local = w_up[0]
    if experts == 4 and tensor_size == 4:
        folds = 4
        blocks = routed_by_columns(tokens, expert_ids, w_gate, up_local, peers, capacity, folds)
        return finish(expert_ids, gate_weights, exchange(blocks), experts, folds)
    slot_pairs = place_slots(expert_ids, experts, capacity)
    selector = build_select(slot_pairs, experts * capacity)
    buffer = jnp.dot(selector, tokens, preferred_element_type=jnp.float32).astype(jnp.bfloat16)
    buffer = buffer.reshape(1, experts, capacity * width // 128, 128)
    buffer = jnp.broadcast_to(buffer, (tensor_size,) + buffer.shape[1:])
    arrived = exchange(buffer.reshape(peers, capacity * width // 128, 128))
    hidden = swiglu_rows(arrived.reshape(peers * capacity, width), gate_local, up_local)
    units = hidden.shape[1]
    returned = exchange(hidden.reshape(peers, capacity * units // 128, 128))
    returned = returned.reshape(tensor_size, experts * capacity, units)
    targets = jnp.arange(experts * capacity, dtype=jnp.int32)
    picker = (slot_pairs[:, :, None] == targets[None, None, :]).astype(jnp.bfloat16)
    gathered = jnp.einsum("tsj,ejf->tsef", picker, returned, preferred_element_type=jnp.float32)
    gathered = gathered.reshape(tok_rows, 2, tensor_size * units)
    return (gate_weights[:, :, None] * gathered).astype(jnp.bfloat16)


def solution(mesh):
    in_specs = (
        P(("groups", "et", "ep"), None),
        P(("groups", "et", "ep"), None),
        P(("groups", "et", "ep"), None),
        P("ep", None, "et"),
        P("ep", None, "et"),
    )
    out_specs = P(("groups", "et", "ep"), None, None)
    return jax.shard_map(body, mesh=mesh, in_specs=in_specs, out_specs=out_specs, check_vma=False)
```

```python
import functools

import jax
import jax.numpy as jnp
from jax import lax
from jax.experimental import pallas as pl
from jax.experimental.pallas import tpu as pltpu
from jax.sharding import PartitionSpec as P

WHOLE = pl.BlockSpec(memory_space=pltpu.VMEM)
OUTSIDE = pl.BlockSpec(memory_space=pltpu.HBM)


def place_slots(id_block, experts, capacity):
    flat_ids = id_block.reshape(-1)
    onehot = (flat_ids[:, None] == jnp.arange(experts, dtype=jnp.int32)[None, :]).astype(jnp.int32)
    before = jnp.cumsum(onehot, axis=0) - onehot
    position = jnp.sum(before * onehot, axis=1)
    return (flat_ids * capacity + position).reshape(id_block.shape)


def build_select(slot_pairs, total):
    targets = jnp.arange(total, dtype=jnp.int32).reshape(-1, 1, 1)
    return jnp.sum(slot_pairs[..., None, :, :] == targets, axis=-1).astype(jnp.bfloat16)


def swiglu_rows(rows, gate_local, up_local):
    gate_val = jnp.dot(rows, gate_local, preferred_element_type=jnp.float32)
    up_val = jnp.dot(rows, up_local, preferred_element_type=jnp.float32)
    return (jax.nn.silu(gate_val) * up_val).astype(jnp.bfloat16)


def exchange(blocks):
    return lax.all_to_all(blocks, ("et", "ep"), split_axis=0, concat_axis=0, tiled=True)


def local_kernel(kernel, out_shape, args, outside=(), flops=0, moved=0, scratch=(), limit=12):
    return pl.pallas_call(
        kernel,
        out_shape=out_shape,
        in_specs=[WHOLE] * len(args) + [OUTSIDE] * len(outside),
        out_specs=jax.tree.map(lambda _: WHOLE, out_shape),
        scratch_shapes=scratch,
        compiler_params=pltpu.CompilerParams(vmem_limit_bytes=limit << 20),
        cost_estimate=pl.CostEstimate(flops=flops, bytes_accessed=moved, transcendentals=0),
    )(*args, *(pltpu.with_memory_space_constraint(array, pltpu.HBM) for array in outside))


def exact_dot(a, b):
    return jnp.dot(a, b, preferred_element_type=jnp.float32)


def transposed_dot(a, b):
    return lax.dot_general(a, b, (((0,), (0,)), ((), ())), preferred_element_type=jnp.float32)


def iota(shape, dim):
    return lax.broadcasted_iota(jnp.int32, shape, dim)


def as_column(row):
    size = row.shape[1]
    eye = iota((size, size), 0) == iota((size, size), 1)
    return jnp.sum(jnp.where(eye, row, jnp.zeros_like(row)), axis=1, keepdims=True)


def as_row(column):
    size = column.shape[0]
    eye = iota((size, size), 0) == iota((size, size), 1)
    return jnp.sum(jnp.where(eye, column, jnp.zeros_like(column)), axis=0, keepdims=True)


def pack_kernel(ids_hbm, tokens_hbm, out_ref, ids_ref, sems):
    named = pltpu.make_async_copy(ids_hbm, ids_ref, sems.at[0])
    named.start()
    copy = pltpu.make_async_copy(tokens_hbm, out_ref.at[:, 128:], sems.at[1])
    copy.start()
    named.wait()
    names = ids_ref[...].astype(jnp.float32)
    lane = iota((out_ref.shape[0], 128), 1)
    out_ref[:, :128] = jnp.where(lane == 0, as_column(names[0:1]), as_column(names[1:2])).astype(out_ref.dtype)
    copy.wait()


def rows_of(ids_block, source, expert, rows, tok_rows, capacity):
    tall = ids_block.shape[0]
    names = ids_block.astype(jnp.float32)
    expert = expert.astype(jnp.float32)
    named = (names[:, 0:1] == expert) | (names[:, 1:2] == expert)
    later, earlier = iota((tall, tall), 0), iota((tall, tall), 1)
    lower = ((later > earlier) & (later // tok_rows == earlier // tok_rows)).astype(jnp.bfloat16)
    flags = jnp.broadcast_to(named.astype(jnp.float32), (tall, 128)).astype(jnp.bfloat16)
    before = exact_dot(lower, flags)[:, 0:1].astype(jnp.int32)
    layer = iota((tall, 1), 0) // tok_rows
    target = jnp.where(named, (layer * 2 + source) * capacity + before, -1)
    return (iota((tall, rows), 1) == target).astype(jnp.bfloat16)


def picked(ref, source, expert, rows, tok_rows, capacity, start, stop):
    sel = rows_of(ref[:, :128], source, expert, rows, tok_rows, capacity)
    return transposed_dot(sel, ref[:, 128 + start : 128 + stop])


def cut_kernel(in_ref, out_ref):
    out_ref[...] = in_ref[:, : out_ref.shape[1]]


def select_kernel(tok_rows, capacity, own_ref, near_ref, *outs):
    expert, core = lax.axis_index("ep") ^ 2, lax.axis_index("ep") % 2
    rows = outs[0].shape[0]
    found = [
        (rows_of(ref[:, :128], source, expert, rows, tok_rows, capacity), ref)
        for ref, source in ((own_ref, core), (near_ref, 1 - core))
    ]
    start = own_ref.shape[1] - sum(out.shape[1] for out in outs)
    for out in outs:
        stop = start + out.shape[1]
        out[...] = sum(transposed_dot(sel, ref[:, start:stop]) for sel, ref in found).astype(out.dtype)
        start = stop


def weight_copies(weights, held, sems, start, step):
    return [
        pltpu.make_async_copy(
            ref.at[pl.ds(start + part * step, step), :], into.at[pl.ds(part * step, step), :], sems.at[which, part]
        )
        for part in range(held[0].shape[0] // step)
        for which, (ref, into) in enumerate(zip(weights, held))
    ]


def fetch_kernel(start, step, tok_rows, capacity, swapped, *refs):
    blocks = refs[: len(swapped)]
    gate_hbm, up_hbm, rows_ref, gate_held, up_held, sems = refs[len(swapped) :]
    copies = weight_copies((gate_hbm, up_hbm), (gate_held, up_held), sems, start, step)
    for copy in copies:
        copy.start()
    rows, width = rows_ref.shape
    expert, core = lax.axis_index("ep"), lax.axis_index("ep") % 2
    rows_ref[...] = sum(
        picked(ref, core ^ other, expert, rows, tok_rows, capacity, 0, width) for ref, other in zip(blocks, swapped)
    ).astype(rows_ref.dtype)
    for copy in copies:
        copy.wait()


def gather_rows(x_ref, stay, far):
    rows = stay.shape[0]
    chip = lax.axis_index("ep") // 2
    x_ref[pl.ds(pl.multiple_of(chip * rows, rows), rows), :] = stay
    x_ref[pl.ds(pl.multiple_of((1 - chip) * rows, rows), rows), :] = far


def partial_product(x_ref, pieces, start):
    total, base, stop = None, 0, start + x_ref.shape[1]
    for piece in pieces:
        low, high = max(base, start), min(base + piece.shape[0], stop)
        if low < high:
            product = exact_dot(x_ref[:, low - start : high - start], piece[low - base : high - base, :])
            total = product if total is None else total + product
        base = base + piece.shape[0]
    return total


def first_kernel(step, tok_rows, capacity, held, other_ref, part_ref, stay_ref, *refs):
    gates, ups = refs[: 2 * held : 2], refs[1 : 2 * held : 2]
    gate_hbm, up_hbm, gate_ref, up_ref, gate_rest, up_rest, x_ref, sems = refs[2 * held :]
    copies = weight_copies((gate_hbm, up_hbm), (gate_rest, up_rest), sems, sum(ref.shape[0] for ref in gates), step)
    for copy in copies:
        copy.start()
    rows, cut = part_ref.shape
    expert, core = lax.axis_index("ep"), lax.axis_index("ep") % 2
    far = picked(other_ref, 1 - core, expert, rows, tok_rows, capacity, 0, cut) + part_ref[...].astype(jnp.float32)
    gather_rows(x_ref, stay_ref[:, :cut], far.astype(x_ref.dtype))
    gate_ref[...] = partial_product(x_ref, gates, 0)
    up_ref[...] = partial_product(x_ref, ups, 0)
    for copy in copies:
        copy.wait()


def middle_step(step, start, held, far_ref, stay_ref, gate_in, up_in, *refs):
    gates, ups = refs[: 2 * held : 2], refs[1 : 2 * held : 2]
    gate_hbm, up_hbm, gate_ref, up_ref, gate_rest, up_rest, x_ref, sems = refs[2 * held :]
    copies = weight_copies((gate_hbm, up_hbm), (gate_rest, up_rest), sems, sum(ref.shape[0] for ref in gates), step)
    for copy in copies:
        copy.start()
    gather_rows(x_ref, stay_ref[:, start : start + far_ref.shape[1]], far_ref[...])
    gate_ref[...] = gate_in[...] + partial_product(x_ref, gates, start)
    up_ref[...] = up_in[...] + partial_product(x_ref, ups, start)
    for copy in copies:
        copy.wait()


def second_kernel(folds, experts, far_ref, stay_ref, gate_in, up_in, *refs):
    gates, ups, (out_ref, x_ref, hidden_ref) = refs[:-3:2], refs[1:-3:2], refs[-3:]
    cut = stay_ref.shape[1] - far_ref.shape[1]
    gather_rows(x_ref, stay_ref[:, cut:], far_ref[...])
    gate_val = gate_in[...] + partial_product(x_ref, gates, cut)
    up_val = up_in[...] + partial_product(x_ref, ups, cut)
    hidden_ref[...] = gate_val / (1.0 + jnp.exp(-gate_val)) * up_val
    store_blocks(folds, experts, hidden_ref, out_ref)


def store_blocks(folds, experts, hidden_ref, out_ref):
    peers = out_ref.shape[0]
    capacity = hidden_ref.shape[0] // peers
    span = hidden_ref.shape[1] // folds
    for peer in range(peers):
        layer, chip, core = peer // experts, peer % experts // 2, peer % 2
        start = (chip * (peers // 2) + layer * 2 + core) * capacity
        rows = hidden_ref[start : start + capacity, :]
        pieces = [rows[:, fold * span : (fold + 1) * span] for fold in range(folds)]
        out_ref[peer] = jnp.concatenate(pieces, axis=0).astype(out_ref.dtype)


def routed_by_columns(tokens, expert_ids, gate_local, up_local, peers, capacity, folds):
    tok_rows, width = tokens.shape
    units = gate_local.shape[1]
    experts = 4
    rows = peers * capacity
    half = rows // 2
    cuts = (width // 4, 2 * width // 3)
    cut = cuts[0]
    helds = (width // 3, width // 6, width // 4)
    step = 256
    kind = tokens.dtype

    def array(*shape):
        return jax.ShapeDtypeStruct(shape, kind)

    def swap(block, bit):
        return lax.ppermute(block, "ep", [(i, i ^ bit) for i in range(experts)])

    packed = local_kernel(
        pack_kernel,
        array(tok_rows, 128 + width),
        (),
        (expert_ids.T, tokens),
        scratch=[pltpu.VMEM((2, tok_rows), jnp.int32), pltpu.SemaphoreType.DMA((2,))],
    )
    own = lax.all_gather(packed, "et", axis=0, tiled=True)
    part = local_kernel(cut_kernel, array(own.shape[0], 128 + cut), (own,))
    near, far = swap(own, 1), swap(part, 2)
    kernel = functools.partial(select_kernel, tok_rows, capacity)
    laters = local_kernel(kernel, [array(half, cuts[1] - cut), array(half, width - cuts[1])], (own, near))
    middle_far, later_far = (swap(later, 2) for later in laters)

    def fetch(start, held, blocks, swapped, span):
        return local_kernel(
            functools.partial(fetch_kernel, start, step, tok_rows, capacity, swapped),
            [array(half, span)] + [pltpu.VMEM((held, units), kind)] * 2,
            blocks,
            (gate_local, up_local),
            scratch=[pltpu.SemaphoreType.DMA((2, held // step))],
        )

    own, near, *laters = lax.optimization_barrier((own, near, *laters))
    stay, *pieces = fetch(0, helds[0], (own, near), (0, 1), width)
    far, *pieces = lax.optimization_barrier((far, *pieces))
    far_other = swap(far, 1)
    far_part, *more = fetch(helds[0], helds[1], (far,), (0,), cut)
    far_other, *more = lax.optimization_barrier((far_other, *more))
    pieces = (*pieces, *more)

    def sums(kernel, rest, blocks, pieces, span):
        return local_kernel(
            functools.partial(kernel, len(pieces) // 2),
            [jax.ShapeDtypeStruct((rows, units), jnp.float32)] * 2 + [pltpu.VMEM((rest, units), kind)] * 2,
            (*blocks, *pieces),
            (gate_local, up_local),
            scratch=[pltpu.VMEM((rows, span), kind), pltpu.SemaphoreType.DMA((2, rest // step))],
        )

    kernel = functools.partial(first_kernel, step, tok_rows, capacity)
    gate_sum, up_sum, *last = sums(kernel, helds[2], (far_other, far_part, stay), pieces, cut)
    middle_far, *last = lax.optimization_barrier((middle_far, *last))
    pieces = (*pieces, *last)
    kernel = functools.partial(middle_step, step, cut)
    rest = width - sum(helds)
    gate_sum, up_sum, *last = sums(kernel, rest, (middle_far, stay, gate_sum, up_sum), pieces, cuts[1] - cut)
    later_far, *last = lax.optimization_barrier((later_far, *last))
    return local_kernel(
        functools.partial(second_kernel, folds, experts),
        array(peers, capacity * folds, units // folds),
        (later_far, stay, gate_sum, up_sum, *pieces, *last),
        scratch=[pltpu.VMEM((rows, width - cuts[1]), kind), pltpu.VMEM((rows, units), jnp.float32)],
    )


def picks_kernel(experts, capacity, folds, ids_ref, weights_ref, picks_ref, column_ref):
    tok_rows = ids_ref.shape[1]
    both = 2 * tok_rows
    ids = [as_column(ids_ref[slot : slot + 1, :]) for slot in range(2)]
    expert = iota((tok_rows, 128), 1)
    named = ((expert == ids[0]) | (expert == ids[1])).astype(jnp.bfloat16)
    lower = (iota((tok_rows, tok_rows), 0) > iota((tok_rows, tok_rows), 1)).astype(jnp.bfloat16)
    before = exact_dot(lower, named).astype(jnp.int32)
    slot_row, token = iota((both, tok_rows), 0), iota((both, tok_rows), 1)
    target = jnp.zeros((both, 1), jnp.int32)
    column = jnp.zeros((both, 1), jnp.float32)
    for slot, chosen in enumerate(ids):
        position = jnp.sum(jnp.where(expert == chosen, before, 0), axis=1, keepdims=True)
        mask = slot_row == 2 * token + slot
        place = as_row(chosen * (folds * capacity) + position)
        target = target + jnp.sum(jnp.where(mask, place, 0), axis=1, keepdims=True)
        column = column + jnp.sum(jnp.where(mask, weights_ref[slot : slot + 1, :], 0.0), axis=1, keepdims=True)
    column_ref[...] = jnp.broadcast_to(column, column_ref.shape)
    lane = iota((both, experts * folds * capacity), 1)
    for fold in range(folds):
        picks_ref[fold * both : (fold + 1) * both, :] = (lane == target + fold * capacity).astype(picks_ref.dtype)


def final_kernel(experts, folds, picks_ref, column_ref, recv_ref, out_ref):
    tok_rows = out_ref.shape[0]
    both = 2 * tok_rows
    peers, tall, span = recv_ref.shape
    column = column_ref[:, 0:1]
    for part in range(peers // experts):
        block = recv_ref[part * experts : (part + 1) * experts].reshape(experts * tall, span)
        rows = exact_dot(picks_ref[...], block)
        for fold in range(folds):
            scaled = rows[fold * both : (fold + 1) * both] * column
            start = (part * folds + fold) * span
            out_ref[:, :, start : start + span] = scaled.astype(out_ref.dtype).reshape(tok_rows, 2, span)


def finish(expert_ids, gate_weights, received, experts, folds):
    tok_rows = expert_ids.shape[0]
    peers, tall, span = received.shape
    capacity = tall // folds
    kind = received.dtype
    picks, column = local_kernel(
        functools.partial(picks_kernel, experts, capacity, folds),
        [
            jax.ShapeDtypeStruct((2 * tok_rows * folds, experts * tall), kind),
            jax.ShapeDtypeStruct((2 * tok_rows, 128), jnp.float32),
        ],
        (expert_ids.T, gate_weights.T),
        moved=1 << 20,
    )
    units = peers // experts * folds * span
    return local_kernel(
        functools.partial(final_kernel, experts, folds),
        jax.ShapeDtypeStruct((tok_rows, 2, units), kind),
        (picks, column, received),
        moved=4 * received.size,
    )


def body(tokens, expert_ids, gate_weights, w_gate, w_up):
    tok_rows, width = tokens.shape
    experts = lax.axis_size("ep")
    tensor_size = lax.axis_size("et")
    peers = experts * tensor_size
    capacity = tok_rows // 2
    gate_local = w_gate[0]
    up_local = w_up[0]
    if experts == 4 and tensor_size == 4:
        folds = 4
        blocks = routed_by_columns(tokens, expert_ids, gate_local, up_local, peers, capacity, folds)
        return finish(expert_ids, gate_weights, exchange(blocks), experts, folds)
    slot_pairs = place_slots(expert_ids, experts, capacity)
    selector = build_select(slot_pairs, experts * capacity)
    buffer = jnp.dot(selector, tokens, preferred_element_type=jnp.float32).astype(jnp.bfloat16)
    buffer = buffer.reshape(1, experts, capacity * width // 128, 128)
    buffer = jnp.broadcast_to(buffer, (tensor_size,) + buffer.shape[1:])
    arrived = exchange(buffer.reshape(peers, capacity * width // 128, 128))
    hidden = swiglu_rows(arrived.reshape(peers * capacity, width), gate_local, up_local)
    units = hidden.shape[1]
    returned = exchange(hidden.reshape(peers, capacity * units // 128, 128))
    returned = returned.reshape(tensor_size, experts * capacity, units)
    targets = jnp.arange(experts * capacity, dtype=jnp.int32)
    picker = (slot_pairs[:, :, None] == targets[None, None, :]).astype(jnp.bfloat16)
    gathered = jnp.einsum("tsj,ejf->tsef", picker, returned, preferred_element_type=jnp.float32)
    gathered = gathered.reshape(tok_rows, 2, tensor_size * units)
    return (gate_weights[:, :, None] * gathered).astype(jnp.bfloat16)


def solution(mesh):
    in_specs = (
        P(("groups", "et", "ep"), None),
        P(("groups", "et", "ep"), None),
        P(("groups", "et", "ep"), None),
        P("ep", None, "et"),
        P("ep", None, "et"),
    )
    out_specs = P(("groups", "et", "ep"), None, None)
    return jax.shard_map(body, mesh=mesh, in_specs=in_specs, out_specs=out_specs, check_vma=False)
```

```python
import functools

import jax
import jax.numpy as jnp
from jax import lax
from jax.experimental import pallas as pl
from jax.experimental.pallas import tpu as pltpu
from jax.sharding import PartitionSpec as P

WHOLE = pl.BlockSpec(memory_space=pltpu.VMEM)
OUTSIDE = pl.BlockSpec(memory_space=pltpu.HBM)


def place_slots(id_block, experts, capacity):
    flat_ids = id_block.reshape(-1)
    onehot = (flat_ids[:, None] == jnp.arange(experts, dtype=jnp.int32)[None, :]).astype(jnp.int32)
    before = jnp.cumsum(onehot, axis=0) - onehot
    position = jnp.sum(before * onehot, axis=1)
    return (flat_ids * capacity + position).reshape(id_block.shape)


def build_select(slot_pairs, total):
    targets = jnp.arange(total, dtype=jnp.int32).reshape(-1, 1, 1)
    return jnp.sum(slot_pairs[..., None, :, :] == targets, axis=-1).astype(jnp.bfloat16)


def swiglu_rows(rows, gate_local, up_local):
    gate_val = jnp.dot(rows, gate_local, preferred_element_type=jnp.float32)
    up_val = jnp.dot(rows, up_local, preferred_element_type=jnp.float32)
    return (jax.nn.silu(gate_val) * up_val).astype(jnp.bfloat16)


def exchange(blocks):
    return lax.all_to_all(blocks, ("et", "ep"), split_axis=0, concat_axis=0, tiled=True)


def local_kernel(kernel, out_shape, args, outside=(), flops=0, moved=0, scratch=(), limit=12):
    return pl.pallas_call(
        kernel,
        out_shape=out_shape,
        in_specs=[WHOLE] * len(args) + [OUTSIDE] * len(outside),
        out_specs=jax.tree.map(lambda _: WHOLE, out_shape),
        scratch_shapes=scratch,
        compiler_params=pltpu.CompilerParams(vmem_limit_bytes=limit << 20),
        cost_estimate=pl.CostEstimate(flops=flops, bytes_accessed=moved, transcendentals=0),
    )(*args, *(pltpu.with_memory_space_constraint(array, pltpu.HBM) for array in outside))


def exact_dot(a, b):
    return jnp.dot(a, b, preferred_element_type=jnp.float32)


def transposed_dot(a, b):
    return lax.dot_general(a, b, (((0,), (0,)), ((), ())), preferred_element_type=jnp.float32)


def iota(shape, dim):
    return lax.broadcasted_iota(jnp.int32, shape, dim)


def as_column(row):
    size = row.shape[1]
    eye = iota((size, size), 0) == iota((size, size), 1)
    return jnp.sum(jnp.where(eye, row, jnp.zeros_like(row)), axis=1, keepdims=True)


def as_row(column):
    size = column.shape[0]
    eye = iota((size, size), 0) == iota((size, size), 1)
    return jnp.sum(jnp.where(eye, column, jnp.zeros_like(column)), axis=0, keepdims=True)


def pack_kernel(ids_hbm, tokens_hbm, _, __, out_ref, ids_ref, sems):
    named = pltpu.make_async_copy(ids_hbm, ids_ref, sems.at[0])
    named.start()
    copy = pltpu.make_async_copy(tokens_hbm, out_ref.at[:, 128:], sems.at[1])
    copy.start()
    named.wait()
    names = ids_ref[...].astype(jnp.float32)
    lane = iota((out_ref.shape[0], 128), 1)
    out_ref[:, :128] = jnp.where(lane == 0, as_column(names[0:1]), as_column(names[1:2])).astype(out_ref.dtype)
    copy.wait()


def rows_of(ids_block, source, expert, rows, tok_rows, capacity):
    tall = ids_block.shape[0]
    names = ids_block.astype(jnp.float32)
    expert = expert.astype(jnp.float32)
    named = (names[:, 0:1] == expert) | (names[:, 1:2] == expert)
    later, earlier = iota((tall, tall), 0), iota((tall, tall), 1)
    lower = ((later > earlier) & (later // tok_rows == earlier // tok_rows)).astype(jnp.bfloat16)
    flags = jnp.broadcast_to(named.astype(jnp.float32), (tall, 128)).astype(jnp.bfloat16)
    before = exact_dot(lower, flags)[:, 0:1].astype(jnp.int32)
    layer = iota((tall, 1), 0) // tok_rows
    target = jnp.where(named, (layer * 2 + source) * capacity + before, -1)
    return (iota((tall, rows), 1) == target).astype(jnp.bfloat16)


def picked(ref, source, expert, rows, tok_rows, capacity, start, stop):
    sel = rows_of(ref[:, :128], source, expert, rows, tok_rows, capacity)
    return transposed_dot(sel, ref[:, 128 + start : 128 + stop])


def cut_kernel(in_ref, out_ref):
    out_ref[...] = in_ref[:, : out_ref.shape[1]]


def select_kernel(tok_rows, capacity, own_ref, near_ref, out_ref):
    expert, core = lax.axis_index("ep") ^ 2, lax.axis_index("ep") % 2
    rows, span = out_ref.shape
    stop = own_ref.shape[1] - 128
    parts = [
        picked(ref, source, expert, rows, tok_rows, capacity, stop - span, stop)
        for ref, source in ((own_ref, core), (near_ref, 1 - core))
    ]
    out_ref[...] = (parts[0] + parts[1]).astype(out_ref.dtype)


def pick_kernel(tok_rows, capacity, swapped, *refs):
    blocks, rows_ref = refs[:-1], refs[-1]
    rows, width = rows_ref.shape
    expert, core = lax.axis_index("ep"), lax.axis_index("ep") % 2
    rows_ref[...] = sum(
        picked(ref, core ^ other, expert, rows, tok_rows, capacity, 0, width) for ref, other in zip(blocks, swapped)
    ).astype(rows_ref.dtype)


def gather_rows(x_ref, stay, far):
    rows = stay.shape[0]
    chip = lax.axis_index("ep") // 2
    x_ref[pl.ds(pl.multiple_of(chip * rows, rows), rows), :] = stay
    x_ref[pl.ds(pl.multiple_of((1 - chip) * rows, rows), rows), :] = far


def first_kernel(tok_rows, capacity, other_ref, part_ref, stay_ref, gate_all, up_all, gate_ref, up_ref, x_ref):
    rows, cut = part_ref.shape
    expert, core = lax.axis_index("ep"), lax.axis_index("ep") % 2
    far = picked(other_ref, 1 - core, expert, rows, tok_rows, capacity, 0, cut) + part_ref[...].astype(jnp.float32)
    gather_rows(x_ref, stay_ref[:, :cut], far.astype(x_ref.dtype))
    gate_ref[...] = exact_dot(x_ref[...], gate_all[0, :cut, :])
    up_ref[...] = exact_dot(x_ref[...], up_all[0, :cut, :])


def second_kernel(folds, experts, far_ref, stay_ref, gate_in, up_in, gate_all, up_all, out_ref, x_ref, hidden_ref):
    cut = stay_ref.shape[1] - far_ref.shape[1]
    gather_rows(x_ref, stay_ref[:, cut:], far_ref[...])
    gate_val = gate_in[...] + exact_dot(x_ref[...], gate_all[0, cut:, :])
    up_val = up_in[...] + exact_dot(x_ref[...], up_all[0, cut:, :])
    hidden_ref[...] = gate_val / (1.0 + jnp.exp(-gate_val)) * up_val
    store_blocks(folds, experts, hidden_ref, out_ref)


def store_blocks(folds, experts, hidden_ref, out_ref):
    peers = out_ref.shape[0]
    capacity = hidden_ref.shape[0] // peers
    span = hidden_ref.shape[1] // folds
    for peer in range(peers):
        layer, chip, core = peer // experts, peer % experts // 2, peer % 2
        start = (chip * (peers // 2) + layer * 2 + core) * capacity
        rows = hidden_ref[start : start + capacity, :]
        pieces = [rows[:, fold * span : (fold + 1) * span] for fold in range(folds)]
        out_ref[peer] = jnp.concatenate(pieces, axis=0).astype(out_ref.dtype)


def routed_by_columns(tokens, expert_ids, w_gate, w_up, peers, capacity, folds):
    tok_rows, width = tokens.shape
    units = w_gate.shape[2]
    experts = 4
    rows = peers * capacity
    half = rows // 2
    cut = 11 * width // 24
    kind = tokens.dtype

    def array(*shape):
        return jax.ShapeDtypeStruct(shape, kind)

    def swap(block, bit):
        return lax.ppermute(block, "ep", [(i, i ^ bit) for i in range(experts)])

    packed = local_kernel(
        pack_kernel,
        array(tok_rows, 128 + width),
        (),
        (expert_ids.T, tokens, w_gate, w_up),
        scratch=[pltpu.VMEM((2, tok_rows), jnp.int32), pltpu.SemaphoreType.DMA((2,))],
    )
    own = lax.all_gather(packed, "et", axis=0, tiled=True)
    part = local_kernel(cut_kernel, array(own.shape[0], 128 + cut), (own,))
    near, far = swap(own, 1), swap(part, 2)
    later = local_kernel(functools.partial(select_kernel, tok_rows, capacity), array(half, width - cut), (own, near))
    later_far = swap(later, 2)

    def pick(blocks, swapped, span):
        kernel = functools.partial(pick_kernel, tok_rows, capacity, swapped)
        return local_kernel(kernel, array(half, span), blocks)

    own, near, later = lax.optimization_barrier((own, near, later))
    stay = pick((own, near), (0, 1), width)
    far, stay = lax.optimization_barrier((far, stay))
    far_other = swap(far, 1)
    far_part = pick((far,), (0,), cut)
    far_other, far_part = lax.optimization_barrier((far_other, far_part))
    gate_sum, up_sum = local_kernel(
        functools.partial(first_kernel, tok_rows, capacity),
        [jax.ShapeDtypeStruct((rows, units), jnp.float32)] * 2,
        (far_other, far_part, stay, w_gate, w_up),
        scratch=[pltpu.VMEM((rows, cut), kind)],
    )
    later_far, gate_sum = lax.optimization_barrier((later_far, gate_sum))
    return local_kernel(
        functools.partial(second_kernel, folds, experts),
        array(peers, capacity * folds, units // folds),
        (later_far, stay, gate_sum, up_sum, w_gate, w_up),
        scratch=[pltpu.VMEM((rows, width - cut), kind), pltpu.VMEM((rows, units), jnp.float32)],
    )


def picks_kernel(experts, capacity, folds, ids_ref, weights_ref, picks_ref, column_ref):
    tok_rows = ids_ref.shape[1]
    both = 2 * tok_rows
    ids = [as_column(ids_ref[slot : slot + 1, :]) for slot in range(2)]
    expert = iota((tok_rows, 128), 1)
    named = ((expert == ids[0]) | (expert == ids[1])).astype(jnp.bfloat16)
    lower = (iota((tok_rows, tok_rows), 0) > iota((tok_rows, tok_rows), 1)).astype(jnp.bfloat16)
    before = exact_dot(lower, named).astype(jnp.int32)
    slot_row, token = iota((both, tok_rows), 0), iota((both, tok_rows), 1)
    target = jnp.zeros((both, 1), jnp.int32)
    column = jnp.zeros((both, 1), jnp.float32)
    for slot, chosen in enumerate(ids):
        position = jnp.sum(jnp.where(expert == chosen, before, 0), axis=1, keepdims=True)
        mask = slot_row == 2 * token + slot
        place = as_row(chosen * (folds * capacity) + position)
        target = target + jnp.sum(jnp.where(mask, place, 0), axis=1, keepdims=True)
        column = column + jnp.sum(jnp.where(mask, weights_ref[slot : slot + 1, :], 0.0), axis=1, keepdims=True)
    column_ref[...] = jnp.broadcast_to(column, column_ref.shape)
    lane = iota((both, experts * folds * capacity), 1)
    for fold in range(folds):
        picks_ref[fold * both : (fold + 1) * both, :] = (lane == target + fold * capacity).astype(picks_ref.dtype)


def final_kernel(experts, folds, picks_ref, column_ref, recv_ref, out_ref):
    tok_rows = out_ref.shape[0]
    both = 2 * tok_rows
    peers, tall, span = recv_ref.shape
    column = column_ref[:, 0:1]
    for part in range(peers // experts):
        block = recv_ref[part * experts : (part + 1) * experts].reshape(experts * tall, span)
        rows = exact_dot(picks_ref[...], block)
        for fold in range(folds):
            scaled = rows[fold * both : (fold + 1) * both] * column
            start = (part * folds + fold) * span
            out_ref[:, :, start : start + span] = scaled.astype(out_ref.dtype).reshape(tok_rows, 2, span)


def finish(expert_ids, gate_weights, received, experts, folds):
    tok_rows = expert_ids.shape[0]
    peers, tall, span = received.shape
    capacity = tall // folds
    kind = received.dtype
    picks, column = local_kernel(
        functools.partial(picks_kernel, experts, capacity, folds),
        [
            jax.ShapeDtypeStruct((2 * tok_rows * folds, experts * tall), kind),
            jax.ShapeDtypeStruct((2 * tok_rows, 128), jnp.float32),
        ],
        (expert_ids.T, gate_weights.T),
        moved=1 << 20,
    )
    units = peers // experts * folds * span
    return local_kernel(
        functools.partial(final_kernel, experts, folds),
        jax.ShapeDtypeStruct((tok_rows, 2, units), kind),
        (picks, column, received),
        moved=4 * received.size,
    )


def body(tokens, expert_ids, gate_weights, w_gate, w_up):
    tok_rows, width = tokens.shape
    experts = lax.axis_size("ep")
    tensor_size = lax.axis_size("et")
    peers = experts * tensor_size
    capacity = tok_rows // 2
    gate_local = w_gate[0]
    up_local = w_up[0]
    if experts == 4 and tensor_size == 4:
        folds = 4
        blocks = routed_by_columns(tokens, expert_ids, w_gate, w_up, peers, capacity, folds)
        return finish(expert_ids, gate_weights, exchange(blocks), experts, folds)
    slot_pairs = place_slots(expert_ids, experts, capacity)
    selector = build_select(slot_pairs, experts * capacity)
    buffer = jnp.dot(selector, tokens, preferred_element_type=jnp.float32).astype(jnp.bfloat16)
    buffer = buffer.reshape(1, experts, capacity * width // 128, 128)
    buffer = jnp.broadcast_to(buffer, (tensor_size,) + buffer.shape[1:])
    arrived = exchange(buffer.reshape(peers, capacity * width // 128, 128))
    hidden = swiglu_rows(arrived.reshape(peers * capacity, width), gate_local, up_local)
    units = hidden.shape[1]
    returned = exchange(hidden.reshape(peers, capacity * units // 128, 128))
    returned = returned.reshape(tensor_size, experts * capacity, units)
    targets = jnp.arange(experts * capacity, dtype=jnp.int32)
    picker = (slot_pairs[:, :, None] == targets[None, None, :]).astype(jnp.bfloat16)
    gathered = jnp.einsum("tsj,ejf->tsef", picker, returned, preferred_element_type=jnp.float32)
    gathered = gathered.reshape(tok_rows, 2, tensor_size * units)
    return (gate_weights[:, :, None] * gathered).astype(jnp.bfloat16)


def solution(mesh):
    in_specs = (
        P(("groups", "et", "ep"), None),
        P(("groups", "et", "ep"), None),
        P(("groups", "et", "ep"), None),
        P("ep", None, "et"),
        P("ep", None, "et"),
    )
    out_specs = P(("groups", "et", "ep"), None, None)
    return jax.shard_map(body, mesh=mesh, in_specs=in_specs, out_specs=out_specs, check_vma=False)
```

```python
import functools

import jax
import jax.numpy as jnp
from jax import lax
from jax.experimental import pallas as pl
from jax.experimental.pallas import tpu as pltpu
from jax.sharding import PartitionSpec as P

WHOLE = pl.BlockSpec(memory_space=pltpu.VMEM)
OUTSIDE = pl.BlockSpec(memory_space=pltpu.HBM)


def place_slots(id_block, experts, capacity):
    flat_ids = id_block.reshape(-1)
    onehot = (flat_ids[:, None] == jnp.arange(experts, dtype=jnp.int32)[None, :]).astype(jnp.int32)
    before = jnp.cumsum(onehot, axis=0) - onehot
    position = jnp.sum(before * onehot, axis=1)
    return (flat_ids * capacity + position).reshape(id_block.shape)


def build_select(slot_pairs, total):
    targets = jnp.arange(total, dtype=jnp.int32).reshape(-1, 1, 1)
    return jnp.sum(slot_pairs[..., None, :, :] == targets, axis=-1).astype(jnp.bfloat16)


def swiglu_rows(rows, gate_local, up_local):
    gate_val = jnp.dot(rows, gate_local, preferred_element_type=jnp.float32)
    up_val = jnp.dot(rows, up_local, preferred_element_type=jnp.float32)
    return (jax.nn.silu(gate_val) * up_val).astype(jnp.bfloat16)


def exchange(blocks):
    return lax.all_to_all(blocks, ("et", "ep"), split_axis=0, concat_axis=0, tiled=True)


def local_kernel(kernel, out_shape, args, outside=(), flops=0, moved=0, scratch=(), limit=12):
    return pl.pallas_call(
        kernel,
        out_shape=out_shape,
        in_specs=[WHOLE] * len(args) + [OUTSIDE] * len(outside),
        out_specs=jax.tree.map(lambda _: WHOLE, out_shape),
        scratch_shapes=scratch,
        compiler_params=pltpu.CompilerParams(vmem_limit_bytes=limit << 20),
        cost_estimate=pl.CostEstimate(flops=flops, bytes_accessed=moved, transcendentals=0),
    )(*args, *(pltpu.with_memory_space_constraint(array, pltpu.HBM) for array in outside))


def exact_dot(a, b):
    return jnp.dot(a, b, preferred_element_type=jnp.float32)


def transposed_dot(a, b):
    return lax.dot_general(a, b, (((0,), (0,)), ((), ())), preferred_element_type=jnp.float32)


def iota(shape, dim):
    return lax.broadcasted_iota(jnp.int32, shape, dim)


def as_column(row):
    size = row.shape[1]
    eye = iota((size, size), 0) == iota((size, size), 1)
    return jnp.sum(jnp.where(eye, row, jnp.zeros_like(row)), axis=1, keepdims=True)


def as_row(column):
    size = column.shape[0]
    eye = iota((size, size), 0) == iota((size, size), 1)
    return jnp.sum(jnp.where(eye, column, jnp.zeros_like(column)), axis=0, keepdims=True)


def pack_kernel(ids_hbm, tokens_hbm, _, __, out_ref, ids_ref, sems):
    named = pltpu.make_async_copy(ids_hbm, ids_ref, sems.at[0])
    named.start()
    copy = pltpu.make_async_copy(tokens_hbm, out_ref.at[:, 128:], sems.at[1])
    copy.start()
    named.wait()
    names = ids_ref[...].astype(jnp.float32)
    lane = iota((out_ref.shape[0], 128), 1)
    out_ref[:, :128] = jnp.where(lane == 0, as_column(names[0:1]), as_column(names[1:2])).astype(out_ref.dtype)
    copy.wait()


def rows_of(ids_block, source, expert, rows, tok_rows, capacity):
    tall = ids_block.shape[0]
    names = ids_block.astype(jnp.float32)
    expert = expert.astype(jnp.float32)
    named = (names[:, 0:1] == expert) | (names[:, 1:2] == expert)
    later, earlier = iota((tall, tall), 0), iota((tall, tall), 1)
    lower = ((later > earlier) & (later // tok_rows == earlier // tok_rows)).astype(jnp.bfloat16)
    flags = jnp.broadcast_to(named.astype(jnp.float32), (tall, 128)).astype(jnp.bfloat16)
    before = exact_dot(lower, flags)[:, 0:1].astype(jnp.int32)
    layer = iota((tall, 1), 0) // tok_rows
    target = jnp.where(named, (layer * 2 + source) * capacity + before, -1)
    return (iota((tall, rows), 1) == target).astype(jnp.bfloat16)


def picked(ref, source, expert, rows, tok_rows, capacity, start, stop):
    sel = rows_of(ref[:, :128], source, expert, rows, tok_rows, capacity)
    return transposed_dot(sel, ref[:, 128 + start : 128 + stop])


def cut_kernel(in_ref, out_ref):
    out_ref[...] = in_ref[:, : out_ref.shape[1]]


def select_kernel(tok_rows, capacity, own_ref, near_ref, *outs):
    expert, core = lax.axis_index("ep") ^ 2, lax.axis_index("ep") % 2
    rows = outs[0].shape[0]
    found = [
        (rows_of(ref[:, :128], source, expert, rows, tok_rows, capacity), ref)
        for ref, source in ((own_ref, core), (near_ref, 1 - core))
    ]
    start = own_ref.shape[1] - sum(out.shape[1] for out in outs)
    for out in outs:
        stop = start + out.shape[1]
        out[...] = sum(transposed_dot(sel, ref[:, start:stop]) for sel, ref in found).astype(out.dtype)
        start = stop


def pick_kernel(tok_rows, capacity, swapped, *refs):
    blocks, rows_ref = refs[:-1], refs[-1]
    rows, width = rows_ref.shape
    expert, core = lax.axis_index("ep"), lax.axis_index("ep") % 2
    rows_ref[...] = sum(
        picked(ref, core ^ other, expert, rows, tok_rows, capacity, 0, width) for ref, other in zip(blocks, swapped)
    ).astype(rows_ref.dtype)


def gather_rows(x_ref, stay, far):
    rows = stay.shape[0]
    chip = lax.axis_index("ep") // 2
    x_ref[pl.ds(pl.multiple_of(chip * rows, rows), rows), :] = stay
    x_ref[pl.ds(pl.multiple_of((1 - chip) * rows, rows), rows), :] = far


def first_kernel(tok_rows, capacity, other_ref, part_ref, stay_ref, gate_all, up_all, gate_ref, up_ref, x_ref):
    rows, cut = part_ref.shape
    expert, core = lax.axis_index("ep"), lax.axis_index("ep") % 2
    far = picked(other_ref, 1 - core, expert, rows, tok_rows, capacity, 0, cut) + part_ref[...].astype(jnp.float32)
    gather_rows(x_ref, stay_ref[:, :cut], far.astype(x_ref.dtype))
    gate_ref[...] = exact_dot(x_ref[...], gate_all[0, :cut, :])
    up_ref[...] = exact_dot(x_ref[...], up_all[0, :cut, :])


def middle_kernel(start, far_ref, stay_ref, gate_in, up_in, gate_all, up_all, gate_ref, up_ref, x_ref):
    stop = start + far_ref.shape[1]
    gather_rows(x_ref, stay_ref[:, start:stop], far_ref[...])
    gate_ref[...] = gate_in[...] + exact_dot(x_ref[...], gate_all[0, start:stop, :])
    up_ref[...] = up_in[...] + exact_dot(x_ref[...], up_all[0, start:stop, :])


def second_kernel(folds, experts, far_ref, stay_ref, gate_in, up_in, gate_all, up_all, out_ref, x_ref, hidden_ref):
    cut = stay_ref.shape[1] - far_ref.shape[1]
    gather_rows(x_ref, stay_ref[:, cut:], far_ref[...])
    gate_val = gate_in[...] + exact_dot(x_ref[...], gate_all[0, cut:, :])
    up_val = up_in[...] + exact_dot(x_ref[...], up_all[0, cut:, :])
    hidden_ref[...] = gate_val / (1.0 + jnp.exp(-gate_val)) * up_val
    store_blocks(folds, experts, hidden_ref, out_ref)


def store_blocks(folds, experts, hidden_ref, out_ref):
    peers = out_ref.shape[0]
    capacity = hidden_ref.shape[0] // peers
    span = hidden_ref.shape[1] // folds
    for peer in range(peers):
        layer, chip, core = peer // experts, peer % experts // 2, peer % 2
        start = (chip * (peers // 2) + layer * 2 + core) * capacity
        rows = hidden_ref[start : start + capacity, :]
        pieces = [rows[:, fold * span : (fold + 1) * span] for fold in range(folds)]
        out_ref[peer] = jnp.concatenate(pieces, axis=0).astype(out_ref.dtype)


def routed_by_columns(tokens, expert_ids, w_gate, w_up, peers, capacity, folds):
    tok_rows, width = tokens.shape
    units = w_gate.shape[2]
    experts = 4
    rows = peers * capacity
    half = rows // 2
    cuts = (width // 6, 11 * width // 24, 3 * width // 4)
    cut = cuts[0]
    kind = tokens.dtype

    def array(*shape):
        return jax.ShapeDtypeStruct(shape, kind)

    def swap(block, bit):
        return lax.ppermute(block, "ep", [(i, i ^ bit) for i in range(experts)])

    packed = local_kernel(
        pack_kernel,
        array(tok_rows, 128 + width),
        (),
        (expert_ids.T, tokens, w_gate, w_up),
        scratch=[pltpu.VMEM((2, tok_rows), jnp.int32), pltpu.SemaphoreType.DMA((2,))],
    )
    own = lax.all_gather(packed, "et", axis=0, tiled=True)
    part = local_kernel(cut_kernel, array(own.shape[0], 128 + cut), (own,))
    near, far = swap(own, 1), swap(part, 2)
    kernel = functools.partial(select_kernel, tok_rows, capacity)
    ends = (*cuts[1:], width)
    laters = local_kernel(kernel, [array(half, stop - start) for start, stop in zip(cuts, ends)], (own, near))
    later_fars = [swap(later, 2) for later in laters]

    def pick(blocks, swapped, span):
        kernel = functools.partial(pick_kernel, tok_rows, capacity, swapped)
        return local_kernel(kernel, array(half, span), blocks)

    own, near, *laters = lax.optimization_barrier((own, near, *laters))
    stay = pick((own, near), (0, 1), width)
    far, stay = lax.optimization_barrier((far, stay))
    far_other = swap(far, 1)
    far_part = pick((far,), (0,), cut)
    far_other, far_part = lax.optimization_barrier((far_other, far_part))

    def sums(kernel, blocks, span):
        out_shape = [jax.ShapeDtypeStruct((rows, units), jnp.float32)] * 2
        return local_kernel(kernel, out_shape, (*blocks, w_gate, w_up), scratch=[pltpu.VMEM((rows, span), kind)])

    gate_sum, up_sum = sums(
        functools.partial(first_kernel, tok_rows, capacity), (far_other, far_part, stay), cut
    )
    for start, later_far in zip(cuts[:-1], later_fars):
        later_far, gate_sum = lax.optimization_barrier((later_far, gate_sum))
        kernel = functools.partial(middle_kernel, start)
        gate_sum, up_sum = sums(kernel, (later_far, stay, gate_sum, up_sum), later_far.shape[1])
    later_far, gate_sum = lax.optimization_barrier((later_fars[-1], gate_sum))
    return local_kernel(
        functools.partial(second_kernel, folds, experts),
        array(peers, capacity * folds, units // folds),
        (later_far, stay, gate_sum, up_sum, w_gate, w_up),
        scratch=[pltpu.VMEM((rows, width - cuts[-1]), kind), pltpu.VMEM((rows, units), jnp.float32)],
    )


def picks_kernel(experts, capacity, folds, ids_ref, weights_ref, picks_ref, column_ref):
    tok_rows = ids_ref.shape[1]
    both = 2 * tok_rows
    ids = [as_column(ids_ref[slot : slot + 1, :]) for slot in range(2)]
    expert = iota((tok_rows, 128), 1)
    named = ((expert == ids[0]) | (expert == ids[1])).astype(jnp.bfloat16)
    lower = (iota((tok_rows, tok_rows), 0) > iota((tok_rows, tok_rows), 1)).astype(jnp.bfloat16)
    before = exact_dot(lower, named).astype(jnp.int32)
    slot_row, token = iota((both, tok_rows), 0), iota((both, tok_rows), 1)
    target = jnp.zeros((both, 1), jnp.int32)
    column = jnp.zeros((both, 1), jnp.float32)
    for slot, chosen in enumerate(ids):
        position = jnp.sum(jnp.where(expert == chosen, before, 0), axis=1, keepdims=True)
        mask = slot_row == 2 * token + slot
        place = as_row(chosen * (folds * capacity) + position)
        target = target + jnp.sum(jnp.where(mask, place, 0), axis=1, keepdims=True)
        column = column + jnp.sum(jnp.where(mask, weights_ref[slot : slot + 1, :], 0.0), axis=1, keepdims=True)
    column_ref[...] = jnp.broadcast_to(column, column_ref.shape)
    lane = iota((both, experts * folds * capacity), 1)
    for fold in range(folds):
        picks_ref[fold * both : (fold + 1) * both, :] = (lane == target + fold * capacity).astype(picks_ref.dtype)


def final_kernel(experts, folds, picks_ref, column_ref, recv_ref, out_ref):
    tok_rows = out_ref.shape[0]
    both = 2 * tok_rows
    peers, tall, span = recv_ref.shape
    column = column_ref[:, 0:1]
    for part in range(peers // experts):
        block = recv_ref[part * experts : (part + 1) * experts].reshape(experts * tall, span)
        rows = exact_dot(picks_ref[...], block)
        for fold in range(folds):
            scaled = rows[fold * both : (fold + 1) * both] * column
            start = (part * folds + fold) * span
            out_ref[:, :, start : start + span] = scaled.astype(out_ref.dtype).reshape(tok_rows, 2, span)


def finish(expert_ids, gate_weights, received, experts, folds):
    tok_rows = expert_ids.shape[0]
    peers, tall, span = received.shape
    capacity = tall // folds
    kind = received.dtype
    picks, column = local_kernel(
        functools.partial(picks_kernel, experts, capacity, folds),
        [
            jax.ShapeDtypeStruct((2 * tok_rows * folds, experts * tall), kind),
            jax.ShapeDtypeStruct((2 * tok_rows, 128), jnp.float32),
        ],
        (expert_ids.T, gate_weights.T),
        moved=1 << 20,
    )
    units = peers // experts * folds * span
    return local_kernel(
        functools.partial(final_kernel, experts, folds),
        jax.ShapeDtypeStruct((tok_rows, 2, units), kind),
        (picks, column, received),
        moved=4 * received.size,
    )


def body(tokens, expert_ids, gate_weights, w_gate, w_up):
    tok_rows, width = tokens.shape
    experts = lax.axis_size("ep")
    tensor_size = lax.axis_size("et")
    peers = experts * tensor_size
    capacity = tok_rows // 2
    gate_local = w_gate[0]
    up_local = w_up[0]
    if experts == 4 and tensor_size == 4:
        folds = 4
        blocks = routed_by_columns(tokens, expert_ids, w_gate, w_up, peers, capacity, folds)
        return finish(expert_ids, gate_weights, exchange(blocks), experts, folds)
    slot_pairs = place_slots(expert_ids, experts, capacity)
    selector = build_select(slot_pairs, experts * capacity)
    buffer = jnp.dot(selector, tokens, preferred_element_type=jnp.float32).astype(jnp.bfloat16)
    buffer = buffer.reshape(1, experts, capacity * width // 128, 128)
    buffer = jnp.broadcast_to(buffer, (tensor_size,) + buffer.shape[1:])
    arrived = exchange(buffer.reshape(peers, capacity * width // 128, 128))
    hidden = swiglu_rows(arrived.reshape(peers * capacity, width), gate_local, up_local)
    units = hidden.shape[1]
    returned = exchange(hidden.reshape(peers, capacity * units // 128, 128))
    returned = returned.reshape(tensor_size, experts * capacity, units)
    targets = jnp.arange(experts * capacity, dtype=jnp.int32)
    picker = (slot_pairs[:, :, None] == targets[None, None, :]).astype(jnp.bfloat16)
    gathered = jnp.einsum("tsj,ejf->tsef", picker, returned, preferred_element_type=jnp.float32)
    gathered = gathered.reshape(tok_rows, 2, tensor_size * units)
    return (gate_weights[:, :, None] * gathered).astype(jnp.bfloat16)


def solution(mesh):
    in_specs = (
        P(("groups", "et", "ep"), None),
        P(("groups", "et", "ep"), None),
        P(("groups", "et", "ep"), None),
        P("ep", None, "et"),
        P("ep", None, "et"),
    )
    out_specs = P(("groups", "et", "ep"), None, None)
    return jax.shard_map(body, mesh=mesh, in_specs=in_specs, out_specs=out_specs, check_vma=False)
```

```python
import functools

import jax
import jax.numpy as jnp
from jax import lax
from jax.experimental import pallas as pl
from jax.experimental.pallas import tpu as pltpu
from jax.sharding import PartitionSpec as P

WHOLE = pl.BlockSpec(memory_space=pltpu.VMEM)
OUTSIDE = pl.BlockSpec(memory_space=pltpu.HBM)


def place_slots(id_block, experts, capacity):
    flat_ids = id_block.reshape(-1)
    onehot = (flat_ids[:, None] == jnp.arange(experts, dtype=jnp.int32)[None, :]).astype(jnp.int32)
    before = jnp.cumsum(onehot, axis=0) - onehot
    position = jnp.sum(before * onehot, axis=1)
    return (flat_ids * capacity + position).reshape(id_block.shape)


def build_select(slot_pairs, total):
    targets = jnp.arange(total, dtype=jnp.int32).reshape(-1, 1, 1)
    return jnp.sum(slot_pairs[..., None, :, :] == targets, axis=-1).astype(jnp.bfloat16)


def swiglu_rows(rows, gate_local, up_local):
    gate_val = jnp.dot(rows, gate_local, preferred_element_type=jnp.float32)
    up_val = jnp.dot(rows, up_local, preferred_element_type=jnp.float32)
    return (jax.nn.silu(gate_val) * up_val).astype(jnp.bfloat16)


def exchange(blocks):
    return lax.all_to_all(blocks, ("et", "ep"), split_axis=0, concat_axis=0, tiled=True)


def local_kernel(kernel, out_shape, args, outside=(), flops=0, moved=0, scratch=(), limit=12):
    return pl.pallas_call(
        kernel,
        out_shape=out_shape,
        in_specs=[WHOLE] * len(args) + [OUTSIDE] * len(outside),
        out_specs=jax.tree.map(lambda _: WHOLE, out_shape),
        scratch_shapes=scratch,
        compiler_params=pltpu.CompilerParams(vmem_limit_bytes=limit << 20),
        cost_estimate=pl.CostEstimate(flops=flops, bytes_accessed=moved, transcendentals=0),
    )(*args, *(pltpu.with_memory_space_constraint(array, pltpu.HBM) for array in outside))


def exact_dot(a, b):
    return jnp.dot(a, b, preferred_element_type=jnp.float32)


def transposed_dot(a, b):
    return lax.dot_general(a, b, (((0,), (0,)), ((), ())), preferred_element_type=jnp.float32)


def iota(shape, dim):
    return lax.broadcasted_iota(jnp.int32, shape, dim)


def as_column(row):
    size = row.shape[1]
    eye = iota((size, size), 0) == iota((size, size), 1)
    return jnp.sum(jnp.where(eye, row, jnp.zeros_like(row)), axis=1, keepdims=True)


def as_row(column):
    size = column.shape[0]
    eye = iota((size, size), 0) == iota((size, size), 1)
    return jnp.sum(jnp.where(eye, column, jnp.zeros_like(column)), axis=0, keepdims=True)


def pack_kernel(ids_hbm, tokens_hbm, _, __, out_ref, ids_ref, sems):
    named = pltpu.make_async_copy(ids_hbm, ids_ref, sems.at[0])
    named.start()
    copy = pltpu.make_async_copy(tokens_hbm, out_ref.at[:, 128:], sems.at[1])
    copy.start()
    named.wait()
    names = ids_ref[...].astype(jnp.float32)
    lane = iota((out_ref.shape[0], 128), 1)
    out_ref[:, :128] = jnp.where(lane == 0, as_column(names[0:1]), as_column(names[1:2])).astype(out_ref.dtype)
    copy.wait()


def rows_of(ids_block, group, source, expert, rows, tok_rows, capacity):
    tall = ids_block.shape[0]
    names = ids_block.astype(jnp.float32)
    expert = expert.astype(jnp.float32)
    named = (names[:, 0:1] == expert) | (names[:, 1:2] == expert)
    later, earlier = iota((tall, tall), 0), iota((tall, tall), 1)
    lower = ((later > earlier) & (later // tok_rows == earlier // tok_rows)).astype(jnp.bfloat16)
    flags = jnp.broadcast_to(named.astype(jnp.float32), (tall, 128)).astype(jnp.bfloat16)
    before = exact_dot(lower, flags)[:, 0:1].astype(jnp.int32)
    target = jnp.where(named & (group >= 0), (group * 2 + source) * capacity + before, -1)
    return (iota((tall, rows), 1) == target).astype(jnp.bfloat16)


def picked(ref, group, source, expert, rows, tok_rows, capacity, start, stop):
    sel = rows_of(ref[:, :128], group, source, expert, rows, tok_rows, capacity)
    return transposed_dot(sel, ref[:, 128 + start : 128 + stop])


def layer_of(ref, tok_rows):
    return iota((ref.shape[0], 1), 0) // tok_rows


def cut_kernel(tok_rows, in_ref, out_ref):
    shape = (out_ref.shape[0], in_ref.shape[0])
    row, place = iota(shape, 0), iota(shape, 1)
    layer = (row // tok_rows + 1) ^ lax.axis_index("et")
    move = (place == layer * tok_rows + row % tok_rows).astype(in_ref.dtype)
    out_ref[...] = exact_dot(move, in_ref[:, : out_ref.shape[1]]).astype(out_ref.dtype)


def select_kernel(tok_rows, capacity, own_ref, near_ref, *outs):
    expert, core = lax.axis_index("ep") ^ 2, lax.axis_index("ep") % 2
    rows = outs[0].shape[0]
    group = (layer_of(own_ref, tok_rows) ^ lax.axis_index("et")) - 1
    found = [
        (rows_of(ref[:, :128], group, source, expert, rows, tok_rows, capacity), ref)
        for ref, source in ((own_ref, core), (near_ref, 1 - core))
    ]
    start = own_ref.shape[1] - sum(out.shape[1] for out in outs)
    for out in outs:
        stop = start + out.shape[1]
        out[...] = sum(transposed_dot(sel, ref[:, start:stop]) for sel, ref in found).astype(out.dtype)
        start = stop


def stay_kernel(tok_rows, capacity, own_ref, near_ref, early_ref, early_other, stay_ref, first_ref):
    expert, core = lax.axis_index("ep"), lax.axis_index("ep") % 2
    group = layer_of(own_ref, tok_rows) ^ lax.axis_index("et")
    for out, refs, place in (
        (stay_ref, (own_ref, near_ref), group),
        (first_ref, (early_ref, early_other), layer_of(early_ref, tok_rows)),
    ):
        rows, width = out.shape
        out[...] = sum(
            picked(ref, place, core ^ other, expert, rows, tok_rows, capacity, 0, width)
            for other, ref in enumerate(refs)
        ).astype(out.dtype)


def pick_kernel(tok_rows, capacity, ref, rows_ref):
    rows, width = rows_ref.shape
    expert, core = lax.axis_index("ep"), lax.axis_index("ep") % 2
    group = layer_of(ref, tok_rows)
    rows_ref[...] = picked(ref, group, core, expert, rows, tok_rows, capacity, 0, width).astype(rows_ref.dtype)


def gather_rows(x_ref, stay, first, far):
    rows = stay.shape[0]
    chip = lax.axis_index("ep") // 2
    x_ref[pl.ds(pl.multiple_of(chip * rows, rows), rows), :] = stay
    far = jnp.concatenate([first.astype(jnp.float32), far.astype(jnp.float32)], axis=0)
    x_ref[pl.ds(pl.multiple_of((1 - chip) * rows, rows), rows), :] = far.astype(x_ref.dtype)


def first_kernel(tok_rows, capacity, other_ref, part_ref, stay_ref, early_ref, gate_all, up_all, *refs):
    gate_ref, up_ref, x_ref = refs
    rows, cut = part_ref.shape
    expert, core = lax.axis_index("ep"), lax.axis_index("ep") % 2
    group = layer_of(other_ref, tok_rows)
    far = picked(other_ref, group, 1 - core, expert, rows, tok_rows, capacity, 0, cut)
    far = far + part_ref[...].astype(jnp.float32)
    gather_rows(x_ref, stay_ref[:, :cut], early_ref[:, :cut], far)
    gate_ref[...] = exact_dot(x_ref[...], gate_all[0, :cut, :])
    up_ref[...] = exact_dot(x_ref[...], up_all[0, :cut, :])


def middle_kernel(start, far_ref, stay_ref, early_ref, gate_in, up_in, gate_all, up_all, gate_ref, up_ref, x_ref):
    stop = start + far_ref.shape[1]
    gather_rows(x_ref, stay_ref[:, start:stop], early_ref[:, start:stop], far_ref[...])
    gate_ref[...] = gate_in[...] + exact_dot(x_ref[...], gate_all[0, start:stop, :])
    up_ref[...] = up_in[...] + exact_dot(x_ref[...], up_all[0, start:stop, :])


def second_kernel(folds, experts, far_ref, stay_ref, early_ref, gate_in, up_in, gate_all, up_all, *refs):
    out_ref, x_ref, hidden_ref = refs
    cut = stay_ref.shape[1] - far_ref.shape[1]
    gather_rows(x_ref, stay_ref[:, cut:], early_ref[:, cut:], far_ref[...])
    gate_val = gate_in[...] + exact_dot(x_ref[...], gate_all[0, cut:, :])
    up_val = up_in[...] + exact_dot(x_ref[...], up_all[0, cut:, :])
    hidden_ref[...] = gate_val / (1.0 + jnp.exp(-gate_val)) * up_val
    store_blocks(folds, experts, hidden_ref, out_ref)


def store_blocks(folds, experts, hidden_ref, out_ref):
    peers = out_ref.shape[0]
    capacity = hidden_ref.shape[0] // peers
    span = hidden_ref.shape[1] // folds
    mine = lax.axis_index("et")
    for peer in range(0, peers, 2):
        layer, chip = peer // experts, peer % experts // 2
        start = chip * (peers // 2) * capacity + (layer ^ mine) * (2 * capacity)
        both = hidden_ref[pl.ds(pl.multiple_of(start, 8), 2 * capacity), :]
        for core in range(2):
            rows = both[core * capacity : (core + 1) * capacity]
            pieces = [rows[:, fold * span : (fold + 1) * span] for fold in range(folds)]
            out_ref[peer + core] = jnp.concatenate(pieces, axis=0).astype(out_ref.dtype)


def routed_by_columns(tokens, expert_ids, w_gate, w_up, peers, capacity, folds):
    tok_rows, width = tokens.shape
    units = w_gate.shape[2]
    experts = 4
    rows = peers * capacity
    half = rows // 2
    cuts = (width // 6, 11 * width // 24, 3 * width // 4)
    cut = cuts[0]
    kind = tokens.dtype

    def array(*shape):
        return jax.ShapeDtypeStruct(shape, kind)

    def swap(block, bit):
        return lax.ppermute(block, "ep", [(i, i ^ bit) for i in range(experts)])

    packed = local_kernel(
        pack_kernel,
        array(tok_rows, 128 + width),
        (),
        (expert_ids.T, tokens, w_gate, w_up),
        scratch=[pltpu.VMEM((2, tok_rows), jnp.int32), pltpu.SemaphoreType.DMA((2,))],
    )
    early = swap(packed, 2)
    own = lax.all_gather(packed, "et", axis=0, tiled=True)
    own, early = lax.optimization_barrier((own, early))
    others = own.shape[0] - tok_rows
    rest = half - 2 * capacity
    part = local_kernel(functools.partial(cut_kernel, tok_rows), array(others, 128 + cut), (own,))
    near, far, early_other = swap(own, 1), swap(part, 2), swap(early, 1)
    kernel = functools.partial(select_kernel, tok_rows, capacity)
    ends = (*cuts[1:], width)
    laters = local_kernel(kernel, [array(rest, stop - start) for start, stop in zip(cuts, ends)], (own, near))
    later_fars = [swap(later, 2) for later in laters]
    own, near, *laters = lax.optimization_barrier((own, near, *laters))
    kernel = functools.partial(stay_kernel, tok_rows, capacity)
    outs = [array(half, width), array(2 * capacity, width)]
    stay, first = local_kernel(kernel, outs, (own, near, early, early_other))
    far, stay = lax.optimization_barrier((far, stay))
    far_other = swap(far, 1)
    far_part = local_kernel(functools.partial(pick_kernel, tok_rows, capacity), array(rest, cut), (far,))
    far_other, far_part = lax.optimization_barrier((far_other, far_part))

    def sums(kernel, blocks, span):
        out_shape = [jax.ShapeDtypeStruct((rows, units), jnp.float32)] * 2
        return local_kernel(kernel, out_shape, (*blocks, w_gate, w_up), scratch=[pltpu.VMEM((rows, span), kind)])

    gate_sum, up_sum = sums(
        functools.partial(first_kernel, tok_rows, capacity), (far_other, far_part, stay, first), cut
    )
    for start, later_far in zip(cuts[:-1], later_fars):
        later_far, gate_sum = lax.optimization_barrier((later_far, gate_sum))
        kernel = functools.partial(middle_kernel, start)
        gate_sum, up_sum = sums(kernel, (later_far, stay, first, gate_sum, up_sum), later_far.shape[1])
    later_far, gate_sum = lax.optimization_barrier((later_fars[-1], gate_sum))
    return local_kernel(
        functools.partial(second_kernel, folds, experts),
        array(peers, capacity * folds, units // folds),
        (later_far, stay, first, gate_sum, up_sum, w_gate, w_up),
        scratch=[pltpu.VMEM((rows, width - cuts[-1]), kind), pltpu.VMEM((rows, units), jnp.float32)],
    )


def picks_kernel(experts, capacity, folds, ids_ref, weights_ref, picks_ref, column_ref):
    tok_rows = ids_ref.shape[1]
    both = 2 * tok_rows
    ids = [as_column(ids_ref[slot : slot + 1, :]) for slot in range(2)]
    expert = iota((tok_rows, 128), 1)
    named = ((expert == ids[0]) | (expert == ids[1])).astype(jnp.bfloat16)
    lower = (iota((tok_rows, tok_rows), 0) > iota((tok_rows, tok_rows), 1)).astype(jnp.bfloat16)
    before = exact_dot(lower, named).astype(jnp.int32)
    slot_row, token = iota((both, tok_rows), 0), iota((both, tok_rows), 1)
    target = jnp.zeros((both, 1), jnp.int32)
    column = jnp.zeros((both, 1), jnp.float32)
    for slot, chosen in enumerate(ids):
        position = jnp.sum(jnp.where(expert == chosen, before, 0), axis=1, keepdims=True)
        mask = slot_row == 2 * token + slot
        place = as_row(chosen * (folds * capacity) + position)
        target = target + jnp.sum(jnp.where(mask, place, 0), axis=1, keepdims=True)
        column = column + jnp.sum(jnp.where(mask, weights_ref[slot : slot + 1, :], 0.0), axis=1, keepdims=True)
    column_ref[...] = jnp.broadcast_to(column, column_ref.shape)
    lane = iota((both, experts * folds * capacity), 1)
    for fold in range(folds):
        picks_ref[fold * both : (fold + 1) * both, :] = (lane == target + fold * capacity).astype(picks_ref.dtype)


def final_kernel(experts, folds, picks_ref, column_ref, recv_ref, out_ref):
    tok_rows = out_ref.shape[0]
    both = 2 * tok_rows
    peers, tall, span = recv_ref.shape
    column = column_ref[:, 0:1]
    for part in range(peers // experts):
        block = recv_ref[part * experts : (part + 1) * experts].reshape(experts * tall, span)
        rows = exact_dot(picks_ref[...], block)
        for fold in range(folds):
            scaled = rows[fold * both : (fold + 1) * both] * column
            start = (part * folds + fold) * span
            out_ref[:, :, start : start + span] = scaled.astype(out_ref.dtype).reshape(tok_rows, 2, span)


def finish(expert_ids, gate_weights, received, experts, folds):
    tok_rows = expert_ids.shape[0]
    peers, tall, span = received.shape
    capacity = tall // folds
    kind = received.dtype
    picks, column = local_kernel(
        functools.partial(picks_kernel, experts, capacity, folds),
        [
            jax.ShapeDtypeStruct((2 * tok_rows * folds, experts * tall), kind),
            jax.ShapeDtypeStruct((2 * tok_rows, 128), jnp.float32),
        ],
        (expert_ids.T, gate_weights.T),
        moved=1 << 20,
    )
    units = peers // experts * folds * span
    return local_kernel(
        functools.partial(final_kernel, experts, folds),
        jax.ShapeDtypeStruct((tok_rows, 2, units), kind),
        (picks, column, received),
        moved=4 * received.size,
    )


def body(tokens, expert_ids, gate_weights, w_gate, w_up):
    tok_rows, width = tokens.shape
    experts = lax.axis_size("ep")
    tensor_size = lax.axis_size("et")
    peers = experts * tensor_size
    capacity = tok_rows // 2
    gate_local = w_gate[0]
    up_local = w_up[0]
    if experts == 4 and tensor_size == 4:
        folds = 4
        blocks = routed_by_columns(tokens, expert_ids, w_gate, w_up, peers, capacity, folds)
        return finish(expert_ids, gate_weights, exchange(blocks), experts, folds)
    slot_pairs = place_slots(expert_ids, experts, capacity)
    selector = build_select(slot_pairs, experts * capacity)
    buffer = jnp.dot(selector, tokens, preferred_element_type=jnp.float32).astype(jnp.bfloat16)
    buffer = buffer.reshape(1, experts, capacity * width // 128, 128)
    buffer = jnp.broadcast_to(buffer, (tensor_size,) + buffer.shape[1:])
    arrived = exchange(buffer.reshape(peers, capacity * width // 128, 128))
    hidden = swiglu_rows(arrived.reshape(peers * capacity, width), gate_local, up_local)
    units = hidden.shape[1]
    returned = exchange(hidden.reshape(peers, capacity * units // 128, 128))
    returned = returned.reshape(tensor_size, experts * capacity, units)
    targets = jnp.arange(experts * capacity, dtype=jnp.int32)
    picker = (slot_pairs[:, :, None] == targets[None, None, :]).astype(jnp.bfloat16)
    gathered = jnp.einsum("tsj,ejf->tsef", picker, returned, preferred_element_type=jnp.float32)
    gathered = gathered.reshape(tok_rows, 2, tensor_size * units)
    return (gate_weights[:, :, None] * gathered).astype(jnp.bfloat16)


def solution(mesh):
    in_specs = (
        P(("groups", "et", "ep"), None),
        P(("groups", "et", "ep"), None),
        P(("groups", "et", "ep"), None),
        P("ep", None, "et"),
        P("ep", None, "et"),
    )
    out_specs = P(("groups", "et", "ep"), None, None)
    return jax.shard_map(body, mesh=mesh, in_specs=in_specs, out_specs=out_specs, check_vma=False)
```

```python
import functools

import jax
import jax.numpy as jnp
from jax import lax
from jax.experimental import pallas as pl
from jax.experimental.pallas import tpu as pltpu
from jax.sharding import PartitionSpec as P

WHOLE = pl.BlockSpec(memory_space=pltpu.VMEM)
OUTSIDE = pl.BlockSpec(memory_space=pltpu.HBM)


def place_slots(id_block, experts, capacity):
    flat_ids = id_block.reshape(-1)
    onehot = (flat_ids[:, None] == jnp.arange(experts, dtype=jnp.int32)[None, :]).astype(jnp.int32)
    before = jnp.cumsum(onehot, axis=0) - onehot
    position = jnp.sum(before * onehot, axis=1)
    return (flat_ids * capacity + position).reshape(id_block.shape)


def build_select(slot_pairs, total):
    targets = jnp.arange(total, dtype=jnp.int32).reshape(-1, 1, 1)
    return jnp.sum(slot_pairs[..., None, :, :] == targets, axis=-1).astype(jnp.bfloat16)


def swiglu_rows(rows, gate_local, up_local):
    gate_val = jnp.dot(rows, gate_local, preferred_element_type=jnp.float32)
    up_val = jnp.dot(rows, up_local, preferred_element_type=jnp.float32)
    return (jax.nn.silu(gate_val) * up_val).astype(jnp.bfloat16)


def exchange(blocks):
    return lax.all_to_all(blocks, ("et", "ep"), split_axis=0, concat_axis=0, tiled=True)


def local_kernel(kernel, out_shape, args, outside=(), flops=0, moved=0, scratch=(), limit=12):
    return pl.pallas_call(
        kernel,
        out_shape=out_shape,
        in_specs=[WHOLE] * len(args) + [OUTSIDE] * len(outside),
        out_specs=jax.tree.map(lambda _: WHOLE, out_shape),
        scratch_shapes=scratch,
        compiler_params=pltpu.CompilerParams(vmem_limit_bytes=limit << 20),
        cost_estimate=pl.CostEstimate(flops=flops, bytes_accessed=moved, transcendentals=0),
    )(*args, *(pltpu.with_memory_space_constraint(array, pltpu.HBM) for array in outside))


def exact_dot(a, b):
    return jnp.dot(a, b, preferred_element_type=jnp.float32)


def transposed_dot(a, b):
    return lax.dot_general(a, b, (((0,), (0,)), ((), ())), preferred_element_type=jnp.float32)


def iota(shape, dim):
    return lax.broadcasted_iota(jnp.int32, shape, dim)


def as_column(row):
    size = row.shape[1]
    eye = iota((size, size), 0) == iota((size, size), 1)
    return jnp.sum(jnp.where(eye, row, jnp.zeros_like(row)), axis=1, keepdims=True)


def as_row(column):
    size = column.shape[0]
    eye = iota((size, size), 0) == iota((size, size), 1)
    return jnp.sum(jnp.where(eye, column, jnp.zeros_like(column)), axis=0, keepdims=True)


def pack_kernel(ids_hbm, tokens_hbm, _, __, out_ref, ids_ref, sems):
    named = pltpu.make_async_copy(ids_hbm, ids_ref, sems.at[0])
    named.start()
    copy = pltpu.make_async_copy(tokens_hbm, out_ref.at[:, 128:], sems.at[1])
    copy.start()
    named.wait()
    names = ids_ref[...].astype(jnp.float32)
    lane = iota((out_ref.shape[0], 128), 1)
    out_ref[:, :128] = jnp.where(lane == 0, as_column(names[0:1]), as_column(names[1:2])).astype(out_ref.dtype)
    copy.wait()


def rows_of(ids_block, group, source, expert, rows, tok_rows, capacity):
    tall = ids_block.shape[0]
    names = ids_block.astype(jnp.float32)
    expert = expert.astype(jnp.float32)
    named = (names[:, 0:1] == expert) | (names[:, 1:2] == expert)
    later, earlier = iota((tall, tall), 0), iota((tall, tall), 1)
    lower = ((later > earlier) & (later // tok_rows == earlier // tok_rows)).astype(jnp.bfloat16)
    flags = jnp.broadcast_to(named.astype(jnp.float32), (tall, 128)).astype(jnp.bfloat16)
    before = exact_dot(lower, flags)[:, 0:1].astype(jnp.int32)
    target = jnp.where(named & (group >= 0), (group * 2 + source) * capacity + before, -1)
    return (iota((tall, rows), 1) == target).astype(jnp.bfloat16)


def picked(ref, group, source, expert, rows, tok_rows, capacity, start, stop):
    sel = rows_of(ref[:, :128], group, source, expert, rows, tok_rows, capacity)
    return transposed_dot(sel, ref[:, 128 + start : 128 + stop])


def layer_of(ref, tok_rows):
    return iota((ref.shape[0], 1), 0) // tok_rows


def cut_kernel(tok_rows, in_ref, out_ref):
    shape = (out_ref.shape[0], in_ref.shape[0])
    row, place = iota(shape, 0), iota(shape, 1)
    layer = (row // tok_rows + 1) ^ lax.axis_index("et")
    move = (place == layer * tok_rows + row % tok_rows).astype(in_ref.dtype)
    out_ref[...] = exact_dot(move, in_ref[:, : out_ref.shape[1]]).astype(out_ref.dtype)


def select_kernel(tok_rows, capacity, own_ref, near_ref, *outs):
    expert, core = lax.axis_index("ep") ^ 2, lax.axis_index("ep") % 2
    rows = outs[0].shape[0]
    group = (layer_of(own_ref, tok_rows) ^ lax.axis_index("et")) - 1
    found = [
        (rows_of(ref[:, :128], group, source, expert, rows, tok_rows, capacity), ref)
        for ref, source in ((own_ref, core), (near_ref, 1 - core))
    ]
    start = own_ref.shape[1] - sum(out.shape[1] for out in outs)
    for out in outs:
        stop = start + out.shape[1]
        out[...] = sum(transposed_dot(sel, ref[:, start:stop]) for sel, ref in found).astype(out.dtype)
        start = stop


def stay_kernel(tok_rows, capacity, own_ref, near_ref, early_ref, early_other, stay_ref, first_ref):
    expert, core = lax.axis_index("ep"), lax.axis_index("ep") % 2
    group = layer_of(own_ref, tok_rows) ^ lax.axis_index("et")
    for out, refs, place in (
        (stay_ref, (own_ref, near_ref), group),
        (first_ref, (early_ref, early_other), layer_of(early_ref, tok_rows)),
    ):
        rows, width = out.shape
        out[...] = sum(
            picked(ref, place, core ^ other, expert, rows, tok_rows, capacity, 0, width)
            for other, ref in enumerate(refs)
        ).astype(out.dtype)


def pick_kernel(tok_rows, capacity, ref, rows_ref):
    rows, width = rows_ref.shape
    expert, core = lax.axis_index("ep"), lax.axis_index("ep") % 2
    group = layer_of(ref, tok_rows)
    rows_ref[...] = picked(ref, group, core, expert, rows, tok_rows, capacity, 0, width).astype(rows_ref.dtype)


def gather_rows(x_ref, stay, first, far):
    rows = stay.shape[0]
    chip = lax.axis_index("ep") // 2
    x_ref[pl.ds(pl.multiple_of(chip * rows, rows), rows), :] = stay
    far = jnp.concatenate([first.astype(jnp.float32), far.astype(jnp.float32)], axis=0)
    x_ref[pl.ds(pl.multiple_of((1 - chip) * rows, rows), rows), :] = far.astype(x_ref.dtype)


def first_kernel(tok_rows, capacity, other_ref, part_ref, stay_ref, early_ref, gate_all, up_all, *refs):
    gate_ref, up_ref, x_ref = refs
    rows, cut = part_ref.shape
    expert, core = lax.axis_index("ep"), lax.axis_index("ep") % 2
    group = layer_of(other_ref, tok_rows)
    far = picked(other_ref, group, 1 - core, expert, rows, tok_rows, capacity, 0, cut)
    far = far + part_ref[...].astype(jnp.float32)
    gather_rows(x_ref, stay_ref[:, :cut], early_ref[:, :cut], far)
    gate_ref[...] = exact_dot(x_ref[...], gate_all[0, :cut, :])
    up_ref[...] = exact_dot(x_ref[...], up_all[0, :cut, :])


def middle_kernel(start, far_ref, stay_ref, early_ref, gate_in, up_in, gate_all, up_all, gate_ref, up_ref, x_ref):
    stop = start + far_ref.shape[1]
    gather_rows(x_ref, stay_ref[:, start:stop], early_ref[:, start:stop], far_ref[...])
    gate_ref[...] = gate_in[...] + exact_dot(x_ref[...], gate_all[0, start:stop, :])
    up_ref[...] = up_in[...] + exact_dot(x_ref[...], up_all[0, start:stop, :])


def second_kernel(folds, experts, far_ref, stay_ref, early_ref, gate_in, up_in, gate_all, up_all, *refs):
    out_ref, x_ref, hidden_ref = refs
    cut = stay_ref.shape[1] - far_ref.shape[1]
    gather_rows(x_ref, stay_ref[:, cut:], early_ref[:, cut:], far_ref[...])
    gate_val = gate_in[...] + exact_dot(x_ref[...], gate_all[0, cut:, :])
    up_val = up_in[...] + exact_dot(x_ref[...], up_all[0, cut:, :])
    hidden_ref[...] = gate_val / (1.0 + jnp.exp(-gate_val)) * up_val
    store_blocks(folds, experts, hidden_ref, out_ref)


def store_blocks(folds, experts, hidden_ref, out_ref):
    peers = out_ref.shape[0]
    capacity = hidden_ref.shape[0] // peers
    span = hidden_ref.shape[1] // folds
    mine = lax.axis_index("et")
    for peer in range(0, peers, 2):
        layer, chip = peer // experts, peer % experts // 2
        start = chip * (peers // 2) * capacity + (layer ^ mine) * (2 * capacity)
        both = hidden_ref[pl.ds(pl.multiple_of(start, 8), 2 * capacity), :]
        for core in range(2):
            rows = both[core * capacity : (core + 1) * capacity]
            pieces = [rows[:, fold * span : (fold + 1) * span] for fold in range(folds)]
            out_ref[peer + core] = jnp.concatenate(pieces, axis=0).astype(out_ref.dtype)


def routed_by_columns(tokens, expert_ids, w_gate, w_up, peers, capacity, folds):
    tok_rows, width = tokens.shape
    units = w_gate.shape[2]
    experts = 4
    rows = peers * capacity
    half = rows // 2
    cuts = (width // 6, 11 * width // 24, 3 * width // 4)
    cut = cuts[0]
    kind = tokens.dtype

    def array(*shape):
        return jax.ShapeDtypeStruct(shape, kind)

    def swap(block, bit):
        return lax.ppermute(block, "ep", [(i, i ^ bit) for i in range(experts)])

    packed = local_kernel(
        pack_kernel,
        array(tok_rows, 128 + width),
        (),
        (expert_ids.T, tokens, w_gate, w_up),
        scratch=[pltpu.VMEM((2, tok_rows), jnp.int32), pltpu.SemaphoreType.DMA((2,))],
    )
    early = swap(packed, 2)
    own = lax.all_gather(packed, "et", axis=0, tiled=True)
    own, early = lax.optimization_barrier((own, early))
    others = own.shape[0] - tok_rows
    rest = half - 2 * capacity
    part = local_kernel(functools.partial(cut_kernel, tok_rows), array(others, 128 + cut), (own,))
    near, far, early_other = swap(own, 1), swap(part, 2), swap(early, 1)
    kernel = functools.partial(select_kernel, tok_rows, capacity)
    ends = (*cuts[1:], width)
    laters = local_kernel(kernel, [array(rest, stop - start) for start, stop in zip(cuts, ends)], (own, near))
    later_fars = [swap(later, 2) for later in laters]
    own, near, *laters = lax.optimization_barrier((own, near, *laters))
    kernel = functools.partial(stay_kernel, tok_rows, capacity)
    outs = [array(half, width), array(2 * capacity, width)]
    stay, first = local_kernel(kernel, outs, (own, near, early, early_other))
    far, stay = lax.optimization_barrier((far, stay))
    far_other = swap(far, 1)
    far_part = local_kernel(functools.partial(pick_kernel, tok_rows, capacity), array(rest, cut), (far,))
    far_other, far_part = lax.optimization_barrier((far_other, far_part))

    def sums(kernel, blocks, span):
        out_shape = [jax.ShapeDtypeStruct((rows, units), jnp.float32)] * 2
        return local_kernel(kernel, out_shape, (*blocks, w_gate, w_up), scratch=[pltpu.VMEM((rows, span), kind)])

    gate_sum, up_sum = sums(
        functools.partial(first_kernel, tok_rows, capacity), (far_other, far_part, stay, first), cut
    )
    for start, later_far in zip(cuts[:-1], later_fars):
        later_far, gate_sum = lax.optimization_barrier((later_far, gate_sum))
        kernel = functools.partial(middle_kernel, start)
        gate_sum, up_sum = sums(kernel, (later_far, stay, first, gate_sum, up_sum), later_far.shape[1])
    later_far, gate_sum = lax.optimization_barrier((later_fars[-1], gate_sum))
    return local_kernel(
        functools.partial(second_kernel, folds, experts),
        pltpu.VMEM((peers, capacity * folds, units // folds), kind),
        (later_far, stay, first, gate_sum, up_sum, w_gate, w_up),
        scratch=[pltpu.VMEM((rows, width - cuts[-1]), kind), pltpu.VMEM((rows, units), jnp.float32)],
    )


def picks_kernel(experts, capacity, folds, ids_ref, weights_ref, picks_ref, column_ref):
    tok_rows = ids_ref.shape[1]
    both = 2 * tok_rows
    ids = [as_column(ids_ref[slot : slot + 1, :]) for slot in range(2)]
    expert = iota((tok_rows, 128), 1)
    named = ((expert == ids[0]) | (expert == ids[1])).astype(jnp.bfloat16)
    lower = (iota((tok_rows, tok_rows), 0) > iota((tok_rows, tok_rows), 1)).astype(jnp.bfloat16)
    before = exact_dot(lower, named).astype(jnp.int32)
    slot_row, token = iota((both, tok_rows), 0), iota((both, tok_rows), 1)
    target = jnp.zeros((both, 1), jnp.int32)
    column = jnp.zeros((both, 1), jnp.float32)
    for slot, chosen in enumerate(ids):
        position = jnp.sum(jnp.where(expert == chosen, before, 0), axis=1, keepdims=True)
        mask = slot_row == 2 * token + slot
        place = as_row(chosen * (folds * capacity) + position)
        target = target + jnp.sum(jnp.where(mask, place, 0), axis=1, keepdims=True)
        column = column + jnp.sum(jnp.where(mask, weights_ref[slot : slot + 1, :], 0.0), axis=1, keepdims=True)
    column_ref[...] = jnp.broadcast_to(column, column_ref.shape)
    lane = iota((both, experts * folds * capacity), 1)
    for fold in range(folds):
        picks_ref[fold * both : (fold + 1) * both, :] = (lane == target + fold * capacity).astype(picks_ref.dtype)


def final_kernel(experts, folds, picks_ref, column_ref, recv_ref, out_ref):
    tok_rows = out_ref.shape[0]
    both = 2 * tok_rows
    peers, tall, span = recv_ref.shape
    column = column_ref[:, 0:1]
    for part in range(peers // experts):
        block = recv_ref[part * experts : (part + 1) * experts].reshape(experts * tall, span)
        rows = exact_dot(picks_ref[...], block)
        for fold in range(folds):
            scaled = rows[fold * both : (fold + 1) * both] * column
            start = (part * folds + fold) * span
            out_ref[:, :, start : start + span] = scaled.astype(out_ref.dtype).reshape(tok_rows, 2, span)


def finish(expert_ids, gate_weights, received, experts, folds):
    tok_rows = expert_ids.shape[0]
    peers, tall, span = received.shape
    capacity = tall // folds
    kind = received.dtype
    picks, column = local_kernel(
        functools.partial(picks_kernel, experts, capacity, folds),
        [
            jax.ShapeDtypeStruct((2 * tok_rows * folds, experts * tall), kind),
            jax.ShapeDtypeStruct((2 * tok_rows, 128), jnp.float32),
        ],
        (expert_ids.T, gate_weights.T),
        moved=1 << 20,
    )
    units = peers // experts * folds * span
    return local_kernel(
        functools.partial(final_kernel, experts, folds),
        jax.ShapeDtypeStruct((tok_rows, 2, units), kind),
        (picks, column, received),
        moved=4 * received.size,
    )


def body(tokens, expert_ids, gate_weights, w_gate, w_up):
    tok_rows, width = tokens.shape
    experts = lax.axis_size("ep")
    tensor_size = lax.axis_size("et")
    peers = experts * tensor_size
    capacity = tok_rows // 2
    gate_local = w_gate[0]
    up_local = w_up[0]
    if experts == 4 and tensor_size == 4:
        folds = 4
        blocks = routed_by_columns(tokens, expert_ids, w_gate, w_up, peers, capacity, folds)
        return finish(expert_ids, gate_weights, exchange(blocks), experts, folds)
    slot_pairs = place_slots(expert_ids, experts, capacity)
    selector = build_select(slot_pairs, experts * capacity)
    buffer = jnp.dot(selector, tokens, preferred_element_type=jnp.float32).astype(jnp.bfloat16)
    buffer = buffer.reshape(1, experts, capacity * width // 128, 128)
    buffer = jnp.broadcast_to(buffer, (tensor_size,) + buffer.shape[1:])
    arrived = exchange(buffer.reshape(peers, capacity * width // 128, 128))
    hidden = swiglu_rows(arrived.reshape(peers * capacity, width), gate_local, up_local)
    units = hidden.shape[1]
    returned = exchange(hidden.reshape(peers, capacity * units // 128, 128))
    returned = returned.reshape(tensor_size, experts * capacity, units)
    targets = jnp.arange(experts * capacity, dtype=jnp.int32)
    picker = (slot_pairs[:, :, None] == targets[None, None, :]).astype(jnp.bfloat16)
    gathered = jnp.einsum("tsj,ejf->tsef", picker, returned, preferred_element_type=jnp.float32)
    gathered = gathered.reshape(tok_rows, 2, tensor_size * units)
    return (gate_weights[:, :, None] * gathered).astype(jnp.bfloat16)


def solution(mesh):
    in_specs = (
        P(("groups", "et", "ep"), None),
        P(("groups", "et", "ep"), None),
        P(("groups", "et", "ep"), None),
        P("ep", None, "et"),
        P("ep", None, "et"),
    )
    out_specs = P(("groups", "et", "ep"), None, None)
    return jax.shard_map(body, mesh=mesh, in_specs=in_specs, out_specs=out_specs, check_vma=False)
```

```python
import functools

import jax
import jax.numpy as jnp
from jax import lax
from jax.experimental import pallas as pl
from jax.experimental.pallas import tpu as pltpu
from jax.sharding import PartitionSpec as P

WHOLE = pl.BlockSpec(memory_space=pltpu.VMEM)
OUTSIDE = pl.BlockSpec(memory_space=pltpu.HBM)


def place_slots(id_block, experts, capacity):
    flat_ids = id_block.reshape(-1)
    onehot = (flat_ids[:, None] == jnp.arange(experts, dtype=jnp.int32)[None, :]).astype(jnp.int32)
    before = jnp.cumsum(onehot, axis=0) - onehot
    position = jnp.sum(before * onehot, axis=1)
    return (flat_ids * capacity + position).reshape(id_block.shape)


def build_select(slot_pairs, total):
    targets = jnp.arange(total, dtype=jnp.int32).reshape(-1, 1, 1)
    return jnp.sum(slot_pairs[..., None, :, :] == targets, axis=-1).astype(jnp.bfloat16)


def swiglu_rows(rows, gate_local, up_local):
    gate_val = jnp.dot(rows, gate_local, preferred_element_type=jnp.float32)
    up_val = jnp.dot(rows, up_local, preferred_element_type=jnp.float32)
    return (jax.nn.silu(gate_val) * up_val).astype(jnp.bfloat16)


def exchange(blocks):
    return lax.all_to_all(blocks, ("et", "ep"), split_axis=0, concat_axis=0, tiled=True)


def local_kernel(kernel, out_shape, args, outside=(), flops=0, moved=0, scratch=(), limit=12):
    return pl.pallas_call(
        kernel,
        out_shape=out_shape,
        in_specs=[WHOLE] * len(args) + [OUTSIDE] * len(outside),
        out_specs=jax.tree.map(lambda _: WHOLE, out_shape),
        scratch_shapes=scratch,
        compiler_params=pltpu.CompilerParams(vmem_limit_bytes=limit << 20),
        cost_estimate=pl.CostEstimate(flops=flops, bytes_accessed=moved, transcendentals=0),
    )(*args, *(pltpu.with_memory_space_constraint(array, pltpu.HBM) for array in outside))


def exact_dot(a, b):
    return jnp.dot(a, b, preferred_element_type=jnp.float32)


def transposed_dot(a, b):
    return lax.dot_general(a, b, (((0,), (0,)), ((), ())), preferred_element_type=jnp.float32)


def iota(shape, dim):
    return lax.broadcasted_iota(jnp.int32, shape, dim)


def as_column(row):
    size = row.shape[1]
    eye = iota((size, size), 0) == iota((size, size), 1)
    return jnp.sum(jnp.where(eye, row, jnp.zeros_like(row)), axis=1, keepdims=True)


def as_row(column):
    size = column.shape[0]
    eye = iota((size, size), 0) == iota((size, size), 1)
    return jnp.sum(jnp.where(eye, column, jnp.zeros_like(column)), axis=0, keepdims=True)


def pack_kernel(ids_hbm, tokens_hbm, _, __, out_ref, ids_ref, sems):
    named = pltpu.make_async_copy(ids_hbm, ids_ref, sems.at[0])
    named.start()
    copy = pltpu.make_async_copy(tokens_hbm, out_ref.at[:, 128:], sems.at[1])
    copy.start()
    named.wait()
    names = ids_ref[...].astype(jnp.float32)
    lane = iota((out_ref.shape[0], 128), 1)
    out_ref[:, :128] = jnp.where(lane == 0, as_column(names[0:1]), as_column(names[1:2])).astype(out_ref.dtype)
    copy.wait()


def rows_of(ids_block, group, source, expert, rows, tok_rows, capacity):
    tall = ids_block.shape[0]
    names = ids_block.astype(jnp.float32)
    expert = expert.astype(jnp.float32)
    named = (names[:, 0:1] == expert) | (names[:, 1:2] == expert)
    later, earlier = iota((tall, tall), 0), iota((tall, tall), 1)
    lower = ((later > earlier) & (later // tok_rows == earlier // tok_rows)).astype(jnp.bfloat16)
    flags = jnp.broadcast_to(named.astype(jnp.float32), (tall, 128)).astype(jnp.bfloat16)
    before = exact_dot(lower, flags)[:, 0:1].astype(jnp.int32)
    target = jnp.where(named & (group >= 0), (group * 2 + source) * capacity + before, -1)
    return (iota((tall, rows), 1) == target).astype(jnp.bfloat16)


def picked(ref, group, source, expert, rows, tok_rows, capacity, start, stop):
    sel = rows_of(ref[:, :128], group, source, expert, rows, tok_rows, capacity)
    return transposed_dot(sel, ref[:, 128 + start : 128 + stop])


def layer_of(ref, tok_rows):
    return iota((ref.shape[0], 1), 0) // tok_rows


def cut_kernel(tok_rows, in_ref, out_ref):
    shape = (out_ref.shape[0], in_ref.shape[0])
    row, place = iota(shape, 0), iota(shape, 1)
    layer = (row // tok_rows + 1) ^ lax.axis_index("et")
    move = (place == layer * tok_rows + row % tok_rows).astype(in_ref.dtype)
    out_ref[...] = exact_dot(move, in_ref[:, : out_ref.shape[1]]).astype(out_ref.dtype)


def select_kernel(tok_rows, capacity, own_ref, near_ref, *outs):
    expert, core = lax.axis_index("ep") ^ 2, lax.axis_index("ep") % 2
    rows = outs[0].shape[0]
    group = (layer_of(own_ref, tok_rows) ^ lax.axis_index("et")) - 1
    found = [
        (rows_of(ref[:, :128], group, source, expert, rows, tok_rows, capacity), ref)
        for ref, source in ((own_ref, core), (near_ref, 1 - core))
    ]
    start = own_ref.shape[1] - sum(out.shape[1] for out in outs)
    for out in outs:
        stop = start + out.shape[1]
        out[...] = sum(transposed_dot(sel, ref[:, start:stop]) for sel, ref in found).astype(out.dtype)
        start = stop


def stay_kernel(tok_rows, capacity, own_ref, near_ref, early_ref, early_other, stay_ref, first_ref):
    expert, core = lax.axis_index("ep"), lax.axis_index("ep") % 2
    group = layer_of(own_ref, tok_rows) ^ lax.axis_index("et")
    for out, refs, place in (
        (stay_ref, (own_ref, near_ref), group),
        (first_ref, (early_ref, early_other), layer_of(early_ref, tok_rows)),
    ):
        rows, width = out.shape
        out[...] = sum(
            picked(ref, place, core ^ other, expert, rows, tok_rows, capacity, 0, width)
            for other, ref in enumerate(refs)
        ).astype(out.dtype)


def pick_kernel(tok_rows, capacity, ref, rows_ref):
    rows, width = rows_ref.shape
    expert, core = lax.axis_index("ep"), lax.axis_index("ep") % 2
    group = layer_of(ref, tok_rows)
    rows_ref[...] = picked(ref, group, core, expert, rows, tok_rows, capacity, 0, width).astype(rows_ref.dtype)


def gather_rows(x_ref, stay, first, far):
    rows = stay.shape[0]
    chip = lax.axis_index("ep") // 2
    x_ref[pl.ds(pl.multiple_of(chip * rows, rows), rows), :] = stay
    far = jnp.concatenate([first.astype(jnp.float32), far.astype(jnp.float32)], axis=0)
    x_ref[pl.ds(pl.multiple_of((1 - chip) * rows, rows), rows), :] = far.astype(x_ref.dtype)


def first_kernel(tok_rows, capacity, other_ref, part_ref, stay_ref, early_ref, gate_all, up_all, *refs):
    gate_ref, up_ref, x_ref = refs
    rows, cut = part_ref.shape
    expert, core = lax.axis_index("ep"), lax.axis_index("ep") % 2
    group = layer_of(other_ref, tok_rows)
    far = picked(other_ref, group, 1 - core, expert, rows, tok_rows, capacity, 0, cut)
    far = far + part_ref[...].astype(jnp.float32)
    gather_rows(x_ref, stay_ref[:, :cut], early_ref[:, :cut], far)
    gate_ref[...] = exact_dot(x_ref[...], gate_all[0, :cut, :])
    up_ref[...] = exact_dot(x_ref[...], up_all[0, :cut, :])


def middle_kernel(start, far_ref, stay_ref, early_ref, gate_in, up_in, gate_all, up_all, gate_ref, up_ref, x_ref):
    stop = start + far_ref.shape[1]
    gather_rows(x_ref, stay_ref[:, start:stop], early_ref[:, start:stop], far_ref[...])
    gate_ref[...] = gate_in[...] + exact_dot(x_ref[...], gate_all[0, start:stop, :])
    up_ref[...] = up_in[...] + exact_dot(x_ref[...], up_all[0, start:stop, :])


def second_kernel(folds, experts, far_ref, stay_ref, early_ref, gate_in, up_in, gate_all, up_all, *refs):
    out_ref, x_ref, hidden_ref = refs
    cut = stay_ref.shape[1] - far_ref.shape[1]
    gather_rows(x_ref, stay_ref[:, cut:], early_ref[:, cut:], far_ref[...])
    gate_val = gate_in[...] + exact_dot(x_ref[...], gate_all[0, cut:, :])
    up_val = up_in[...] + exact_dot(x_ref[...], up_all[0, cut:, :])
    hidden_ref[...] = gate_val / (1.0 + jnp.exp(-gate_val)) * up_val
    store_blocks(folds, experts, hidden_ref, out_ref)


def store_blocks(folds, experts, hidden_ref, out_ref):
    peers = out_ref.shape[0]
    capacity = hidden_ref.shape[0] // peers
    span = hidden_ref.shape[1] // folds
    mine = lax.axis_index("et")
    for peer in range(0, peers, 2):
        layer, chip = peer // experts, peer % experts // 2
        start = chip * (peers // 2) * capacity + (layer ^ mine) * (2 * capacity)
        both = hidden_ref[pl.ds(pl.multiple_of(start, 8), 2 * capacity), :]
        for core in range(2):
            rows = both[core * capacity : (core + 1) * capacity]
            pieces = [rows[:, fold * span : (fold + 1) * span] for fold in range(folds)]
            out_ref[peer + core] = jnp.concatenate(pieces, axis=0).astype(out_ref.dtype)


def routed_by_columns(tokens, expert_ids, w_gate, w_up, peers, capacity, folds):
    tok_rows, width = tokens.shape
    units = w_gate.shape[2]
    experts = 4
    rows = peers * capacity
    half = rows // 2
    cuts = (width // 6, 11 * width // 24, 3 * width // 4)
    cut = cuts[0]
    kind = tokens.dtype

    def array(*shape):
        return jax.ShapeDtypeStruct(shape, kind)

    def swap(block, bit):
        return lax.ppermute(block, "ep", [(i, i ^ bit) for i in range(experts)])

    packed = local_kernel(
        pack_kernel,
        array(tok_rows, 128 + width),
        (),
        (expert_ids.T, tokens, w_gate, w_up),
        scratch=[pltpu.VMEM((2, tok_rows), jnp.int32), pltpu.SemaphoreType.DMA((2,))],
    )
    early = swap(packed, 2)
    own = lax.all_gather(packed, "et", axis=0, tiled=True)
    own, early = lax.optimization_barrier((own, early))
    others = own.shape[0] - tok_rows
    rest = half - 2 * capacity
    part = local_kernel(functools.partial(cut_kernel, tok_rows), array(others, 128 + cut), (own,))
    near, far, early_other = swap(own, 1), swap(part, 2), swap(early, 1)
    kernel = functools.partial(select_kernel, tok_rows, capacity)
    ends = (*cuts[1:], width)
    laters = local_kernel(kernel, [array(rest, stop - start) for start, stop in zip(cuts, ends)], (own, near))
    later_fars = [swap(later, 2) for later in laters]
    own, near, *laters = lax.optimization_barrier((own, near, *laters))
    kernel = functools.partial(stay_kernel, tok_rows, capacity)
    outs = [array(half, width), array(2 * capacity, width)]
    stay, first = local_kernel(kernel, outs, (own, near, early, early_other))
    far_other = swap(far, 1)
    far_part = local_kernel(functools.partial(pick_kernel, tok_rows, capacity), array(rest, cut), (far,))
    far_other, far_part, stay = lax.optimization_barrier((far_other, far_part, stay))

    def sums(kernel, blocks, span):
        out_shape = [jax.ShapeDtypeStruct((rows, units), jnp.float32)] * 2
        return local_kernel(kernel, out_shape, (*blocks, w_gate, w_up), scratch=[pltpu.VMEM((rows, span), kind)])

    gate_sum, up_sum = sums(
        functools.partial(first_kernel, tok_rows, capacity), (far_other, far_part, stay, first), cut
    )
    for start, later_far in zip(cuts[:-1], later_fars):
        later_far, gate_sum = lax.optimization_barrier((later_far, gate_sum))
        kernel = functools.partial(middle_kernel, start)
        gate_sum, up_sum = sums(kernel, (later_far, stay, first, gate_sum, up_sum), later_far.shape[1])
    later_far, gate_sum = lax.optimization_barrier((later_fars[-1], gate_sum))
    return local_kernel(
        functools.partial(second_kernel, folds, experts),
        pltpu.VMEM((peers, capacity * folds, units // folds), kind),
        (later_far, stay, first, gate_sum, up_sum, w_gate, w_up),
        scratch=[pltpu.VMEM((rows, width - cuts[-1]), kind), pltpu.VMEM((rows, units), jnp.float32)],
    )


def picks_kernel(experts, capacity, folds, ids_ref, weights_ref, picks_ref, column_ref):
    tok_rows = ids_ref.shape[1]
    both = 2 * tok_rows
    ids = [as_column(ids_ref[slot : slot + 1, :]) for slot in range(2)]
    expert = iota((tok_rows, 128), 1)
    named = ((expert == ids[0]) | (expert == ids[1])).astype(jnp.bfloat16)
    lower = (iota((tok_rows, tok_rows), 0) > iota((tok_rows, tok_rows), 1)).astype(jnp.bfloat16)
    before = exact_dot(lower, named).astype(jnp.int32)
    slot_row, token = iota((both, tok_rows), 0), iota((both, tok_rows), 1)
    target = jnp.zeros((both, 1), jnp.int32)
    column = jnp.zeros((both, 1), jnp.float32)
    for slot, chosen in enumerate(ids):
        position = jnp.sum(jnp.where(expert == chosen, before, 0), axis=1, keepdims=True)
        mask = slot_row == 2 * token + slot
        place = as_row(chosen * (folds * capacity) + position)
        target = target + jnp.sum(jnp.where(mask, place, 0), axis=1, keepdims=True)
        column = column + jnp.sum(jnp.where(mask, weights_ref[slot : slot + 1, :], 0.0), axis=1, keepdims=True)
    column_ref[...] = jnp.broadcast_to(column, column_ref.shape)
    lane = iota((both, experts * folds * capacity), 1)
    for fold in range(folds):
        picks_ref[fold * both : (fold + 1) * both, :] = (lane == target + fold * capacity).astype(picks_ref.dtype)


def final_kernel(experts, folds, picks_ref, column_ref, recv_ref, out_hbm, out_ref, sems):
    tok_rows = out_ref.shape[0]
    both = 2 * tok_rows
    peers, tall, span = recv_ref.shape
    column = column_ref[:, 0:1]
    copies = []
    for part in range(peers // experts):
        block = recv_ref[part * experts : (part + 1) * experts].reshape(experts * tall, span)
        rows = exact_dot(picks_ref[...], block)
        for fold in range(folds):
            scaled = rows[fold * both : (fold + 1) * both] * column
            start = (part * folds + fold) * span
            out_ref[:, :, start : start + span] = scaled.astype(out_ref.dtype).reshape(tok_rows, 2, span)
        columns = slice(part * folds * span, (part + 1) * folds * span)
        copy = pltpu.make_async_copy(out_ref.at[:, :, columns], out_hbm.at[:, :, columns], sems.at[part])
        copy.start()
        copies.append(copy)
    for copy in copies:
        copy.wait()


def finish(expert_ids, gate_weights, received, experts, folds):
    tok_rows = expert_ids.shape[0]
    peers, tall, span = received.shape
    capacity = tall // folds
    kind = received.dtype
    picks, column = local_kernel(
        functools.partial(picks_kernel, experts, capacity, folds),
        [
            jax.ShapeDtypeStruct((2 * tok_rows * folds, experts * tall), kind),
            jax.ShapeDtypeStruct((2 * tok_rows, 128), jnp.float32),
        ],
        (expert_ids.T, gate_weights.T),
        moved=1 << 20,
    )
    units = peers // experts * folds * span
    return pl.pallas_call(
        functools.partial(final_kernel, experts, folds),
        out_shape=jax.ShapeDtypeStruct((tok_rows, 2, units), kind),
        in_specs=[WHOLE] * 3,
        out_specs=OUTSIDE,
        scratch_shapes=[pltpu.VMEM((tok_rows, 2, units), kind), pltpu.SemaphoreType.DMA((peers // experts,))],
        compiler_params=pltpu.CompilerParams(vmem_limit_bytes=12 << 20),
    )(picks, column, received)


def body(tokens, expert_ids, gate_weights, w_gate, w_up):
    tok_rows, width = tokens.shape
    experts = lax.axis_size("ep")
    tensor_size = lax.axis_size("et")
    peers = experts * tensor_size
    capacity = tok_rows // 2
    gate_local = w_gate[0]
    up_local = w_up[0]
    if experts == 4 and tensor_size == 4:
        folds = 4
        blocks = routed_by_columns(tokens, expert_ids, w_gate, w_up, peers, capacity, folds)
        return finish(expert_ids, gate_weights, exchange(blocks), experts, folds)
    slot_pairs = place_slots(expert_ids, experts, capacity)
    selector = build_select(slot_pairs, experts * capacity)
    buffer = jnp.dot(selector, tokens, preferred_element_type=jnp.float32).astype(jnp.bfloat16)
    buffer = buffer.reshape(1, experts, capacity * width // 128, 128)
    buffer = jnp.broadcast_to(buffer, (tensor_size,) + buffer.shape[1:])
    arrived = exchange(buffer.reshape(peers, capacity * width // 128, 128))
    hidden = swiglu_rows(arrived.reshape(peers * capacity, width), gate_local, up_local)
    units = hidden.shape[1]
    returned = exchange(hidden.reshape(peers, capacity * units // 128, 128))
    returned = returned.reshape(tensor_size, experts * capacity, units)
    targets = jnp.arange(experts * capacity, dtype=jnp.int32)
    picker = (slot_pairs[:, :, None] == targets[None, None, :]).astype(jnp.bfloat16)
    gathered = jnp.einsum("tsj,ejf->tsef", picker, returned, preferred_element_type=jnp.float32)
    gathered = gathered.reshape(tok_rows, 2, tensor_size * units)
    return (gate_weights[:, :, None] * gathered).astype(jnp.bfloat16)


def solution(mesh):
    in_specs = (
        P(("groups", "et", "ep"), None),
        P(("groups", "et", "ep"), None),
        P(("groups", "et", "ep"), None),
        P("ep", None, "et"),
        P("ep", None, "et"),
    )
    out_specs = P(("groups", "et", "ep"), None, None)
    return jax.shard_map(body, mesh=mesh, in_specs=in_specs, out_specs=out_specs, check_vma=False)
```

```python
import functools

import jax
import jax.numpy as jnp
from jax import lax
from jax.experimental import pallas as pl
from jax.experimental.pallas import tpu as pltpu
from jax.sharding import PartitionSpec as P

WHOLE = pl.BlockSpec(memory_space=pltpu.VMEM)
OUTSIDE = pl.BlockSpec(memory_space=pltpu.HBM)


def place_slots(id_block, experts, capacity):
    flat_ids = id_block.reshape(-1)
    onehot = (flat_ids[:, None] == jnp.arange(experts, dtype=jnp.int32)[None, :]).astype(jnp.int32)
    before = jnp.cumsum(onehot, axis=0) - onehot
    position = jnp.sum(before * onehot, axis=1)
    return (flat_ids * capacity + position).reshape(id_block.shape)


def build_select(slot_pairs, total):
    targets = jnp.arange(total, dtype=jnp.int32).reshape(-1, 1, 1)
    return jnp.sum(slot_pairs[..., None, :, :] == targets, axis=-1).astype(jnp.bfloat16)


def swiglu_rows(rows, gate_local, up_local):
    gate_val = jnp.dot(rows, gate_local, preferred_element_type=jnp.float32)
    up_val = jnp.dot(rows, up_local, preferred_element_type=jnp.float32)
    return (jax.nn.silu(gate_val) * up_val).astype(jnp.bfloat16)


def exchange(blocks):
    return lax.all_to_all(blocks, ("et", "ep"), split_axis=0, concat_axis=0, tiled=True)


def local_kernel(kernel, out_shape, args, outside=(), flops=0, moved=0, scratch=(), limit=12):
    return pl.pallas_call(
        kernel,
        out_shape=out_shape,
        in_specs=[WHOLE] * len(args) + [OUTSIDE] * len(outside),
        out_specs=jax.tree.map(lambda _: WHOLE, out_shape),
        scratch_shapes=scratch,
        compiler_params=pltpu.CompilerParams(vmem_limit_bytes=limit << 20),
        cost_estimate=pl.CostEstimate(flops=flops, bytes_accessed=moved, transcendentals=0),
    )(*args, *(pltpu.with_memory_space_constraint(array, pltpu.HBM) for array in outside))


def exact_dot(a, b):
    return jnp.dot(a, b, preferred_element_type=jnp.float32)


def transposed_dot(a, b):
    return lax.dot_general(a, b, (((0,), (0,)), ((), ())), preferred_element_type=jnp.float32)


def iota(shape, dim):
    return lax.broadcasted_iota(jnp.int32, shape, dim)


def as_column(row):
    size = row.shape[1]
    eye = iota((size, size), 0) == iota((size, size), 1)
    return jnp.sum(jnp.where(eye, row, jnp.zeros_like(row)), axis=1, keepdims=True)


def as_row(column):
    size = column.shape[0]
    eye = iota((size, size), 0) == iota((size, size), 1)
    return jnp.sum(jnp.where(eye, column, jnp.zeros_like(column)), axis=0, keepdims=True)


def pack_kernel(ids_hbm, tokens_hbm, _, __, out_ref, ids_ref, sems):
    named = pltpu.make_async_copy(ids_hbm, ids_ref, sems.at[0])
    named.start()
    copy = pltpu.make_async_copy(tokens_hbm, out_ref.at[:, 128:], sems.at[1])
    copy.start()
    named.wait()
    names = ids_ref[...].astype(jnp.float32)
    lane = iota((out_ref.shape[0], 128), 1)
    out_ref[:, :128] = jnp.where(lane == 0, as_column(names[0:1]), as_column(names[1:2])).astype(out_ref.dtype)
    copy.wait()


def rows_of(ids_block, group, source, expert, rows, tok_rows, capacity):
    tall = ids_block.shape[0]
    names = ids_block.astype(jnp.float32)
    expert = expert.astype(jnp.float32)
    named = (names[:, 0:1] == expert) | (names[:, 1:2] == expert)
    later, earlier = iota((tall, tall), 0), iota((tall, tall), 1)
    lower = ((later > earlier) & (later // tok_rows == earlier // tok_rows)).astype(jnp.bfloat16)
    flags = jnp.broadcast_to(named.astype(jnp.float32), (tall, 128)).astype(jnp.bfloat16)
    before = exact_dot(lower, flags)[:, 0:1].astype(jnp.int32)
    target = jnp.where(named & (group >= 0), (group * 2 + source) * capacity + before, -1)
    return (iota((tall, rows), 1) == target).astype(jnp.bfloat16)


def picked(ref, group, source, expert, rows, tok_rows, capacity, start, stop):
    sel = rows_of(ref[:, :128], group, source, expert, rows, tok_rows, capacity)
    return transposed_dot(sel, ref[:, 128 + start : 128 + stop])


def layer_of(ref, tok_rows):
    return iota((ref.shape[0], 1), 0) // tok_rows


def cut_kernel(tok_rows, in_ref, out_ref):
    shape = (out_ref.shape[0], in_ref.shape[0])
    row, place = iota(shape, 0), iota(shape, 1)
    layer = (row // tok_rows + 1) ^ lax.axis_index("et")
    move = (place == layer * tok_rows + row % tok_rows).astype(in_ref.dtype)
    out_ref[...] = exact_dot(move, in_ref[:, : out_ref.shape[1]]).astype(out_ref.dtype)


def select_kernel(tok_rows, capacity, start, own_ref, near_ref, *outs):
    expert, core = lax.axis_index("ep") ^ 2, lax.axis_index("ep") % 2
    rows = outs[0].shape[0]
    group = (layer_of(own_ref, tok_rows) ^ lax.axis_index("et")) - 1
    found = [
        (rows_of(ref[:, :128], group, source, expert, rows, tok_rows, capacity), ref)
        for ref, source in ((own_ref, core), (near_ref, 1 - core))
    ]
    start = 128 + start
    for out in outs:
        stop = start + out.shape[1]
        out[...] = sum(transposed_dot(sel, ref[:, start:stop]) for sel, ref in found).astype(out.dtype)
        start = stop


def stay_kernel(tok_rows, capacity, own_ref, near_ref, early_ref, early_other, stay_ref, first_ref):
    expert, core = lax.axis_index("ep"), lax.axis_index("ep") % 2
    group = layer_of(own_ref, tok_rows) ^ lax.axis_index("et")
    for out, refs, place in (
        (stay_ref, (own_ref, near_ref), group),
        (first_ref, (early_ref, early_other), layer_of(early_ref, tok_rows)),
    ):
        rows, width = out.shape
        out[...] = sum(
            picked(ref, place, core ^ other, expert, rows, tok_rows, capacity, 0, width)
            for other, ref in enumerate(refs)
        ).astype(out.dtype)


def pick_kernel(tok_rows, capacity, ref, rows_ref):
    rows, width = rows_ref.shape
    expert, core = lax.axis_index("ep"), lax.axis_index("ep") % 2
    group = layer_of(ref, tok_rows)
    rows_ref[...] = picked(ref, group, core, expert, rows, tok_rows, capacity, 0, width).astype(rows_ref.dtype)


def gather_rows(x_ref, stay, first, far):
    rows = stay.shape[0]
    chip = lax.axis_index("ep") // 2
    x_ref[pl.ds(pl.multiple_of(chip * rows, rows), rows), :] = stay
    far = jnp.concatenate([first.astype(jnp.float32), far.astype(jnp.float32)], axis=0)
    x_ref[pl.ds(pl.multiple_of((1 - chip) * rows, rows), rows), :] = far.astype(x_ref.dtype)


def first_kernel(tok_rows, capacity, other_ref, part_ref, stay_ref, early_ref, gate_all, up_all, *refs):
    gate_ref, up_ref, x_ref = refs
    rows, cut = part_ref.shape
    expert, core = lax.axis_index("ep"), lax.axis_index("ep") % 2
    group = layer_of(other_ref, tok_rows)
    far = picked(other_ref, group, 1 - core, expert, rows, tok_rows, capacity, 0, cut)
    far = far + part_ref[...].astype(jnp.float32)
    gather_rows(x_ref, stay_ref[:, :cut], early_ref[:, :cut], far)
    gate_ref[...] = exact_dot(x_ref[...], gate_all[0, :cut, :])
    up_ref[...] = exact_dot(x_ref[...], up_all[0, :cut, :])


def middle_kernel(start, far_ref, stay_ref, early_ref, gate_in, up_in, gate_all, up_all, gate_ref, up_ref, x_ref):
    stop = start + far_ref.shape[1]
    gather_rows(x_ref, stay_ref[:, start:stop], early_ref[:, start:stop], far_ref[...])
    gate_ref[...] = gate_in[...] + exact_dot(x_ref[...], gate_all[0, start:stop, :])
    up_ref[...] = up_in[...] + exact_dot(x_ref[...], up_all[0, start:stop, :])


def second_kernel(folds, experts, far_ref, stay_ref, early_ref, gate_in, up_in, gate_all, up_all, *refs):
    out_ref, x_ref, hidden_ref = refs
    cut = stay_ref.shape[1] - far_ref.shape[1]
    gather_rows(x_ref, stay_ref[:, cut:], early_ref[:, cut:], far_ref[...])
    gate_val = gate_in[...] + exact_dot(x_ref[...], gate_all[0, cut:, :])
    up_val = up_in[...] + exact_dot(x_ref[...], up_all[0, cut:, :])
    hidden_ref[...] = gate_val / (1.0 + jnp.exp(-gate_val)) * up_val
    store_blocks(folds, experts, hidden_ref, out_ref)


def store_blocks(folds, experts, hidden_ref, out_ref):
    peers = out_ref.shape[0]
    capacity = hidden_ref.shape[0] // peers
    span = hidden_ref.shape[1] // folds
    mine = lax.axis_index("et")
    for peer in range(0, peers, 2):
        layer, chip = peer // experts, peer % experts // 2
        start = chip * (peers // 2) * capacity + (layer ^ mine) * (2 * capacity)
        both = hidden_ref[pl.ds(pl.multiple_of(start, 8), 2 * capacity), :]
        for core in range(2):
            rows = both[core * capacity : (core + 1) * capacity]
            pieces = [rows[:, fold * span : (fold + 1) * span] for fold in range(folds)]
            out_ref[peer + core] = jnp.concatenate(pieces, axis=0).astype(out_ref.dtype)


def routed_by_columns(tokens, expert_ids, w_gate, w_up, peers, capacity, folds):
    tok_rows, width = tokens.shape
    units = w_gate.shape[2]
    experts = 4
    rows = peers * capacity
    half = rows // 2
    cuts = (width // 6, 11 * width // 24, 3 * width // 4)
    cut = cuts[0]
    kind = tokens.dtype

    def array(*shape):
        return jax.ShapeDtypeStruct(shape, kind)

    def swap(block, bit):
        return lax.ppermute(block, "ep", [(i, i ^ bit) for i in range(experts)])

    packed = local_kernel(
        pack_kernel,
        array(tok_rows, 128 + width),
        (),
        (expert_ids.T, tokens, w_gate, w_up),
        scratch=[pltpu.VMEM((2, tok_rows), jnp.int32), pltpu.SemaphoreType.DMA((2,))],
    )
    early = swap(packed, 2)
    own = lax.all_gather(packed, "et", axis=0, tiled=True)
    own, early = lax.optimization_barrier((own, early))
    others = own.shape[0] - tok_rows
    rest = half - 2 * capacity
    part = local_kernel(functools.partial(cut_kernel, tok_rows), array(others, 128 + cut), (own,))
    near, far, early_other = swap(own, 1), swap(part, 2), swap(early, 1)
    ends = (*cuts[1:], width)
    spans = [array(rest, stop - start) for start, stop in zip(cuts, ends)]
    laters = [
        part
        for low, high in ((0, 1), (1, len(cuts)))
        for part in local_kernel(
            functools.partial(select_kernel, tok_rows, capacity, cuts[low]), spans[low:high], (own, near)
        )
    ]
    later_fars = [swap(later, 2) for later in laters]
    own, near, *laters = lax.optimization_barrier((own, near, *laters))
    kernel = functools.partial(stay_kernel, tok_rows, capacity)
    outs = [array(half, width), array(2 * capacity, width)]
    stay, first = local_kernel(kernel, outs, (own, near, early, early_other))
    far_other = swap(far, 1)
    far_part = local_kernel(functools.partial(pick_kernel, tok_rows, capacity), array(rest, cut), (far,))
    far_other, far_part, stay = lax.optimization_barrier((far_other, far_part, stay))

    def sums(kernel, blocks, span):
        out_shape = [jax.ShapeDtypeStruct((rows, units), jnp.float32)] * 2
        return local_kernel(kernel, out_shape, (*blocks, w_gate, w_up), scratch=[pltpu.VMEM((rows, span), kind)])

    gate_sum, up_sum = sums(
        functools.partial(first_kernel, tok_rows, capacity), (far_other, far_part, stay, first), cut
    )
    for start, later_far in zip(cuts[:-1], later_fars):
        later_far, gate_sum = lax.optimization_barrier((later_far, gate_sum))
        kernel = functools.partial(middle_kernel, start)
        gate_sum, up_sum = sums(kernel, (later_far, stay, first, gate_sum, up_sum), later_far.shape[1])
    later_far, gate_sum = lax.optimization_barrier((later_fars[-1], gate_sum))
    return local_kernel(
        functools.partial(second_kernel, folds, experts),
        pltpu.VMEM((peers, capacity * folds, units // folds), kind),
        (later_far, stay, first, gate_sum, up_sum, w_gate, w_up),
        scratch=[pltpu.VMEM((rows, width - cuts[-1]), kind), pltpu.VMEM((rows, units), jnp.float32)],
    )


def picks_kernel(experts, capacity, folds, ids_ref, weights_ref, picks_ref, column_ref):
    tok_rows = ids_ref.shape[1]
    both = 2 * tok_rows
    ids = [as_column(ids_ref[slot : slot + 1, :]) for slot in range(2)]
    expert = iota((tok_rows, 128), 1)
    named = ((expert == ids[0]) | (expert == ids[1])).astype(jnp.bfloat16)
    lower = (iota((tok_rows, tok_rows), 0) > iota((tok_rows, tok_rows), 1)).astype(jnp.bfloat16)
    before = exact_dot(lower, named).astype(jnp.int32)
    slot_row, token = iota((both, tok_rows), 0), iota((both, tok_rows), 1)
    target = jnp.zeros((both, 1), jnp.int32)
    column = jnp.zeros((both, 1), jnp.float32)
    for slot, chosen in enumerate(ids):
        position = jnp.sum(jnp.where(expert == chosen, before, 0), axis=1, keepdims=True)
        mask = slot_row == 2 * token + slot
        place = as_row(chosen * (folds * capacity) + position)
        target = target + jnp.sum(jnp.where(mask, place, 0), axis=1, keepdims=True)
        column = column + jnp.sum(jnp.where(mask, weights_ref[slot : slot + 1, :], 0.0), axis=1, keepdims=True)
    column_ref[...] = jnp.broadcast_to(column, column_ref.shape)
    lane = iota((both, experts * folds * capacity), 1)
    for fold in range(folds):
        picks_ref[fold * both : (fold + 1) * both, :] = (lane == target + fold * capacity).astype(picks_ref.dtype)


def final_kernel(experts, folds, picks_ref, column_ref, recv_ref, out_hbm, out_ref, sems):
    tok_rows = out_ref.shape[0]
    both = 2 * tok_rows
    peers, tall, span = recv_ref.shape
    column = column_ref[:, 0:1]
    copies = []
    for part in range(peers // experts):
        block = recv_ref[part * experts : (part + 1) * experts].reshape(experts * tall, span)
        rows = exact_dot(picks_ref[...], block)
        for fold in range(folds):
            scaled = rows[fold * both : (fold + 1) * both] * column
            start = (part * folds + fold) * span
            out_ref[:, :, start : start + span] = scaled.astype(out_ref.dtype).reshape(tok_rows, 2, span)
        columns = slice(part * folds * span, (part + 1) * folds * span)
        copy = pltpu.make_async_copy(out_ref.at[:, :, columns], out_hbm.at[:, :, columns], sems.at[part])
        copy.start()
        copies.append(copy)
    for copy in copies:
        copy.wait()


def finish(expert_ids, gate_weights, received, experts, folds):
    tok_rows = expert_ids.shape[0]
    peers, tall, span = received.shape
    capacity = tall // folds
    kind = received.dtype
    picks, column = local_kernel(
        functools.partial(picks_kernel, experts, capacity, folds),
        [
            jax.ShapeDtypeStruct((2 * tok_rows * folds, experts * tall), kind),
            jax.ShapeDtypeStruct((2 * tok_rows, 128), jnp.float32),
        ],
        (expert_ids.T, gate_weights.T),
        moved=1 << 20,
    )
    units = peers // experts * folds * span
    return pl.pallas_call(
        functools.partial(final_kernel, experts, folds),
        out_shape=jax.ShapeDtypeStruct((tok_rows, 2, units), kind),
        in_specs=[WHOLE] * 3,
        out_specs=OUTSIDE,
        scratch_shapes=[pltpu.VMEM((tok_rows, 2, units), kind), pltpu.SemaphoreType.DMA((peers // experts,))],
        compiler_params=pltpu.CompilerParams(vmem_limit_bytes=12 << 20),
    )(picks, column, received)


def body(tokens, expert_ids, gate_weights, w_gate, w_up):
    tok_rows, width = tokens.shape
    experts = lax.axis_size("ep")
    tensor_size = lax.axis_size("et")
    peers = experts * tensor_size
    capacity = tok_rows // 2
    gate_local = w_gate[0]
    up_local = w_up[0]
    if experts == 4 and tensor_size == 4:
        folds = 4
        blocks = routed_by_columns(tokens, expert_ids, w_gate, w_up, peers, capacity, folds)
        return finish(expert_ids, gate_weights, exchange(blocks), experts, folds)
    slot_pairs = place_slots(expert_ids, experts, capacity)
    selector = build_select(slot_pairs, experts * capacity)
    buffer = jnp.dot(selector, tokens, preferred_element_type=jnp.float32).astype(jnp.bfloat16)
    buffer = buffer.reshape(1, experts, capacity * width // 128, 128)
    buffer = jnp.broadcast_to(buffer, (tensor_size,) + buffer.shape[1:])
    arrived = exchange(buffer.reshape(peers, capacity * width // 128, 128))
    hidden = swiglu_rows(arrived.reshape(peers * capacity, width), gate_local, up_local)
    units = hidden.shape[1]
    returned = exchange(hidden.reshape(peers, capacity * units // 128, 128))
    returned = returned.reshape(tensor_size, experts * capacity, units)
    targets = jnp.arange(experts * capacity, dtype=jnp.int32)
    picker = (slot_pairs[:, :, None] == targets[None, None, :]).astype(jnp.bfloat16)
    gathered = jnp.einsum("tsj,ejf->tsef", picker, returned, preferred_element_type=jnp.float32)
    gathered = gathered.reshape(tok_rows, 2, tensor_size * units)
    return (gate_weights[:, :, None] * gathered).astype(jnp.bfloat16)


def solution(mesh):
    in_specs = (
        P(("groups", "et", "ep"), None),
        P(("groups", "et", "ep"), None),
        P(("groups", "et", "ep"), None),
        P("ep", None, "et"),
        P("ep", None, "et"),
    )
    out_specs = P(("groups", "et", "ep"), None, None)
    return jax.shard_map(body, mesh=mesh, in_specs=in_specs, out_specs=out_specs, check_vma=False)
```

```python
import functools

import jax
import jax.numpy as jnp
from jax import lax
from jax.experimental import pallas as pl
from jax.experimental.pallas import tpu as pltpu
from jax.sharding import PartitionSpec as P

WHOLE = pl.BlockSpec(memory_space=pltpu.VMEM)
OUTSIDE = pl.BlockSpec(memory_space=pltpu.HBM)


def place_slots(id_block, experts, capacity):
    flat_ids = id_block.reshape(-1)
    onehot = (flat_ids[:, None] == jnp.arange(experts, dtype=jnp.int32)[None, :]).astype(jnp.int32)
    before = jnp.cumsum(onehot, axis=0) - onehot
    position = jnp.sum(before * onehot, axis=1)
    return (flat_ids * capacity + position).reshape(id_block.shape)


def build_select(slot_pairs, total):
    targets = jnp.arange(total, dtype=jnp.int32).reshape(-1, 1, 1)
    return jnp.sum(slot_pairs[..., None, :, :] == targets, axis=-1).astype(jnp.bfloat16)


def swiglu_rows(rows, gate_local, up_local):
    gate_val = jnp.dot(rows, gate_local, preferred_element_type=jnp.float32)
    up_val = jnp.dot(rows, up_local, preferred_element_type=jnp.float32)
    return (jax.nn.silu(gate_val) * up_val).astype(jnp.bfloat16)


def exchange(blocks):
    return lax.all_to_all(blocks, ("et", "ep"), split_axis=0, concat_axis=0, tiled=True)


def local_kernel(kernel, out_shape, args, outside=(), flops=0, moved=0, scratch=(), limit=12):
    return pl.pallas_call(
        kernel,
        out_shape=out_shape,
        in_specs=[WHOLE] * len(args) + [OUTSIDE] * len(outside),
        out_specs=jax.tree.map(lambda _: WHOLE, out_shape),
        scratch_shapes=scratch,
        compiler_params=pltpu.CompilerParams(vmem_limit_bytes=limit << 20),
        cost_estimate=pl.CostEstimate(flops=flops, bytes_accessed=moved, transcendentals=0),
    )(*args, *(pltpu.with_memory_space_constraint(array, pltpu.HBM) for array in outside))


def exact_dot(a, b):
    return jnp.dot(a, b, preferred_element_type=jnp.float32)


def transposed_dot(a, b):
    return lax.dot_general(a, b, (((0,), (0,)), ((), ())), preferred_element_type=jnp.float32)


def iota(shape, dim):
    return lax.broadcasted_iota(jnp.int32, shape, dim)


def as_column(row):
    size = row.shape[1]
    eye = iota((size, size), 0) == iota((size, size), 1)
    return jnp.sum(jnp.where(eye, row, jnp.zeros_like(row)), axis=1, keepdims=True)


def as_row(column):
    size = column.shape[0]
    eye = iota((size, size), 0) == iota((size, size), 1)
    return jnp.sum(jnp.where(eye, column, jnp.zeros_like(column)), axis=0, keepdims=True)


def pack_kernel(ids_hbm, tokens_hbm, _, __, out_ref, ids_ref, sems):
    named = pltpu.make_async_copy(ids_hbm, ids_ref, sems.at[0])
    named.start()
    copy = pltpu.make_async_copy(tokens_hbm, out_ref.at[:, 128:], sems.at[1])
    copy.start()
    named.wait()
    names = ids_ref[...].astype(jnp.float32)
    lane = iota((out_ref.shape[0], 128), 1)
    out_ref[:, :128] = jnp.where(lane == 0, as_column(names[0:1]), as_column(names[1:2])).astype(out_ref.dtype)
    copy.wait()


def rows_of(ids_block, group, source, expert, rows, tok_rows, capacity):
    tall = ids_block.shape[0]
    names = ids_block.astype(jnp.float32)
    expert = expert.astype(jnp.float32)
    named = (names[:, 0:1] == expert) | (names[:, 1:2] == expert)
    later, earlier = iota((tall, tall), 0), iota((tall, tall), 1)
    lower = ((later > earlier) & (later // tok_rows == earlier // tok_rows)).astype(jnp.bfloat16)
    flags = jnp.broadcast_to(named.astype(jnp.float32), (tall, 128)).astype(jnp.bfloat16)
    before = exact_dot(lower, flags)[:, 0:1].astype(jnp.int32)
    target = jnp.where(named & (group >= 0), (group * 2 + source) * capacity + before, -1)
    return (iota((tall, rows), 1) == target).astype(jnp.bfloat16)


def picked(ref, group, source, expert, rows, tok_rows, capacity, start, stop):
    sel = rows_of(ref[:, :128], group, source, expert, rows, tok_rows, capacity)
    return transposed_dot(sel, ref[:, 128 + start : 128 + stop])


def layer_of(ref, tok_rows):
    return iota((ref.shape[0], 1), 0) // tok_rows


def cut_kernel(tok_rows, in_ref, out_ref):
    shape = (out_ref.shape[0], in_ref.shape[0])
    row, place = iota(shape, 0), iota(shape, 1)
    layer = (row // tok_rows + 1) ^ lax.axis_index("et")
    move = (place == layer * tok_rows + row % tok_rows).astype(in_ref.dtype)
    out_ref[...] = exact_dot(move, in_ref[:, : out_ref.shape[1]]).astype(out_ref.dtype)


def select_kernel(tok_rows, capacity, own_ref, near_ref, *outs):
    expert, core = lax.axis_index("ep") ^ 2, lax.axis_index("ep") % 2
    rows = outs[0].shape[0]
    group = (layer_of(own_ref, tok_rows) ^ lax.axis_index("et")) - 1
    found = [
        (rows_of(ref[:, :128], group, source, expert, rows, tok_rows, capacity), ref)
        for ref, source in ((own_ref, core), (near_ref, 1 - core))
    ]
    start = own_ref.shape[1] - sum(out.shape[1] for out in outs)
    for out in outs:
        stop = start + out.shape[1]
        out[...] = sum(transposed_dot(sel, ref[:, start:stop]) for sel, ref in found).astype(out.dtype)
        start = stop


def stay_kernel(tok_rows, capacity, own_ref, near_ref, early_ref, early_other, stay_ref, first_ref):
    expert, core = lax.axis_index("ep"), lax.axis_index("ep") % 2
    group = layer_of(own_ref, tok_rows) ^ lax.axis_index("et")
    for out, refs, place in (
        (stay_ref, (own_ref, near_ref), group),
        (first_ref, (early_ref, early_other), layer_of(early_ref, tok_rows)),
    ):
        rows, width = out.shape
        out[...] = sum(
            picked(ref, place, core ^ other, expert, rows, tok_rows, capacity, 0, width)
            for other, ref in enumerate(refs)
        ).astype(out.dtype)


def pick_kernel(tok_rows, capacity, ref, rows_ref):
    rows, width = rows_ref.shape
    expert, core = lax.axis_index("ep"), lax.axis_index("ep") % 2
    group = layer_of(ref, tok_rows)
    rows_ref[...] = picked(ref, group, core, expert, rows, tok_rows, capacity, 0, width).astype(rows_ref.dtype)


def gather_rows(x_ref, stay, first, far):
    rows = stay.shape[0]
    chip = lax.axis_index("ep") // 2
    x_ref[pl.ds(pl.multiple_of(chip * rows, rows), rows), :] = stay
    far = jnp.concatenate([first.astype(jnp.float32), far.astype(jnp.float32)], axis=0)
    x_ref[pl.ds(pl.multiple_of((1 - chip) * rows, rows), rows), :] = far.astype(x_ref.dtype)


def first_kernel(tok_rows, capacity, other_ref, part_ref, stay_ref, early_ref, gate_all, up_all, *refs):
    gate_ref, up_ref, x_ref = refs
    rows, cut = part_ref.shape
    expert, core = lax.axis_index("ep"), lax.axis_index("ep") % 2
    group = layer_of(other_ref, tok_rows)
    far = picked(other_ref, group, 1 - core, expert, rows, tok_rows, capacity, 0, cut)
    far = far + part_ref[...].astype(jnp.float32)
    gather_rows(x_ref, stay_ref[:, :cut], early_ref[:, :cut], far)
    gate_ref[...] = exact_dot(x_ref[...], gate_all[0, :cut, :])
    up_ref[...] = exact_dot(x_ref[...], up_all[0, :cut, :])


def middle_kernel(start, far_ref, stay_ref, early_ref, gate_in, up_in, gate_all, up_all, gate_ref, up_ref, x_ref):
    stop = start + far_ref.shape[1]
    gather_rows(x_ref, stay_ref[:, start:stop], early_ref[:, start:stop], far_ref[...])
    gate_ref[...] = gate_in[...] + exact_dot(x_ref[...], gate_all[0, start:stop, :])
    up_ref[...] = up_in[...] + exact_dot(x_ref[...], up_all[0, start:stop, :])


def second_kernel(folds, experts, far_ref, stay_ref, early_ref, gate_in, up_in, gate_all, up_all, *refs):
    out_ref, x_ref, hidden_ref = refs
    cut = stay_ref.shape[1] - far_ref.shape[1]
    gather_rows(x_ref, stay_ref[:, cut:], early_ref[:, cut:], far_ref[...])
    gate_val = gate_in[...] + exact_dot(x_ref[...], gate_all[0, cut:, :])
    up_val = up_in[...] + exact_dot(x_ref[...], up_all[0, cut:, :])
    half = 0.5 * gate_val
    hidden_ref[...] = (half + half * jnp.tanh(half)) * up_val
    store_blocks(folds, experts, hidden_ref, out_ref)


def store_blocks(folds, experts, hidden_ref, out_ref):
    peers = out_ref.shape[0]
    capacity = hidden_ref.shape[0] // peers
    span = hidden_ref.shape[1] // folds
    mine = lax.axis_index("et")
    for peer in range(0, peers, 2):
        layer, chip = peer // experts, peer % experts // 2
        start = chip * (peers // 2) * capacity + (layer ^ mine) * (2 * capacity)
        both = hidden_ref[pl.ds(pl.multiple_of(start, 8), 2 * capacity), :]
        for core in range(2):
            rows = both[core * capacity : (core + 1) * capacity]
            pieces = [rows[:, fold * span : (fold + 1) * span] for fold in range(folds)]
            out_ref[peer + core] = jnp.concatenate(pieces, axis=0).astype(out_ref.dtype)


def routed_by_columns(tokens, expert_ids, w_gate, w_up, peers, capacity, folds):
    tok_rows, width = tokens.shape
    units = w_gate.shape[2]
    experts = 4
    rows = peers * capacity
    half = rows // 2
    cuts = (width // 6, 11 * width // 24, 3 * width // 4)
    cut = cuts[0]
    kind = tokens.dtype

    def array(*shape):
        return jax.ShapeDtypeStruct(shape, kind)

    def swap(block, bit):
        return lax.ppermute(block, "ep", [(i, i ^ bit) for i in range(experts)])

    packed = local_kernel(
        pack_kernel,
        array(tok_rows, 128 + width),
        (),
        (expert_ids.T, tokens, w_gate, w_up),
        scratch=[pltpu.VMEM((2, tok_rows), jnp.int32), pltpu.SemaphoreType.DMA((2,))],
    )
    early = swap(packed, 2)
    own = lax.all_gather(packed, "et", axis=0, tiled=True)
    own, early = lax.optimization_barrier((own, early))
    others = own.shape[0] - tok_rows
    rest = half - 2 * capacity
    part = local_kernel(functools.partial(cut_kernel, tok_rows), array(others, 128 + cut), (own,))
    near, far, early_other = swap(own, 1), swap(part, 2), swap(early, 1)
    kernel = functools.partial(select_kernel, tok_rows, capacity)
    ends = (*cuts[1:], width)
    laters = local_kernel(kernel, [array(rest, stop - start) for start, stop in zip(cuts, ends)], (own, near))
    later_fars = [swap(later, 2) for later in laters]
    own, near, *laters = lax.optimization_barrier((own, near, *laters))
    kernel = functools.partial(stay_kernel, tok_rows, capacity)
    outs = [array(half, width), array(2 * capacity, width)]
    stay, first = local_kernel(kernel, outs, (own, near, early, early_other))
    far_other = swap(far, 1)
    far_part = local_kernel(functools.partial(pick_kernel, tok_rows, capacity), array(rest, cut), (far,))
    far_other, far_part, stay = lax.optimization_barrier((far_other, far_part, stay))

    def sums(kernel, blocks, span):
        out_shape = [jax.ShapeDtypeStruct((rows, units), jnp.float32)] * 2
        return local_kernel(kernel, out_shape, (*blocks, w_gate, w_up), scratch=[pltpu.VMEM((rows, span), kind)])

    gate_sum, up_sum = sums(
        functools.partial(first_kernel, tok_rows, capacity), (far_other, far_part, stay, first), cut
    )
    for start, later_far in zip(cuts[:-1], later_fars):
        later_far, gate_sum = lax.optimization_barrier((later_far, gate_sum))
        kernel = functools.partial(middle_kernel, start)
        gate_sum, up_sum = sums(kernel, (later_far, stay, first, gate_sum, up_sum), later_far.shape[1])
    later_far, gate_sum = lax.optimization_barrier((later_fars[-1], gate_sum))
    return local_kernel(
        functools.partial(second_kernel, folds, experts),
        pltpu.VMEM((peers, capacity * folds, units // folds), kind),
        (later_far, stay, first, gate_sum, up_sum, w_gate, w_up),
        scratch=[pltpu.VMEM((rows, width - cuts[-1]), kind), pltpu.VMEM((rows, units), jnp.float32)],
    )


def picks_kernel(experts, capacity, folds, ids_ref, weights_ref, picks_ref, column_ref):
    tok_rows = ids_ref.shape[1]
    both = 2 * tok_rows
    ids = [as_column(ids_ref[slot : slot + 1, :]) for slot in range(2)]
    expert = iota((tok_rows, 128), 1)
    named = ((expert == ids[0]) | (expert == ids[1])).astype(jnp.bfloat16)
    lower = (iota((tok_rows, tok_rows), 0) > iota((tok_rows, tok_rows), 1)).astype(jnp.bfloat16)
    before = exact_dot(lower, named).astype(jnp.int32)
    slot_row, token = iota((both, tok_rows), 0), iota((both, tok_rows), 1)
    target = jnp.zeros((both, 1), jnp.int32)
    column = jnp.zeros((both, 1), jnp.float32)
    for slot, chosen in enumerate(ids):
        position = jnp.sum(jnp.where(expert == chosen, before, 0), axis=1, keepdims=True)
        mask = slot_row == 2 * token + slot
        place = as_row(chosen * (folds * capacity) + position)
        target = target + jnp.sum(jnp.where(mask, place, 0), axis=1, keepdims=True)
        column = column + jnp.sum(jnp.where(mask, weights_ref[slot : slot + 1, :], 0.0), axis=1, keepdims=True)
    column_ref[...] = jnp.broadcast_to(column, column_ref.shape)
    lane = iota((both, experts * folds * capacity), 1)
    for fold in range(folds):
        picks_ref[fold * both : (fold + 1) * both, :] = (lane == target + fold * capacity).astype(picks_ref.dtype)


def final_kernel(experts, folds, picks_ref, column_ref, recv_ref, out_hbm, out_ref, sems):
    tok_rows = out_ref.shape[0]
    both = 2 * tok_rows
    peers, tall, span = recv_ref.shape
    column = column_ref[:, 0:1]
    copies = []
    for part in range(peers // experts):
        block = recv_ref[part * experts : (part + 1) * experts].reshape(experts * tall, span)
        rows = exact_dot(picks_ref[...], block)
        for fold in range(folds):
            scaled = rows[fold * both : (fold + 1) * both] * column
            start = (part * folds + fold) * span
            out_ref[:, :, start : start + span] = scaled.astype(out_ref.dtype).reshape(tok_rows, 2, span)
        columns = slice(part * folds * span, (part + 1) * folds * span)
        copy = pltpu.make_async_copy(out_ref.at[:, :, columns], out_hbm.at[:, :, columns], sems.at[part])
        copy.start()
        copies.append(copy)
    for copy in copies:
        copy.wait()


def finish(expert_ids, gate_weights, received, experts, folds):
    tok_rows = expert_ids.shape[0]
    peers, tall, span = received.shape
    capacity = tall // folds
    kind = received.dtype
    picks, column = local_kernel(
        functools.partial(picks_kernel, experts, capacity, folds),
        [
            jax.ShapeDtypeStruct((2 * tok_rows * folds, experts * tall), kind),
            jax.ShapeDtypeStruct((2 * tok_rows, 128), jnp.float32),
        ],
        (expert_ids.T, gate_weights.T),
        moved=1 << 20,
    )
    units = peers // experts * folds * span
    return pl.pallas_call(
        functools.partial(final_kernel, experts, folds),
        out_shape=jax.ShapeDtypeStruct((tok_rows, 2, units), kind),
        in_specs=[WHOLE] * 3,
        out_specs=OUTSIDE,
        scratch_shapes=[pltpu.VMEM((tok_rows, 2, units), kind), pltpu.SemaphoreType.DMA((peers // experts,))],
        compiler_params=pltpu.CompilerParams(vmem_limit_bytes=12 << 20),
    )(picks, column, received)


def body(tokens, expert_ids, gate_weights, w_gate, w_up):
    tok_rows, width = tokens.shape
    experts = lax.axis_size("ep")
    tensor_size = lax.axis_size("et")
    peers = experts * tensor_size
    capacity = tok_rows // 2
    gate_local = w_gate[0]
    up_local = w_up[0]
    if experts == 4 and tensor_size == 4:
        folds = 4
        blocks = routed_by_columns(tokens, expert_ids, w_gate, w_up, peers, capacity, folds)
        return finish(expert_ids, gate_weights, exchange(blocks), experts, folds)
    slot_pairs = place_slots(expert_ids, experts, capacity)
    selector = build_select(slot_pairs, experts * capacity)
    buffer = jnp.dot(selector, tokens, preferred_element_type=jnp.float32).astype(jnp.bfloat16)
    buffer = buffer.reshape(1, experts, capacity * width // 128, 128)
    buffer = jnp.broadcast_to(buffer, (tensor_size,) + buffer.shape[1:])
    arrived = exchange(buffer.reshape(peers, capacity * width // 128, 128))
    hidden = swiglu_rows(arrived.reshape(peers * capacity, width), gate_local, up_local)
    units = hidden.shape[1]
    returned = exchange(hidden.reshape(peers, capacity * units // 128, 128))
    returned = returned.reshape(tensor_size, experts * capacity, units)
    targets = jnp.arange(experts * capacity, dtype=jnp.int32)
    picker = (slot_pairs[:, :, None] == targets[None, None, :]).astype(jnp.bfloat16)
    gathered = jnp.einsum("tsj,ejf->tsef", picker, returned, preferred_element_type=jnp.float32)
    gathered = gathered.reshape(tok_rows, 2, tensor_size * units)
    return (gate_weights[:, :, None] * gathered).astype(jnp.bfloat16)


def solution(mesh):
    in_specs = (
        P(("groups", "et", "ep"), None),
        P(("groups", "et", "ep"), None),
        P(("groups", "et", "ep"), None),
        P("ep", None, "et"),
        P("ep", None, "et"),
    )
    out_specs = P(("groups", "et", "ep"), None, None)
    return jax.shard_map(body, mesh=mesh, in_specs=in_specs, out_specs=out_specs, check_vma=False)
```
